32 devices in a mesh: rep: 2 (over x), fsdp: 16 (over z, y, core).
Axes of the slice: x: 2, y: 2, z: 4, core: 2. Of those that a mesh axis runs over, the one named last changes fastest.
Arguments:
- tokens: bfloat16 [64, 512, 768], P(('rep', 'fsdp')), may hold values from -6 to 6
- mask_pos: int32 [64, 128], P(('rep', 'fsdp')), may hold values from 0 to 511, as said below
- group_id: int32 [64], P(('rep', 'fsdp')), may hold values from 0 to 1, as said below
- cotangent: bfloat16 [64, 512, 768], P(('rep', 'fsdp')), may hold values from -6 to 6
- w_qkv: float32 [768, 2304], P('fsdp'), may hold values from -0.21875 to 0.21875
- b_query: float32 [768], P('fsdp'), may hold values from -3 to 3
- b_value: float32 [768], P('fsdp'), may hold values from -3 to 3
- w_out: float32 [768, 768], P('fsdp'), may hold values from -3 to 3
- b_out: float32 [768], P('fsdp'), may hold values from -3 to 3
- w_up: float32 [768, 3072], P('fsdp'), may hold values from -0.21875 to 0.21875
- b_up: float32 [3072], P('fsdp'), may hold values from -3 to 3
- w_down: float32 [3072, 768], P('fsdp'), may hold values from -0.109375 to 0.109375
- b_down: float32 [768], P('fsdp'), may hold values from -3 to 3
- ln1_gain: float32 [768], P('fsdp'), may hold values from 0.1 to 1.9
- ln1_bias: float32 [768], P('fsdp'), may hold values from -3 to 3
- ln2_gain: float32 [768], P('fsdp'), may hold values from 0.1 to 1.9
- ln2_bias: float32 [768], P('fsdp'), may hold values from -3 to 3
- mask_embed: float32 [768], P('fsdp'), may hold values from -4 to 4
Outputs:
- output: bfloat16 [64, 512, 768], P(('rep', 'fsdp'))
- token_grad: bfloat16 [64, 512, 768], P(('rep', 'fsdp'))
- w_qkv_grad: float32 [768, 2304], P('fsdp')
- b_query_grad: float32 [768], P('fsdp')
- b_value_grad: float32 [768], P('fsdp')
- w_out_grad: float32 [768, 768], P('fsdp')
- b_out_grad: float32 [768], P('fsdp')
- w_up_grad: float32 [768, 3072], P('fsdp')
- b_up_grad: float32 [3072], P('fsdp')
- w_down_grad: float32 [3072, 768], P('fsdp')
- b_down_grad: float32 [768], P('fsdp')
- ln1_gain_grad: float32 [768], P('fsdp')
- ln1_bias_grad: float32 [768], P('fsdp')
- ln2_gain_grad: float32 [768], P('fsdp')
- ln2_bias_grad: float32 [768], P('fsdp')
- mask_embed_grad: float32 [768], P('fsdp')
The draws below stay inside these ranges and needn't reach their ends.
Inputs may be any that keep to these rules, and one draw needn't show every extreme that they name: `group_id`: all 2 clips of one device share one group id; both ids occur in every draw. A clip of group 1 has half of 512 patches, the rest of its rows are padding. `mask_pos`: the 128 positions of a clip are distinct and lie below the clip's number of patches.
All inputs are finite; a program needn't handle non-finite values.
Results may differ from the reference program's by a relative error of at most 0.014.
The reference program's roundings to bfloat16 on the way count: a program that leaves them out, or rounds other values in their place, can miss the bound.
Values may be sent and summed in bfloat16 or wider, within the bound.
No kernel may reach another device: no remote copies, remote signals or barrier semaphores. Data moves between devices by JAX's collectives and lax.ppermute only.
A program may use at most 192 MiB of HBM per device.

```python
import jax
import jax.numpy as jnp
from jax import lax

D = 768
HEADS = 12
FF = 3072
SEQ = 512
NMASK = 128
CLIP_DEV = 2
CLIPS = 64


def group_draw(key):
    blocks = CLIPS // CLIP_DEV
    raw_ids = jax.random.randint(jax.random.fold_in(key, 101), (blocks,), 0, 2)
    raw_ids = raw_ids.at[0].set(0).at[blocks - 1].set(1)
    return jnp.repeat(raw_ids, CLIP_DEV).astype(jnp.int32)


def draw_group_id(key, part):
    return group_draw(key)


def draw_mask_pos(key, part):
    groups = group_draw(key)
    key = jax.random.fold_in(key, 7)
    lengths = jnp.where(groups == 0, SEQ, SEQ // 2)
    positions = jnp.arange(SEQ, dtype=jnp.int32)
    ranking = jax.random.randint(key, (CLIPS, SEQ), 0, 1 << 20) * SEQ + positions[None, :]
    ranking = jnp.where(positions[None, :] < lengths[:, None], ranking, ranking + (1 << 30))
    order = jnp.argsort(ranking, axis=1, stable=True)
    return order[:, :NMASK].astype(jnp.int32)


def shard_levels(own_key, shape, shards, smallest, high):
    loudness = 1.0
    for axis_at, shards_of in shards:
        heights = jax.random.uniform(jax.random.fold_in(jax.random.fold_in(own_key, 6), axis_at), (shards_of,), jnp.float32, smallest / len(shards), high / len(shards))
        loudness = loudness * jnp.repeat(jnp.exp(heights), shape[axis_at] // shards_of).reshape((-1,) + (1,) * (len(shape) - 1 - axis_at))
    return loudness


def scatter_about(key, dims, deviation, bound, cuts=(), held_as=jnp.bfloat16):
    values = deviation * jax.random.normal(key, dims, jnp.float32)
    if cuts:
        values = values * shard_levels(key, dims, cuts, -0.22, 0.18)
    return jnp.clip(values, -bound, bound).astype(held_as)


def setup_inputs(seed: int = 0) -> dict:
    splits = jax.random.split(jax.random.key(seed), 19)
    tokens = scatter_about(splits[0], (CLIPS, SEQ, D), 1.0, 6.0, ((0, 32),))
    mask_pos = draw_mask_pos(jax.random.fold_in(splits[18], 71), 0)
    group_id = draw_group_id(jax.random.fold_in(splits[18], 71), 0)
    cotangent = scatter_about(splits[3], (CLIPS, SEQ, D), 1.0, 6.0, ((0, 32),))
    w_qkv = scatter_about(splits[4], (D, 3 * D), D ** -0.5, 0.21875, ((0, 16),), jnp.float32)
    b_query = scatter_about(splits[5], (D,), 0.5, 3.0, ((0, 16),), jnp.float32)
    b_value = scatter_about(splits[6], (D,), 0.5, 3.0, ((0, 16),), jnp.float32)
    w_out = scatter_about(splits[7], (D, D), (max(4, D // 256)) ** -0.5, 3.0, ((0, 16),), jnp.float32)
    b_out = scatter_about(splits[8], (D,), 0.5, 3.0, ((0, 16),), jnp.float32)
    w_up = scatter_about(splits[9], (D, FF), D ** -0.5, 0.21875, ((0, 16),), jnp.float32)
    b_up = scatter_about(splits[10], (FF,), 0.5, 3.0, ((0, 16),), jnp.float32)
    w_down = scatter_about(splits[11], (FF, D), FF ** -0.5, 0.109375, ((0, 16),), jnp.float32)
    b_down = scatter_about(splits[12], (D,), 0.5, 3.0, ((0, 16),), jnp.float32)
    ln1_gain = jnp.clip(1.0 + 0.18 * jax.random.normal(splits[13], (D,), jnp.float32), 0.1, 1.9)
    ln1_bias = scatter_about(splits[14], (D,), 0.5, 3.0, ((0, 16),), jnp.float32)
    ln2_gain = jnp.clip(1.0 + 0.18 * jax.random.normal(splits[15], (D,), jnp.float32), 0.1, 1.9)
    ln2_bias = scatter_about(splits[16], (D,), 0.5, 3.0, ((0, 16),), jnp.float32)
    mask_embed = scatter_about(splits[17], (D,), 1.0, 4.0, ((0, 16),), jnp.float32)
    return dict(tokens=tokens, mask_pos=mask_pos, group_id=group_id, cotangent=cotangent, w_qkv=w_qkv, b_query=b_query, b_value=b_value, w_out=w_out, b_out=b_out, w_up=w_up, b_up=b_up, w_down=w_down, b_down=b_down, ln1_gain=ln1_gain, ln1_bias=ln1_bias, ln2_gain=ln2_gain, ln2_bias=ln2_bias, mask_embed=mask_embed)


@jax.custom_vjp
def low(v):
    return lax.optimization_barrier(v.astype(jnp.bfloat16)).astype(jnp.float32)

@jax.custom_vjp
def low_back(v):
    return v

def low_keep(v):
    return (low(v), None)

def low_pass(kept, grad):
    return (grad,)

def back_keep(v):
    return (v, None)

def back_low(kept, grad):
    return (low(grad),)
low.defvjp(low_keep, low_pass)
low_back.defvjp(back_keep, back_low)
EPS = 1e-06
PRECISE = lax.Precision.HIGHEST

def layer_norm(values, ln_gain, offset):
    centre = values - lax.optimization_barrier(jnp.mean(values, -1, keepdims=True))
    spread = lax.optimization_barrier(jnp.mean(centre * centre, -1, keepdims=True))
    return centre * lax.rsqrt(spread + EPS) * ln_gain + offset

def project_rows(inputs, matrix):
    return jnp.einsum('csd,de->cse', inputs, matrix, precision=PRECISE)

def forward(params, rows_in, masked, valid_rows):
    w_qkv, b_query, b_value, w_out, b_out, w_up, b_up, w_down, b_down, gain_one, bias_one, gain_two, bias_two, mask_embed = [low(member) for member in params]
    clip_count, seq_len, feature_dim = rows_in.shape
    head_dim = feature_dim // HEADS
    blended = jnp.where(masked[..., None], mask_embed, rows_in)
    normed = low(layer_norm(blended, gain_one, bias_one))
    joined = project_rows(normed, w_qkv)
    head_shape = (clip_count, seq_len, HEADS, head_dim)
    query_rows = low_back(low(joined[..., :feature_dim] + b_query)).reshape(head_shape)
    key_rows = low_back(low(joined[..., feature_dim:2 * feature_dim])).reshape(head_shape)
    value_rows = low_back(low(joined[..., 2 * feature_dim:] + b_value)).reshape(head_shape)
    scores = jnp.einsum('cqhe,ckhe->chqk', query_rows, key_rows, precision=PRECISE)
    scores = low_back(scores * head_dim ** (-0.5))
    scores = jnp.where(valid_rows[:, None, None, :], scores, -1e+30)
    row_top = lax.optimization_barrier(jnp.max(scores, -1, keepdims=True))
    exp_scores = jnp.exp(scores - row_top)
    softmax = low(exp_scores / lax.optimization_barrier(jnp.sum(exp_scores, -1, keepdims=True)))
    attended = jnp.einsum('chqk,ckhe->cqhe', softmax, value_rows, precision=PRECISE)
    attended = low_back(low(attended.reshape(clip_count, seq_len, feature_dim)))
    branch = low_back(project_rows(attended, w_out) + b_out)
    hidden = blended + branch
    normed_two = low(layer_norm(hidden, gain_two, bias_two))
    pre_act = low_back(project_rows(normed_two, w_up) + b_up)
    activated = low(jax.nn.gelu(pre_act, approximate=False))
    result = low_back(project_rows(activated, w_down) + b_down)
    return (hidden + result) * valid_rows[..., None].astype(jnp.float32)

def reference(tokens, mask_pos, group_id, cotangent, w_qkv, b_query, b_value, w_out, b_out, w_up, b_up, w_down, b_down, ln1_gain, ln1_bias, ln2_gain, ln2_bias, mask_embed):
    params = (w_qkv, b_query, b_value, w_out, b_out, w_up, b_up, w_down, b_down, ln1_gain, ln1_bias, ln2_gain, ln2_bias, mask_embed)
    positions = jnp.arange(SEQ, dtype=jnp.int32)
    masked = jnp.any(mask_pos[:, :, None] == positions[None, None, :], axis=1)
    lengths = jnp.where(group_id == 0, SEQ, SEQ // 2).astype(jnp.int32)
    valid_rows = positions[None, :] < lengths[:, None]
    per_step = max(1, 4096 // SEQ)
    while CLIPS % per_step:
        per_step -= 1
    batches = CLIPS // per_step

    def regroup(values_in):
        return values_in.reshape((batches, per_step) + values_in.shape[1:])

    def advance(running, block_in):
        rows_in, mask_in, keep_in, cot_in = block_in

        def run_block(weights, inputs):
            return forward(weights, inputs, mask_in, keep_in)
        result, pull_back = jax.vjp(run_block, params, rows_in.astype(jnp.float32))
        weight_grads, input_grad = pull_back(cot_in.astype(jnp.float32))
        running = jax.tree.map(jnp.add, running, weight_grads)
        return (running, (result.astype(jnp.bfloat16), input_grad.astype(jnp.bfloat16)))
    zero_sums = tuple((jnp.zeros_like(member) for member in params))
    grad_sums, (output, token_grad) = lax.scan(advance, zero_sums, (regroup(tokens), regroup(masked), regroup(valid_rows), regroup(cotangent)))
    output = output.reshape(tokens.shape)
    token_grad = token_grad.reshape(tokens.shape)
    return (output, token_grad, grad_sums[0], grad_sums[1], grad_sums[2], grad_sums[3], grad_sums[4], grad_sums[5], grad_sums[6], grad_sums[7], grad_sums[8], grad_sums[9], grad_sums[10], grad_sums[11], grad_sums[12], grad_sums[13])
```

```python
import functools

import jax
import jax.numpy as jnp
from jax import lax
from jax.experimental import pallas as pl
from jax.experimental.pallas import tpu as pltpu
from jax.sharding import PartitionSpec as P

HEADS = 12
BLOCKS = 16
EPS = 1e-06
BF = jnp.bfloat16
F32 = jnp.float32
VMEM_LIMIT = 56 * 1024 * 1024

B_QUERY, B_VALUE, B_OUT, B_DOWN, GAIN1, BIAS1, GAIN2, BIAS2, EMBED, B_UP = range(10)
VECS = 13


def dot(a, b):
    return jnp.dot(a, b, preferred_element_type=F32)


def dot_nt(a, b):
    return lax.dot_general(a, b, (((1,), (1,)), ((), ())), preferred_element_type=F32)


def dot_tn(a, b):
    return lax.dot_general(a, b, (((0,), (0,)), ((), ())), preferred_element_type=F32)


def normalise(values):
    centre = values - jnp.mean(values, -1, keepdims=True)
    spread = jnp.mean(centre * centre, -1, keepdims=True)
    r = lax.rsqrt(spread + EPS)
    return centre * r, r


def norm_back(x_hat, r, q, gain):
    qg = q * gain
    m1 = jnp.mean(qg, -1, keepdims=True)
    m2 = jnp.mean(qg * x_hat, -1, keepdims=True)
    return r * (qg - m1 - x_hat * m2)


def colsum(values):
    return jnp.sum(values, 0, keepdims=True)


def gelu_both(u):
    x = jnp.abs(u)
    t = pl.reciprocal(1.0 + x * (0.3275911 * 0.7071067811865476), approx=False)
    e = jnp.exp2(u * u * (-0.5 * 1.4426950408889634))
    poly = 0.5 * 1.061405429
    for c in (-1.453152027, 1.421413741, -0.284496736, 0.254829592):
        poly = poly * t + 0.5 * c
    tail = poly * t * e
    cdf = jnp.where(u < 0, tail, 1.0 - tail)
    return u * cdf, cdf + u * (e * 0.3989422804014327)


def forward_kernel(group_ref, tok_ref, mask_ref, vec_ref, wq_ref, wk_ref, wv_ref, normed_ref, qkv_ref, att_ref, lse_ref):
    clip = pl.program_id(0)
    seq, dim = tok_ref.shape[1], tok_ref.shape[2]
    vec = lambda k: vec_ref[k : k + 1, :]
    step = seq // 2
    for r in range(0, seq, step):
        rows = slice(r, r + step)
        blended = jnp.where(mask_ref[0, rows] > 0, vec(EMBED), tok_ref[0, rows].astype(F32))
        x_hat, _ = normalise(blended)
        normed = (x_hat * vec(GAIN1) + vec(BIAS1)).astype(BF)
        normed_ref[0, rows] = normed
        qkv_ref[0, rows, 0:dim] = (dot(normed, wq_ref[...].reshape(dim, dim)) + vec(B_QUERY)).astype(BF)
        qkv_ref[0, rows, dim : 2 * dim] = dot(normed, wk_ref[...].reshape(dim, dim)).astype(BF)
        qkv_ref[0, rows, 2 * dim :] = (dot(normed, wv_ref[...].reshape(dim, dim)) + vec(B_VALUE)).astype(BF)
    head = dim // HEADS
    scale = head**-0.5 * 1.4426950408889634

    def attend(length):
        if length < seq:
            att_ref[0, length:, :] = jnp.zeros((seq - length, dim), BF)
            lse_ref[0, :, :] = jnp.zeros((HEADS, seq), F32)
        chunk = min(length, 256)
        lane = lax.broadcasted_iota(jnp.int32, (chunk, 2 * head), 1)
        for pair in range(HEADS // 2):
            at = pair * 2 * head
            k = qkv_ref[0, 0:length, dim + at : dim + at + 2 * head]
            vt = qkv_ref[0, 0:length, 2 * dim + at : 2 * dim + at + 2 * head].T
            for c in range(0, length, chunk):
                q = qkv_ref[0, c : c + chunk, at : at + 2 * head]
                outs = []
                for h in range(2):
                    qm = jnp.where((lane < head) == (h == 0), q, jnp.zeros_like(q))
                    st = dot_nt(k, qm) * scale
                    top = jnp.max(st, 0, keepdims=True)
                    e = jnp.exp2(st - top)
                    total = jnp.sum(e, 0, keepdims=True)
                    p = (e * (1.0 / total)).astype(BF)
                    outs.append(dot(vt[h * head : (h + 1) * head], p))
                    lse_ref[0, 2 * pair + h : 2 * pair + h + 1, c : c + chunk] = top + jnp.log2(total)
                att_ref[0, c : c + chunk, at : at + 2 * head] = jnp.concatenate(outs, 0).T.astype(BF)

    full = group_ref[clip] == 0
    pl.when(full)(lambda: attend(seq))
    pl.when(jnp.logical_not(full))(lambda: attend(seq // 2))


def weight_spec(index):
    return pl.BlockSpec((BLOCKS, 48, 768), lambda *g: (0, index, 0))


def forward_call(group_id, tokens, mask, vecs, w1):
    clips, seq, dim = tokens.shape
    row = lambda *tail: pl.BlockSpec((1, *tail), lambda c, *_: (c,) + (0,) * len(tail))
    return pl.pallas_call(
        forward_kernel,
        grid_spec=pltpu.PrefetchScalarGridSpec(
            num_scalar_prefetch=1,
            grid=(clips,),
            in_specs=[
                row(seq, dim),
                row(seq, 1),
                pl.BlockSpec(vecs.shape, lambda *g: (0, 0)),
                weight_spec(0),
                weight_spec(1),
                weight_spec(2),
            ],
            out_specs=[row(seq, dim), row(seq, 3 * dim), row(seq, dim), row(HEADS, seq)],
        ),
        out_shape=[
            jax.ShapeDtypeStruct((clips, seq, dim), BF),
            jax.ShapeDtypeStruct((clips, seq, 3 * dim), BF),
            jax.ShapeDtypeStruct((clips, seq, dim), BF),
            jax.ShapeDtypeStruct((clips, HEADS, seq), F32),
        ],
        compiler_params=pltpu.CompilerParams(vmem_limit_bytes=VMEM_LIMIT),
        cost_estimate=pl.CostEstimate(flops=9 * 10**9, bytes_accessed=16 * 2**20, transcendentals=0),
        name="attention_forward",
    )(group_id, tokens, mask, vecs, w1, w1, w1)


def mlp_kernel(
    group_ref, tok_ref, mask_ref, cot_ref, att_ref, vec_ref, wo_ref, wu_ref, wd_ref,
    out_ref, gh_ref, gatt_ref, gwo_ref, gwu_ref, gwd_ref, gvec_ref,
    hidden, n2, gr, act, gpre, acc, gn2,
):
    j = pl.program_id(0)
    steps = pl.num_programs(0)
    rows_all, dim = tok_ref.shape
    seq = rows_all // group_ref.shape[0]
    vec = lambda k: vec_ref[k : k + 1, :]
    step = 256
    keeps = [group_ref[r // seq] == 0 if (r % seq) >= seq // 2 else None for r in range(0, rows_all, step)]
    weight = [1.0 if keep is None else jnp.where(keep, 1.0, 0.0) for keep in keeps]

    @pl.when(j == 0)
    def _():
        gvec_ref[...] = jnp.zeros_like(gvec_ref)
        w_out = wo_ref[...].reshape(dim, dim)
        for i, r in enumerate(range(0, rows_all, step)):
            rows = slice(r, r + step)
            blended = jnp.where(mask_ref[rows] > 0, vec(EMBED), tok_ref[rows].astype(F32))
            h = blended + dot(att_ref[rows], w_out) + vec(B_OUT)
            hidden[rows] = h
            x_hat, _ = normalise(h)
            n2[rows] = (x_hat * vec(GAIN2) + vec(BIAS2)).astype(BF)
            g = cot_ref[rows].astype(F32) * weight[i]
            gr[rows] = g.astype(BF)
            gvec_ref[B_DOWN : B_DOWN + 1] += colsum(g)
            acc[rows] = h + vec(B_DOWN)
            gn2[rows] = jnp.zeros((step, dim), F32)

    w_up = wu_ref[...].reshape(dim, dim)
    w_down = wd_ref[...].reshape(dim, dim)
    b_up = vec_ref[pl.ds(B_UP + j, 1), :]
    bsum = jnp.zeros((1, dim), F32)
    for r in range(0, rows_all, step):
        rows = slice(r, r + step)
        pre = dot(n2[rows], w_up) + b_up
        ga = dot_nt(gr[rows], w_down)
        value, slope = gelu_both(pre)
        value = value.astype(BF)
        act[rows] = value
        grad = (slope * ga).astype(BF)
        gpre[rows] = grad
        bsum += colsum(grad.astype(F32))
        acc[rows] += dot(value, w_down)
        gn2[rows] += dot_nt(grad, w_up)
    gvec_ref[pl.ds(B_UP + j, 1), :] = bsum
    gwd_ref[...] = dot_tn(act[...], gr[...]).astype(BF).reshape(gwd_ref.shape)
    gwu_ref[...] = dot_tn(n2[...], gpre[...]).astype(BF).reshape(gwu_ref.shape)

    @pl.when(j == steps - 1)
    def _():
        w_out = wo_ref[...].reshape(dim, dim)
        for i, r in enumerate(range(0, rows_all, step)):
            rows = slice(r, r + step)
            out_ref[rows] = (acc[rows] * weight[i]).astype(BF)
            x_hat, scale = normalise(hidden[rows])
            q = gn2[rows]
            gvec_ref[GAIN2 : GAIN2 + 1] += colsum(q * x_hat)
            gvec_ref[BIAS2 : BIAS2 + 1] += colsum(q)
            gh = cot_ref[rows].astype(F32) * weight[i] + norm_back(x_hat, scale, q, vec(GAIN2))
            gh_ref[rows] = gh
            gb = gh.astype(BF)
            gpre[rows] = gb
            gvec_ref[B_OUT : B_OUT + 1] += colsum(gb.astype(F32))
            gatt_ref[rows] = dot_nt(gb, w_out).astype(BF)
        gwo_ref[...] = dot_tn(att_ref[...], gpre[...]).astype(BF).reshape(gwo_ref.shape)


def mlp_call(group_id, tokens, mask, cotangent, att, vecs, w1, w2):
    rows, dim = tokens.shape
    whole = lambda *shape: pl.BlockSpec(shape, lambda *g: (0,) * len(shape))
    out = lambda shape, kind: jax.ShapeDtypeStruct(shape, kind)
    return pl.pallas_call(
        mlp_kernel,
        grid_spec=pltpu.PrefetchScalarGridSpec(
            num_scalar_prefetch=1,
            grid=(4,),
            in_specs=[
                whole(rows, dim),
                whole(rows, 1),
                whole(rows, dim),
                whole(rows, dim),
                whole(*vecs.shape),
                weight_spec(3),
                pl.BlockSpec((BLOCKS, 48, dim), lambda j, *_: (0, j, 0)),
                pl.BlockSpec((4, 192, dim), lambda j, *_: (j, 1, 0)),
            ],
            out_specs=[
                whole(rows, dim),
                whole(rows, dim),
                whole(rows, dim),
                whole(BLOCKS, 48, dim),
                pl.BlockSpec((BLOCKS, 48, dim), lambda j, *_: (0, j, 0)),
                pl.BlockSpec((4, 192, dim), lambda j, *_: (j, 0, 0)),
                whole(16, dim),
            ],
            scratch_shapes=[
                pltpu.VMEM((rows, dim), F32),
                pltpu.VMEM((rows, dim), BF),
                pltpu.VMEM((rows, dim), BF),
                pltpu.VMEM((rows, dim), BF),
                pltpu.VMEM((rows, dim), BF),
                pltpu.VMEM((rows, dim), F32),
                pltpu.VMEM((rows, dim), F32),
            ],
        ),
        out_shape=[
            out((rows, dim), BF),
            out((rows, dim), F32),
            out((rows, dim), BF),
            out((BLOCKS, 48, dim), BF),
            out((BLOCKS, 192, dim), BF),
            out((BLOCKS, 192, dim), BF),
            out((16, dim), F32),
        ],
        compiler_params=pltpu.CompilerParams(vmem_limit_bytes=VMEM_LIMIT),
        cost_estimate=pl.CostEstimate(flops=32 * 10**9, bytes_accessed=40 * 2**20, transcendentals=0),
        name="mlp",
    )(group_id, tokens, mask, cotangent, att, vecs, w1, w2, w2)


def backward_kernel(
    group_ref, tok_ref, mask_ref, normed_ref, qkv_ref, lse_ref, gatt_ref, gh_ref, vec_ref, wq_ref, wk_ref, wv_ref,
    tg_ref, gw_ref, gvec_ref, gj,
):
    clip = pl.program_id(0)
    seq, dim = tok_ref.shape[1], tok_ref.shape[2]
    vec = lambda k: vec_ref[k : k + 1, :]
    head = dim // HEADS
    scale = head**-0.5
    base = clip * seq

    def back(length):
        if length < seq:
            gj[pl.ds(base + length, seq - length), :] = jnp.zeros((seq - length, 3 * dim), BF)
        chunk = min(length, 256)
        lane = lax.broadcasted_iota(jnp.int32, (chunk, 2 * head), 1)
        for pair in range(HEADS // 2):
            at = pair * 2 * head
            k = qkv_ref[0, 0:length, dim + at : dim + at + 2 * head]
            v = qkv_ref[0, 0:length, 2 * dim + at : 2 * dim + at + 2 * head]
            kt = k.T
            dk = jnp.zeros((length, 2 * head), F32)
            dv = jnp.zeros((length, 2 * head), F32)
            for c in range(0, length, chunk):
                q = qkv_ref[0, c : c + chunk, at : at + 2 * head]
                ga = gatt_ref[0, c : c + chunk, at : at + 2 * head]
                outs = []
                for h in range(2):
                    own = (lane < head) == (h == 0)
                    qm = jnp.where(own, q, jnp.zeros_like(q))
                    gm = jnp.where(own, ga, jnp.zeros_like(ga))
                    st = dot_nt(k, qm) * (scale * 1.4426950408889634)
                    p = jnp.exp2(st - lse_ref[0, 2 * pair + h : 2 * pair + h + 1, c : c + chunk])
                    gp = dot_nt(v, gm)
                    inner = jnp.sum(p * gp, 0, keepdims=True)
                    ds = (p * (gp - inner)).astype(BF)
                    dk += dot(ds, qm)
                    dv += dot(p.astype(BF), gm)
                    outs.append(dot(kt[h * head : (h + 1) * head], ds))
                dq = (jnp.concatenate(outs, 0).T * scale).astype(BF)
                gj[pl.ds(base + c, chunk), at : at + 2 * head] = dq
            gj[pl.ds(base, length), dim + at : dim + at + 2 * head] = (dk * scale).astype(BF)
            gj[pl.ds(base, length), 2 * dim + at : 2 * dim + at + 2 * head] = dv.astype(BF)

    full = group_ref[clip] == 0
    pl.when(full)(lambda: back(seq))
    pl.when(jnp.logical_not(full))(lambda: back(seq // 2))

    @pl.when(clip == 0)
    def _():
        gvec_ref[...] = jnp.zeros_like(gvec_ref)

    step = seq // 2
    for r in range(0, seq, step):
        rows = slice(r, r + step)
        here = pl.ds(base + r, step)
        gq, gk, gv = (gj[here, i * dim : (i + 1) * dim] for i in range(3))
        gvec_ref[B_QUERY : B_QUERY + 1] += colsum(gq.astype(F32))
        gvec_ref[B_VALUE : B_VALUE + 1] += colsum(gv.astype(F32))
        g = dot_nt(gq, wq_ref[...].reshape(dim, dim))
        g += dot_nt(gk, wk_ref[...].reshape(dim, dim))
        g += dot_nt(gv, wv_ref[...].reshape(dim, dim))
        masked = mask_ref[0, rows] > 0
        x_hat, r_std = normalise(jnp.where(masked, vec(EMBED), tok_ref[0, rows].astype(F32)))
        gvec_ref[GAIN1 : GAIN1 + 1] += colsum(g * x_hat)
        gvec_ref[BIAS1 : BIAS1 + 1] += colsum(g)
        total = gh_ref[0, rows] + norm_back(x_hat, r_std, g, vec(GAIN1))
        tg_ref[0, rows] = jnp.where(masked, 0.0, total).astype(BF)
        gvec_ref[EMBED : EMBED + 1] += colsum(jnp.where(masked, total, 0.0))

    @pl.when(clip == pl.num_programs(0) - 1)
    def _():
        for i in range(3):
            part = dot_tn(normed_ref[...], gj[:, i * dim : (i + 1) * dim])
            gw_ref[:, 48 * i : 48 * (i + 1), :] = part.astype(BF).reshape(BLOCKS, 48, dim)


def backward_call(group_id, tokens, mask, normed, qkv, lse, gatt, gh, vecs, w1):
    clips, seq, dim = tokens.shape
    row = lambda *tail: pl.BlockSpec((1, *tail), lambda c, *_: (c,) + (0,) * len(tail))
    whole = lambda *shape: pl.BlockSpec(shape, lambda *g: (0,) * len(shape))
    return pl.pallas_call(
        backward_kernel,
        grid_spec=pltpu.PrefetchScalarGridSpec(
            num_scalar_prefetch=1,
            grid=(clips,),
            in_specs=[
                row(seq, dim),
                row(seq, 1),
                whole(clips * seq, dim),
                row(seq, 3 * dim),
                row(HEADS, seq),
                row(seq, dim),
                row(seq, dim),
                whole(*vecs.shape),
                weight_spec(0),
                weight_spec(1),
                weight_spec(2),
            ],
            out_specs=[row(seq, dim), whole(BLOCKS, 144, dim), whole(16, dim)],
            scratch_shapes=[pltpu.VMEM((clips * seq, 3 * dim), BF)],
        ),
        out_shape=[
            jax.ShapeDtypeStruct((clips, seq, dim), BF),
            jax.ShapeDtypeStruct((BLOCKS, 144, dim), BF),
            jax.ShapeDtypeStruct((16, dim), F32),
        ],
        compiler_params=pltpu.CompilerParams(vmem_limit_bytes=VMEM_LIMIT),
        cost_estimate=pl.CostEstimate(flops=24 * 10**9, bytes_accessed=24 * 2**20, transcendentals=0),
        name="attention_backward",
    )(group_id, tokens, mask, normed.reshape(clips * seq, dim), qkv, lse, gatt, gh, vecs, w1, w1, w1)


def to_blocks(gathered, kinds):
    n, rows, dim = gathered.shape
    m = n // BLOCKS
    parts = gathered.reshape(BLOCKS, m, kinds, rows // kinds, dim)
    return jnp.swapaxes(parts, 1, 2).reshape(BLOCKS, rows * m, dim)


def from_blocks(blocks, kinds, n):
    _, rows, dim = blocks.shape
    m = n // BLOCKS
    parts = blocks.reshape(BLOCKS, kinds, m, rows // (kinds * m), dim)
    return jnp.swapaxes(parts, 1, 2).reshape(n, rows // m, dim)


def split_columns(matrix, dim):
    return [matrix[:, i : i + dim] for i in range(0, matrix.shape[1], dim)]


def local(n, tokens, mask_pos, group_id, cotangent, *masters):
    (w_qkv, b_query, b_value, w_out, b_out, w_up, b_up, w_down, b_down,
     ln1_gain, ln1_bias, ln2_gain, ln2_bias, mask_embed) = (m.astype(BF) for m in masters)
    clips, seq, dim = tokens.shape
    vec_local = jnp.concatenate(
        [b_query, b_value, b_out, b_down, ln1_gain, ln1_bias, ln2_gain, ln2_bias, mask_embed, b_up]
    )
    width = dim // n
    vec_rows = jnp.pad(vec_local, (0, 16 * dim - vec_local.shape[0])).reshape(16, dim)
    pack1 = jnp.concatenate(split_columns(w_qkv, dim) + [w_out, vec_rows], 0)
    pack2 = jnp.concatenate(split_columns(w_up, dim) + [w_down], 0)
    all1 = lax.all_gather(pack1, "fsdp", axis=0)
    all2 = lax.all_gather(pack2, "fsdp", axis=0)
    used = pack1.shape[0] - 16
    vec_all = all1[:, used, : VECS * width].reshape(n, VECS, width)
    vecs = jnp.concatenate(
        [
            jnp.swapaxes(vec_all[:, :B_UP], 0, 1).reshape(B_UP, dim),
            vec_all[:, B_UP:].reshape(4, dim),
            jnp.zeros((3, dim), BF),
        ]
    ).astype(F32)
    if n == BLOCKS:
        w1, w2 = all1, all2
    else:
        w1 = to_blocks(all1[:, :used], 4)
        up = 4 * width
        w2 = jnp.concatenate([to_blocks(all2[:, :up], 4), to_blocks(all2[:, up:], 1)], 1)

    positions = lax.iota(jnp.int32, seq)
    mask = jnp.any(mask_pos[:, :, None] == positions[None, None, :], axis=1).astype(F32)[..., None]
    normed, qkv, att, lse = forward_call(group_id, tokens, mask, vecs, w1)
    flat = lambda a: a.reshape(clips * seq, a.shape[-1])
    output, gh, gatt, g_out, g_up, g_down, gvec_mlp = mlp_call(
        group_id, flat(tokens), flat(mask), flat(cotangent), flat(att), vecs, w1, w2
    )
    token_grad, g_qkv, gvec_att = backward_call(
        group_id, tokens, mask, normed, qkv, lse, gatt.reshape(tokens.shape), gh.reshape(tokens.shape), vecs, w1
    )
    gvec = gvec_mlp + gvec_att
    gvec = jnp.concatenate(
        [
            jnp.swapaxes(gvec[:B_UP].reshape(B_UP, n, width), 0, 1),
            gvec[B_UP:VECS].reshape(n, 4, width),
        ],
        1,
    ).reshape(n, VECS * width)
    gvec = jnp.pad(gvec.astype(BF)[:, None, :], ((0, 0), (0, 15), (0, dim - VECS * width)))
    send2 = jnp.concatenate([from_blocks(g_up, 4, n), from_blocks(g_down, 1, n)], 1)
    send1 = jnp.concatenate([from_blocks(g_qkv, 3, n), from_blocks(g_out, 1, n), gvec], 1)

    def reduce(send):
        own = lax.psum_scatter(send, "fsdp", scatter_dimension=0)
        other = lax.ppermute(own, "rep", [(0, 1), (1, 0)])
        return own.astype(F32) + other.astype(F32)

    sum2, sum1 = reduce(send2), reduce(send1)
    join = lambda a, k: jnp.concatenate([a[i * width : (i + 1) * width] for i in range(k)], 1)
    vg = sum1[4 * width, : VECS * width]
    vg = [vg[i * width : (i + 1) * width] for i in range(B_UP)] + [vg[B_UP * width :]]
    return (
        output.reshape(tokens.shape),
        token_grad,
        join(sum1, 3),
        vg[B_QUERY],
        vg[B_VALUE],
        sum1[3 * width : 4 * width],
        vg[B_OUT],
        join(sum2, 4),
        vg[B_UP],
        sum2[4 * width :],
        vg[B_DOWN],
        vg[GAIN1],
        vg[BIAS1],
        vg[GAIN2],
        vg[BIAS2],
        vg[EMBED],
    )


def solution(mesh):
    clip3, clip2, clip1 = P(("rep", "fsdp"), None, None), P(("rep", "fsdp"), None), P(("rep", "fsdp"))
    mat, line = P("fsdp", None), P("fsdp")
    params = (mat, line, line, mat, line, mat, line, mat, line, line, line, line, line, line)
    return jax.shard_map(
        functools.partial(local, mesh.shape["fsdp"]),
        mesh=mesh,
        in_specs=(clip3, clip2, clip1, clip3) + params,
        out_specs=(clip3, clip3) + params,
        check_vma=False,
    )
```

```python
import functools

import jax
import jax.numpy as jnp
from jax import lax
from jax.experimental import pallas as pl
from jax.experimental.pallas import tpu as pltpu
from jax.sharding import PartitionSpec as P

HEADS = 12
BLOCKS = 16
EPS = 1e-06
BF = jnp.bfloat16
F32 = jnp.float32
VMEM_LIMIT = 56 * 1024 * 1024

B_QUERY, B_VALUE, B_OUT, B_DOWN, GAIN1, BIAS1, GAIN2, BIAS2, EMBED, B_UP = range(10)
VECS = 13


def dot(a, b):
    return jnp.dot(a, b, preferred_element_type=F32)


def dot_nt(a, b):
    return lax.dot_general(a, b, (((1,), (1,)), ((), ())), preferred_element_type=F32)


def dot_tn(a, b):
    return lax.dot_general(a, b, (((0,), (0,)), ((), ())), preferred_element_type=F32)


def normalise(values):
    centre = values - jnp.mean(values, -1, keepdims=True)
    spread = jnp.mean(centre * centre, -1, keepdims=True)
    r = lax.rsqrt(spread + EPS)
    return centre * r, r


def norm_back(x_hat, r, q, gain):
    qg = q * gain
    m1 = jnp.mean(qg, -1, keepdims=True)
    m2 = jnp.mean(qg * x_hat, -1, keepdims=True)
    return r * (qg - m1 - x_hat * m2)


def colsum(values):
    return jnp.sum(values, 0, keepdims=True)


def gelu_both(u):
    x = jnp.abs(u)
    t = pl.reciprocal(1.0 + x * (0.3275911 * 0.7071067811865476), approx=False)
    e = jnp.exp2(u * u * (-0.5 * 1.4426950408889634))
    poly = 0.5 * 1.061405429
    for c in (-1.453152027, 1.421413741, -0.284496736, 0.254829592):
        poly = poly * t + 0.5 * c
    tail = poly * t * e
    cdf = jnp.where(u < 0, tail, 1.0 - tail)
    return u * cdf, cdf + u * (e * 0.3989422804014327)


def pack_kernel(
    w_qkv, w_out, w_up, w_down, b_query, b_value, b_out, b_down, g1, b1, g2, b2, embed, b_up, one_ref, two_ref, table
):
    width, dim = w_out.shape
    for i in range(3):
        one_ref[i * width : (i + 1) * width] = w_qkv[:, i * dim : (i + 1) * dim].astype(BF)
    table[...] = jnp.zeros_like(table)
    for k, ref in enumerate((b_query, b_value, b_out, b_down, g1, b1, g2, b2, embed, b_up)):
        table[k : k + 1, 0 : ref.shape[1]] = ref[...]
    one_ref[3 * width :] = table[...].astype(BF)
    two_ref[0 : 4 * width] = w_down[...].astype(BF)
    for i in range(4):
        two_ref[(4 + i) * width : (5 + i) * width] = w_up[:, i * dim : (i + 1) * dim].astype(BF)
    two_ref[8 * width :] = w_out[...].astype(BF)


def pack_call(masters):
    (w_qkv, b_query, b_value, w_out, b_out, w_up, b_up, w_down, b_down,
     ln1_gain, ln1_bias, ln2_gain, ln2_bias, mask_embed) = masters
    width, dim = w_out.shape
    vectors = (b_query, b_value, b_out, b_down, ln1_gain, ln1_bias, ln2_gain, ln2_bias, mask_embed, b_up)
    return pl.pallas_call(
        pack_kernel,
        out_shape=[
            jax.ShapeDtypeStruct((3 * width + 16, dim), BF),
            jax.ShapeDtypeStruct((9 * width, dim), BF),
        ],
        scratch_shapes=[pltpu.VMEM((16, dim), F32)],
        name="pack",
    )(w_qkv, w_out, w_up, w_down, *(v.reshape(1, -1) for v in vectors))


def load_pieces(place, pieces, dest, sems):
    z, y, c, r = (place[i] for i in range(4))
    half = dest.shape[1] // 2
    kinds = ((0, 0, 0), (1, 0, 0), (0, 1, 0), (1, 1, 0), (1, 1, 2))
    copies = []
    for p, ref in enumerate(pieces):
        dx, dy, first = kinds[p % 5]
        dc = p // 5
        for k in range(ref.shape[0]):
            at = ((z + 4 - k - first) % 4) * 4 + (y ^ dy) * 2 + (c ^ dc)
            rows = pl.ds(pl.multiple_of((r ^ dx) * half, 16), half)
            copies.append(pltpu.make_async_copy(ref.at[k], dest.at[at, rows], sems.at[len(copies)]))
    for copy in copies:
        copy.start()
    for copy in copies:
        copy.wait()


def forward_kernel(count, group_ref, place_ref, tok_ref, mask_ref, *refs):
    pieces = refs[:count]
    normed_ref, qkv_ref, att_ref, lse_ref, vec_ref, w1_ref, sems = refs[count:]
    clip = pl.program_id(0)
    seq, dim = tok_ref.shape[1], tok_ref.shape[2]

    @pl.when(clip == 0)
    def _():
        if count == 1:
            copy = pltpu.make_async_copy(pieces[0], w1_ref, sems.at[0])
            copy.start()
            copy.wait()
        else:
            load_pieces(place_ref, pieces, w1_ref, sems)
        table = [w1_ref[i, 144:160, :].astype(F32) for i in range(BLOCKS)]
        vec_ref[0:B_UP] = jnp.concatenate([t[0:B_UP, 0:48] for t in table], 1)
        for j in range(4):
            vec_ref[B_UP + j : B_UP + j + 1] = jnp.concatenate(
                [t[B_UP : B_UP + 1, 0:192] for t in table[4 * j : 4 * j + 4]], 1
            )
        vec_ref[VECS:] = jnp.zeros((16 - VECS, dim), F32)

    vec = lambda k: vec_ref[k : k + 1, :]
    weight = lambda k: w1_ref[:, 48 * k : 48 * (k + 1), :].reshape(dim, dim)
    step = seq // 2
    for r in range(0, seq, step):
        rows = slice(r, r + step)
        blended = jnp.where(mask_ref[0, rows] > 0, vec(EMBED), tok_ref[0, rows].astype(F32))
        x_hat, _ = normalise(blended)
        normed = (x_hat * vec(GAIN1) + vec(BIAS1)).astype(BF)
        normed_ref[0, rows] = normed
        qkv_ref[0, rows, 0:dim] = (dot(normed, weight(0)) + vec(B_QUERY)).astype(BF)
        qkv_ref[0, rows, dim : 2 * dim] = dot(normed, weight(1)).astype(BF)
        qkv_ref[0, rows, 2 * dim :] = (dot(normed, weight(2)) + vec(B_VALUE)).astype(BF)
    head = dim // HEADS
    scale = head**-0.5 * 1.4426950408889634

    def attend(length):
        if length < seq:
            att_ref[0, length:, :] = jnp.zeros((seq - length, dim), BF)
            lse_ref[0, :, :] = jnp.zeros((HEADS, seq), F32)
        chunk = min(length, 256)
        lane = lax.broadcasted_iota(jnp.int32, (chunk, 2 * head), 1)
        for pair in range(HEADS // 2):
            at = pair * 2 * head
            k = qkv_ref[0, 0:length, dim + at : dim + at + 2 * head]
            vt = qkv_ref[0, 0:length, 2 * dim + at : 2 * dim + at + 2 * head].T
            for c in range(0, length, chunk):
                q = qkv_ref[0, c : c + chunk, at : at + 2 * head]
                outs = []
                for h in range(2):
                    qm = jnp.where((lane < head) == (h == 0), q, jnp.zeros_like(q))
                    st = dot_nt(k, qm) * scale
                    top = jnp.max(st, 0, keepdims=True)
                    e = jnp.exp2(st - top)
                    total = jnp.sum(e, 0, keepdims=True)
                    p = (e * (1.0 / total)).astype(BF)
                    outs.append(dot(vt[h * head : (h + 1) * head], p))
                    lse_ref[0, 2 * pair + h : 2 * pair + h + 1, c : c + chunk] = top + jnp.log2(total)
                att_ref[0, c : c + chunk, at : at + 2 * head] = jnp.concatenate(outs, 0).T.astype(BF)

    full = group_ref[clip] == 0
    pl.when(full)(lambda: attend(seq))
    pl.when(jnp.logical_not(full))(lambda: attend(seq // 2))


def weight_spec(index):
    return pl.BlockSpec((BLOCKS, 48, 768), lambda *g: (0, index, 0))


def forward_call(group_id, place, tokens, mask, pieces):
    clips, seq, dim = tokens.shape
    row = lambda *tail: pl.BlockSpec((1, *tail), lambda c, *_: (c,) + (0,) * len(tail))
    whole = lambda *shape: pl.BlockSpec(shape, lambda *g: (0,) * len(shape))
    return pl.pallas_call(
        functools.partial(forward_kernel, len(pieces)),
        grid_spec=pltpu.PrefetchScalarGridSpec(
            num_scalar_prefetch=2,
            grid=(clips,),
            in_specs=[row(seq, dim), row(seq, 1)] + [pl.BlockSpec(memory_space=pl.ANY)] * len(pieces),
            out_specs=[row(seq, dim), row(seq, 3 * dim), row(seq, dim), row(HEADS, seq), whole(16, dim), whole(BLOCKS, 160, dim)],
            scratch_shapes=[pltpu.SemaphoreType.DMA((32,))],
        ),
        out_shape=[
            jax.ShapeDtypeStruct((clips, seq, dim), BF),
            jax.ShapeDtypeStruct((clips, seq, 3 * dim), BF),
            jax.ShapeDtypeStruct((clips, seq, dim), BF),
            jax.ShapeDtypeStruct((clips, HEADS, seq), F32),
            jax.ShapeDtypeStruct((16, dim), F32),
            jax.ShapeDtypeStruct((BLOCKS, 160, dim), BF),
        ],
        compiler_params=pltpu.CompilerParams(vmem_limit_bytes=VMEM_LIMIT),
        cost_estimate=pl.CostEstimate(flops=9 * 10**9, bytes_accessed=16 * 2**20, transcendentals=0),
        name="attention_forward",
    )(group_id, place, tokens, mask, *pieces)


def mlp_kernel(
    group_ref, tok_ref, mask_ref, cot_ref, att_ref, vec_ref, wo_ref, wu_ref, wd_ref,
    out_ref, gh_ref, gatt_ref, gw_ref, gvec_ref,
    hidden, n2, gr, act, gpre, acc, gn2, stage_d, stage_u, sem_d, sem_u,
):
    j = pl.program_id(0)
    steps = pl.num_programs(0)
    slot = j % 2

    def copies(step, at):
        return (
            pltpu.make_async_copy(stage_d.at[at], gw_ref.at[pl.ds(step * 4, 4), 0:192], sem_d.at[at]),
            pltpu.make_async_copy(stage_u.at[at], gw_ref.at[:, pl.ds(pl.multiple_of(192 + 48 * step, 16), 48)], sem_u.at[at]),
        )

    rows_all, dim = tok_ref.shape
    seq = rows_all // group_ref.shape[0]
    vec = lambda k: vec_ref[k : k + 1, :]
    step = 256
    keeps = [group_ref[r // seq] == 0 if (r % seq) >= seq // 2 else None for r in range(0, rows_all, step)]
    weight = [1.0 if keep is None else jnp.where(keep, 1.0, 0.0) for keep in keeps]

    @pl.when(j == 0)
    def _():
        gvec_ref[...] = jnp.zeros_like(gvec_ref)
        w_out = wo_ref[...].reshape(dim, dim)
        for i, r in enumerate(range(0, rows_all, step)):
            rows = slice(r, r + step)
            blended = jnp.where(mask_ref[rows] > 0, vec(EMBED), tok_ref[rows].astype(F32))
            h = blended + dot(att_ref[rows], w_out) + vec(B_OUT)
            hidden[rows] = h
            x_hat, _ = normalise(h)
            n2[rows] = (x_hat * vec(GAIN2) + vec(BIAS2)).astype(BF)
            g = cot_ref[rows].astype(F32) * weight[i]
            gr[rows] = g.astype(BF)
            gvec_ref[B_DOWN : B_DOWN + 1] += colsum(g)
            acc[rows] = h + vec(B_DOWN)
            gn2[rows] = jnp.zeros((step, dim), F32)

    w_up = wu_ref[...].reshape(dim, dim)
    w_down = wd_ref[...].reshape(dim, dim)
    b_up = vec_ref[pl.ds(B_UP + j, 1), :]
    bsum = jnp.zeros((1, dim), F32)
    for r in range(0, rows_all, step):
        rows = slice(r, r + step)
        pre = dot(n2[rows], w_up) + b_up
        ga = dot_nt(gr[rows], w_down)
        value, slope = gelu_both(pre)
        value = value.astype(BF)
        act[rows] = value
        grad = (slope * ga).astype(BF)
        gpre[rows] = grad
        bsum += colsum(grad.astype(F32))
        acc[rows] += dot(value, w_down)
        gn2[rows] += dot_nt(grad, w_up)
    gvec_ref[pl.ds(B_UP + j, 1), :] = bsum

    @pl.when(j >= 2)
    def _():
        for copy in copies(j - 2, slot):
            copy.wait()

    now = copies(j, slot)
    stage_d[slot] = dot_tn(act[...], gr[...]).astype(BF).reshape(4, 192, dim)
    now[0].start()
    stage_u[slot] = dot_tn(n2[...], gpre[...]).astype(BF).reshape(BLOCKS, 48, dim)
    now[1].start()

    @pl.when(j == steps - 1)
    def _():
        w_out = wo_ref[...].reshape(dim, dim)
        for i, r in enumerate(range(0, rows_all, step)):
            rows = slice(r, r + step)
            out_ref[rows] = (acc[rows] * weight[i]).astype(BF)
            x_hat, scale = normalise(hidden[rows])
            q = gn2[rows]
            gvec_ref[GAIN2 : GAIN2 + 1] += colsum(q * x_hat)
            gvec_ref[BIAS2 : BIAS2 + 1] += colsum(q)
            gh = cot_ref[rows].astype(F32) * weight[i] + norm_back(x_hat, scale, q, vec(GAIN2))
            gh_ref[rows] = gh
            gb = gh.astype(BF)
            gpre[rows] = gb
            gvec_ref[B_OUT : B_OUT + 1] += colsum(gb.astype(F32))
            gatt_ref[rows] = dot_nt(gb, w_out).astype(BF)
        for copy in copies(j - 1, 1 - slot):
            copy.wait()
        stage_u[1 - slot] = dot_tn(att_ref[...], gpre[...]).astype(BF).reshape(BLOCKS, 48, dim)
        last = pltpu.make_async_copy(stage_u.at[1 - slot], gw_ref.at[:, 384:432], sem_u.at[1 - slot])
        last.start()
        for copy in copies(j, slot):
            copy.wait()
        last.wait()


def mlp_call(group_id, tokens, mask, cotangent, att, vecs, w2):
    rows, dim = tokens.shape
    whole = lambda *shape: pl.BlockSpec(shape, lambda *g: (0,) * len(shape))
    out = lambda shape, kind: jax.ShapeDtypeStruct(shape, kind)
    return pl.pallas_call(
        mlp_kernel,
        grid_spec=pltpu.PrefetchScalarGridSpec(
            num_scalar_prefetch=1,
            grid=(4,),
            in_specs=[
                whole(rows, dim),
                whole(rows, 1),
                whole(rows, dim),
                whole(rows, dim),
                whole(*vecs.shape),
                weight_spec(8),
                pl.BlockSpec((BLOCKS, 48, dim), lambda j, *_: (0, 4 + j, 0)),
                pl.BlockSpec((4, 192, dim), lambda j, *_: (j, 0, 0)),
            ],
            out_specs=[
                whole(rows, dim),
                whole(rows, dim),
                whole(rows, dim),
                pl.BlockSpec(memory_space=pl.ANY),
                whole(16, dim),
            ],
            scratch_shapes=[
                pltpu.VMEM((rows, dim), F32),
                pltpu.VMEM((rows, dim), BF),
                pltpu.VMEM((rows, dim), BF),
                pltpu.VMEM((rows, dim), BF),
                pltpu.VMEM((rows, dim), BF),
                pltpu.VMEM((rows, dim), F32),
                pltpu.VMEM((rows, dim), F32),
                pltpu.VMEM((2, 4, 192, dim), BF),
                pltpu.VMEM((2, BLOCKS, 48, dim), BF),
                pltpu.SemaphoreType.DMA((2,)),
                pltpu.SemaphoreType.DMA((2,)),
            ],
        ),
        out_shape=[
            out((rows, dim), BF),
            out((rows, dim), F32),
            out((rows, dim), BF),
            out((BLOCKS, 432, dim), BF),
            out((16, dim), F32),
        ],
        compiler_params=pltpu.CompilerParams(vmem_limit_bytes=VMEM_LIMIT),
        cost_estimate=pl.CostEstimate(flops=32 * 10**9, bytes_accessed=40 * 2**20, transcendentals=0),
        name="mlp",
    )(group_id, tokens, mask, cotangent, att, vecs, w2, w2, w2)


def backward_kernel(
    group_ref, tok_ref, mask_ref, normed_ref, qkv_ref, lse_ref, gatt_ref, gh_ref, vec_ref, wq_ref, wk_ref, wv_ref, gmlp_ref,
    tg_ref, gw_ref, gvec_ref, gj,
):
    clip = pl.program_id(0)
    seq, dim = tok_ref.shape[1], tok_ref.shape[2]
    vec = lambda k: vec_ref[k : k + 1, :]
    head = dim // HEADS
    scale = head**-0.5
    base = clip * seq

    def back(length):
        if length < seq:
            gj[pl.ds(base + length, seq - length), :] = jnp.zeros((seq - length, 3 * dim), BF)
        chunk = min(length, 256)
        lane = lax.broadcasted_iota(jnp.int32, (chunk, 2 * head), 1)
        for pair in range(HEADS // 2):
            at = pair * 2 * head
            k = qkv_ref[0, 0:length, dim + at : dim + at + 2 * head]
            v = qkv_ref[0, 0:length, 2 * dim + at : 2 * dim + at + 2 * head]
            kt = k.T
            dk = jnp.zeros((length, 2 * head), F32)
            dv = jnp.zeros((length, 2 * head), F32)
            for c in range(0, length, chunk):
                q = qkv_ref[0, c : c + chunk, at : at + 2 * head]
                ga = gatt_ref[0, c : c + chunk, at : at + 2 * head]
                outs = []
                for h in range(2):
                    own = (lane < head) == (h == 0)
                    qm = jnp.where(own, q, jnp.zeros_like(q))
                    gm = jnp.where(own, ga, jnp.zeros_like(ga))
                    st = dot_nt(k, qm) * (scale * 1.4426950408889634)
                    p = jnp.exp2(st - lse_ref[0, 2 * pair + h : 2 * pair + h + 1, c : c + chunk])
                    gp = dot_nt(v, gm)
                    inner = jnp.sum(p * gp, 0, keepdims=True)
                    ds = (p * (gp - inner)).astype(BF)
                    dk += dot(ds, qm)
                    dv += dot(p.astype(BF), gm)
                    outs.append(dot(kt[h * head : (h + 1) * head], ds))
                dq = (jnp.concatenate(outs, 0).T * scale).astype(BF)
                gj[pl.ds(base + c, chunk), at : at + 2 * head] = dq
            gj[pl.ds(base, length), dim + at : dim + at + 2 * head] = (dk * scale).astype(BF)
            gj[pl.ds(base, length), 2 * dim + at : 2 * dim + at + 2 * head] = dv.astype(BF)

    full = group_ref[clip] == 0
    pl.when(full)(lambda: back(seq))
    pl.when(jnp.logical_not(full))(lambda: back(seq // 2))

    @pl.when(clip == 0)
    def _():
        gvec_ref[...] = gmlp_ref[...]

    step = seq // 2
    for r in range(0, seq, step):
        rows = slice(r, r + step)
        here = pl.ds(base + r, step)
        gq, gk, gv = (gj[here, i * dim : (i + 1) * dim] for i in range(3))
        gvec_ref[B_QUERY : B_QUERY + 1] += colsum(gq.astype(F32))
        gvec_ref[B_VALUE : B_VALUE + 1] += colsum(gv.astype(F32))
        g = dot_nt(gq, wq_ref[...].reshape(dim, dim))
        g += dot_nt(gk, wk_ref[...].reshape(dim, dim))
        g += dot_nt(gv, wv_ref[...].reshape(dim, dim))
        masked = mask_ref[0, rows] > 0
        x_hat, r_std = normalise(jnp.where(masked, vec(EMBED), tok_ref[0, rows].astype(F32)))
        gvec_ref[GAIN1 : GAIN1 + 1] += colsum(g * x_hat)
        gvec_ref[BIAS1 : BIAS1 + 1] += colsum(g)
        total = gh_ref[0, rows] + norm_back(x_hat, r_std, g, vec(GAIN1))
        tg_ref[0, rows] = jnp.where(masked, 0.0, total).astype(BF)
        gvec_ref[EMBED : EMBED + 1] += colsum(jnp.where(masked, total, 0.0))

    @pl.when(clip == pl.num_programs(0) - 1)
    def _():
        for i in range(3):
            part = dot_tn(normed_ref[...], gj[:, i * dim : (i + 1) * dim])
            gw_ref[:, 48 * i : 48 * (i + 1), :] = part.astype(BF).reshape(BLOCKS, 48, dim)
        table = gvec_ref[...]
        for i in range(BLOCKS):
            few = table[0:B_UP, 48 * i : 48 * (i + 1)]
            few = jnp.concatenate([few, jnp.zeros((B_UP, dim - 48), F32)], 1)
            at = 192 * (i % 4)
            up = table[B_UP + i // 4 : B_UP + i // 4 + 1, at : at + 192]
            up = jnp.concatenate([up, jnp.zeros((1, dim - 192), F32)], 1)
            few = jnp.concatenate([few, up, jnp.zeros((16 - B_UP - 1, dim), F32)], 0)
            gw_ref[i, 144:160, :] = few.astype(BF)


def backward_call(group_id, tokens, mask, normed, qkv, lse, gatt, gh, vecs, w1, gvec):
    clips, seq, dim = tokens.shape
    row = lambda *tail: pl.BlockSpec((1, *tail), lambda c, *_: (c,) + (0,) * len(tail))
    whole = lambda *shape: pl.BlockSpec(shape, lambda *g: (0,) * len(shape))
    return pl.pallas_call(
        backward_kernel,
        grid_spec=pltpu.PrefetchScalarGridSpec(
            num_scalar_prefetch=1,
            grid=(clips,),
            in_specs=[
                row(seq, dim),
                row(seq, 1),
                whole(clips * seq, dim),
                row(seq, 3 * dim),
                row(HEADS, seq),
                row(seq, dim),
                row(seq, dim),
                whole(*vecs.shape),
                weight_spec(0),
                weight_spec(1),
                weight_spec(2),
                whole(16, dim),
            ],
            out_specs=[row(seq, dim), whole(BLOCKS, 160, dim), whole(16, dim)],
            scratch_shapes=[pltpu.VMEM((clips * seq, 3 * dim), BF)],
        ),
        out_shape=[
            jax.ShapeDtypeStruct((clips, seq, dim), BF),
            jax.ShapeDtypeStruct((BLOCKS, 160, dim), BF),
            jax.ShapeDtypeStruct((16, dim), F32),
        ],
        compiler_params=pltpu.CompilerParams(vmem_limit_bytes=VMEM_LIMIT),
        cost_estimate=pl.CostEstimate(flops=24 * 10**9, bytes_accessed=24 * 2**20, transcendentals=0),
        name="attention_backward",
    )(group_id, tokens, mask, normed.reshape(clips * seq, dim), qkv, lse, gatt, gh, vecs, w1, w1, w1, gvec)


def to_blocks(gathered, kinds):
    n, rows, dim = gathered.shape
    m = n // BLOCKS
    parts = gathered.reshape(BLOCKS, m, kinds, rows // kinds, dim)
    return jnp.swapaxes(parts, 1, 2).reshape(BLOCKS, rows * m, dim)


def from_blocks(blocks, kinds, n):
    _, rows, dim = blocks.shape
    m = n // BLOCKS
    parts = blocks.reshape(BLOCKS, kinds, m, rows // (kinds * m), dim)
    return jnp.swapaxes(parts, 1, 2).reshape(n, rows // m, dim)


def split_columns(matrix, dim):
    return [matrix[:, i : i + dim] for i in range(0, matrix.shape[1], dim)]


def swap(bit):
    return [(i, i ^ bit) for i in range(BLOCKS)]


def turn(k):
    return [(i, (i + 4 * k) % BLOCKS) for i in range(BLOCKS)]


REP = [(0, 1), (1, 0)]


def gather_pieces(pack, r):
    rows = pack.shape[0] // 2
    half = lax.dynamic_slice_in_dim(pack, r * rows, rows, 0)
    along_z = jnp.stack([half] + [lax.ppermute(half, "fsdp", turn(k)) for k in (1, 2, 3)])
    by_x = lax.ppermute(along_z, "rep", REP)
    by_y = lax.ppermute(along_z, "fsdp", swap(2))
    by_xy = lax.ppermute(by_x[:2], "fsdp", swap(2))
    by_yx = lax.ppermute(by_y[2:], "rep", REP)
    own = [along_z, by_x, by_y, by_xy, by_yx]
    return own + [lax.ppermute(piece, "fsdp", swap(1)) for piece in own]


def add(a, b):
    return (a.astype(F32) + b.astype(F32)).astype(BF)


def pick(a, i, axis):
    return lax.dynamic_index_in_dim(a, i, axis, keepdims=False)


def scatter_pieces(grads, z, y, c, r):
    _, rows, dim = grads.shape
    grads = grads.reshape(4, 2, 2, rows, dim)
    summed = add(pick(grads, c, 2), lax.ppermute(pick(grads, 1 - c, 2), "fsdp", swap(1)))
    summed = summed.reshape(4, 2, 2, rows // 2, dim)
    a, b = summed[:2], summed[2:]
    a = add(pick(a, r, 2), lax.ppermute(pick(a, 1 - r, 2), "rep", REP))
    b = add(pick(b, y, 1), lax.ppermute(pick(b, 1 - y, 1), "fsdp", swap(2)))
    a = add(pick(a, y, 1), lax.ppermute(pick(a, 1 - y, 1), "fsdp", swap(2)))
    b = add(pick(b, r, 1), lax.ppermute(pick(b, 1 - r, 1), "rep", REP))
    both = jnp.concatenate([a, b])
    total = pick(both, z, 0).astype(F32)
    for k in (1, 2, 3):
        total += lax.ppermute(pick(both, (z + k) % 4, 0), "fsdp", turn(k)).astype(F32)
    mine = total.astype(BF)
    other = lax.ppermute(mine, "rep", REP)
    return jnp.where(r == 0, jnp.concatenate([mine, other]), jnp.concatenate([other, mine])).astype(F32)


def scatter_whole(send):
    own = lax.psum_scatter(send, "fsdp", scatter_dimension=0)
    other = lax.ppermute(own, "rep", REP)
    return own.astype(F32) + other.astype(F32)


def local(n, tokens, mask_pos, group_id, cotangent, *masters):
    clips, seq, dim = tokens.shape
    width = dim // n
    me, r = lax.axis_index("fsdp"), lax.axis_index("rep")
    z, y, c = me // 4, (me // 2) % 2, me % 2
    place = jnp.stack([z, y, c, r]).astype(jnp.int32)
    if n == BLOCKS:
        pack1, pack2 = pack_call(masters)
        w2 = lax.all_gather(pack2, "fsdp", axis=0)
        pieces = gather_pieces(pack1, r)
    else:
        (w_qkv, b_query, b_value, w_out, b_out, w_up, b_up, w_down, b_down,
         ln1_gain, ln1_bias, ln2_gain, ln2_bias, mask_embed) = (m.astype(BF) for m in masters)
        gather = lambda a: lax.all_gather(a, "fsdp", axis=0)
        vec_all = gather(
            jnp.concatenate(
                [b_query, b_value, b_out, b_down, ln1_gain, ln1_bias, ln2_gain, ln2_bias, mask_embed, b_up]
            )
        )
        flat = jnp.swapaxes(vec_all[:, : B_UP * width].reshape(n, B_UP, width), 0, 1).reshape(B_UP, BLOCKS, dim // BLOCKS)
        table = jnp.zeros((BLOCKS, 16, dim), BF)
        table = table.at[:, :B_UP, : dim // BLOCKS].set(jnp.swapaxes(flat, 0, 1))
        table = table.at[:, B_UP, : 4 * dim // BLOCKS].set(vec_all[:, B_UP * width :].reshape(BLOCKS, 4 * dim // BLOCKS))
        one = to_blocks(gather(jnp.concatenate(split_columns(w_qkv, dim))), 3)
        pieces = [jnp.concatenate([one, table], 1)]
        w2 = jnp.concatenate(
            [
                to_blocks(gather(w_down), 1),
                to_blocks(gather(jnp.concatenate(split_columns(w_up, dim) + [w_out])), 5),
            ],
            1,
        )

    positions = lax.iota(jnp.int32, seq)
    mask = jnp.any(mask_pos[:, :, None] == positions[None, None, :], axis=1).astype(F32)[..., None]
    normed, qkv, att, lse, vecs, w1 = forward_call(group_id, place, tokens, mask, pieces)
    flat = lambda a: a.reshape(clips * seq, a.shape[-1])
    output, gh, gatt, g2, gvec = mlp_call(
        group_id, flat(tokens), flat(mask), flat(cotangent), flat(att), vecs, w2
    )
    token_grad, g1, _ = backward_call(
        group_id, tokens, mask, normed, qkv, lse, gatt.reshape(tokens.shape), gh.reshape(tokens.shape), vecs, w1, gvec
    )
    join = lambda a, k: jnp.concatenate([a[i * width : (i + 1) * width] for i in range(k)], 1)
    if n == BLOCKS:
        sum2 = scatter_whole(g2)
        sum1 = scatter_pieces(g1, z, y, c, r)
        qkv_grad, down_grad = join(sum1, 3), sum2[: 4 * width]
        up_grad, out_grad = join(sum2[4 * width :], 4), sum2[8 * width :]
        vg = [sum1[3 * width + k, :width] for k in range(B_UP)] + [sum1[3 * width + B_UP, : 4 * width]]
    else:
        down_grad = scatter_whole(from_blocks(g2[:, :192], 1, n))
        rest = scatter_whole(from_blocks(g2[:, 192:], 5, n))
        up_grad, out_grad = join(rest, 4), rest[4 * width :]
        qkv_grad = join(scatter_whole(from_blocks(g1[:, :144], 3, n)), 3)
        few = jnp.swapaxes(g1[:, 144 : 144 + B_UP, : dim // BLOCKS], 0, 1).reshape(B_UP, dim)
        up = g1[:, 144 + B_UP, : 4 * dim // BLOCKS].reshape(n, 4 * width)
        few = jnp.swapaxes(few.reshape(B_UP, n, width), 0, 1).reshape(n, B_UP * width)
        line = scatter_whole(jnp.concatenate([few, up], 1))
        vg = [line[i * width : (i + 1) * width] for i in range(B_UP)] + [line[B_UP * width :]]
    return (
        output.reshape(tokens.shape),
        token_grad,
        qkv_grad,
        vg[B_QUERY],
        vg[B_VALUE],
        out_grad,
        vg[B_OUT],
        up_grad,
        vg[B_UP],
        down_grad,
        vg[B_DOWN],
        vg[GAIN1],
        vg[BIAS1],
        vg[GAIN2],
        vg[BIAS2],
        vg[EMBED],
    )


def solution(mesh):
    clip3, clip2, clip1 = P(("rep", "fsdp"), None, None), P(("rep", "fsdp"), None), P(("rep", "fsdp"))
    mat, line = P("fsdp", None), P("fsdp")
    params = (mat, line, line, mat, line, mat, line, mat, line, line, line, line, line, line)
    return jax.shard_map(
        functools.partial(local, mesh.shape["fsdp"]),
        mesh=mesh,
        in_specs=(clip3, clip2, clip1, clip3) + params,
        out_specs=(clip3, clip3) + params,
        check_vma=False,
    )
```

```python
import functools

import jax
import jax.numpy as jnp
from jax import lax
from jax.experimental import pallas as pl
from jax.experimental.pallas import tpu as pltpu
from jax.sharding import PartitionSpec as P

HEADS = 12
BLOCKS = 16
EPS = 1e-06
BF = jnp.bfloat16
F32 = jnp.float32
VMEM_LIMIT = 56 * 1024 * 1024

B_QUERY, B_VALUE, B_OUT, B_DOWN, GAIN1, BIAS1, GAIN2, BIAS2, EMBED, B_UP = range(10)
VECS = 13


def dot(a, b):
    return jnp.dot(a, b, preferred_element_type=F32)


def dot_nt(a, b):
    return lax.dot_general(a, b, (((1,), (1,)), ((), ())), preferred_element_type=F32)


def dot_tn(a, b):
    return lax.dot_general(a, b, (((0,), (0,)), ((), ())), preferred_element_type=F32)


def normalise(values):
    centre = values - jnp.mean(values, -1, keepdims=True)
    spread = jnp.mean(centre * centre, -1, keepdims=True)
    r = lax.rsqrt(spread + EPS)
    return centre * r, r


def norm_back(x_hat, r, q, gain):
    qg = q * gain
    m1 = jnp.mean(qg, -1, keepdims=True)
    m2 = jnp.mean(qg * x_hat, -1, keepdims=True)
    return r * (qg - m1 - x_hat * m2)


def colsum(values):
    return jnp.sum(values, 0, keepdims=True)


def gelu_both(u):
    x = jnp.abs(u)
    t = pl.reciprocal(1.0 + x * (0.3275911 * 0.7071067811865476), approx=False)
    e = jnp.exp2(u * u * (-0.5 * 1.4426950408889634))
    poly = 0.5 * 1.061405429
    for c in (-1.453152027, 1.421413741, -0.284496736, 0.254829592):
        poly = poly * t + 0.5 * c
    tail = poly * t * e
    cdf = jnp.where(u < 0, tail, 1.0 - tail)
    return u * cdf, cdf + u * (e * 0.3989422804014327)


def pack_kernel(
    w_qkv, w_out, w_up, w_down, b_query, b_value, b_out, b_down, g1, b1, g2, b2, embed, b_up, one_ref, two_ref, table
):
    width, dim = w_out.shape
    for i in range(3):
        one_ref[i * width : (i + 1) * width] = w_qkv[:, i * dim : (i + 1) * dim].astype(BF)
    one_ref[3 * width : 4 * width] = w_out[...].astype(BF)
    table[...] = jnp.zeros_like(table)
    for k, ref in enumerate((b_query, b_value, b_out, b_down, g1, b1, g2, b2, embed, b_up)):
        table[k : k + 1, 0 : ref.shape[1]] = ref[...]
    one_ref[4 * width :] = table[...].astype(BF)
    two_ref[0 : 4 * width] = w_down[...].astype(BF)
    for i in range(4):
        two_ref[(4 + i) * width : (5 + i) * width] = w_up[:, i * dim : (i + 1) * dim].astype(BF)


def pack_call(masters):
    (w_qkv, b_query, b_value, w_out, b_out, w_up, b_up, w_down, b_down,
     ln1_gain, ln1_bias, ln2_gain, ln2_bias, mask_embed) = masters
    width, dim = w_out.shape
    vectors = (b_query, b_value, b_out, b_down, ln1_gain, ln1_bias, ln2_gain, ln2_bias, mask_embed, b_up)
    return pl.pallas_call(
        pack_kernel,
        out_shape=[
            jax.ShapeDtypeStruct((4 * width + 16, dim), BF),
            jax.ShapeDtypeStruct((8 * width, dim), BF),
        ],
        scratch_shapes=[pltpu.VMEM((16, dim), F32)],
        name="pack",
    )(w_qkv, w_out, w_up, w_down, *(v.reshape(1, -1) for v in vectors))


def load_pieces(place, pieces, dest, sems):
    z, y, c, r = (place[i] for i in range(4))
    half = dest.shape[2] // 2
    kinds = ((0, 0, 0), (1, 0, 0), (0, 1, 0), (1, 1, 0), (1, 1, 2))
    copies = []
    for p, ref in enumerate(pieces):
        dx, dy, first = kinds[p % 5]
        dc = p // 5
        for k in range(ref.shape[0]):
            at = ((z + 4 - k - first) % 4) * 4 + (y ^ dy) * 2 + (c ^ dc)
            lanes = pl.ds(pl.multiple_of((r ^ dx) * half, 128), half)
            copies.append(pltpu.make_async_copy(ref.at[k], dest.at[at, :, lanes], sems.at[len(copies)]))
    for copy in copies:
        copy.start()
    for copy in copies:
        copy.wait()


def forward_kernel(count, group_ref, place_ref, tok_ref, mask_ref, *refs):
    pieces = refs[:count]
    normed_ref, qkv_ref, att_ref, lse_ref, vec_ref, w1_ref, sems = refs[count:]
    clip = pl.program_id(0)
    seq, dim = tok_ref.shape[1], tok_ref.shape[2]

    @pl.when(clip == 0)
    def _():
        if count == 1:
            copy = pltpu.make_async_copy(pieces[0], w1_ref, sems.at[0])
            copy.start()
            copy.wait()
        else:
            load_pieces(place_ref, pieces, w1_ref, sems)
        table = [w1_ref[i, 192:208, :].astype(F32) for i in range(BLOCKS)]
        vec_ref[0:B_UP] = jnp.concatenate([t[0:B_UP, 0:48] for t in table], 1)
        for j in range(4):
            vec_ref[B_UP + j : B_UP + j + 1] = jnp.concatenate(
                [t[B_UP : B_UP + 1, 0:192] for t in table[4 * j : 4 * j + 4]], 1
            )
        vec_ref[VECS:] = jnp.zeros((16 - VECS, dim), F32)

    vec = lambda k: vec_ref[k : k + 1, :]
    weight = lambda k: w1_ref[:, 48 * k : 48 * (k + 1), :].reshape(dim, dim)
    step = seq // 2
    for r in range(0, seq, step):
        rows = slice(r, r + step)
        blended = jnp.where(mask_ref[0, rows] > 0, vec(EMBED), tok_ref[0, rows].astype(F32))
        x_hat, _ = normalise(blended)
        normed = (x_hat * vec(GAIN1) + vec(BIAS1)).astype(BF)
        normed_ref[0, rows] = normed
        qkv_ref[0, rows, 0:dim] = (dot(normed, weight(0)) + vec(B_QUERY)).astype(BF)
        qkv_ref[0, rows, dim : 2 * dim] = dot(normed, weight(1)).astype(BF)
        qkv_ref[0, rows, 2 * dim :] = (dot(normed, weight(2)) + vec(B_VALUE)).astype(BF)
    head = dim // HEADS
    scale = head**-0.5 * 1.4426950408889634

    def attend(length):
        if length < seq:
            att_ref[0, length:, :] = jnp.zeros((seq - length, dim), BF)
            lse_ref[0, :, :] = jnp.zeros((HEADS, seq), F32)
        chunk = min(length, 512)
        lane = lax.broadcasted_iota(jnp.int32, (chunk, 2 * head), 1)

        @pl.loop(0, HEADS // 2, unroll=2)
        def _(pair):
            lanes = lambda i: pl.ds(pl.multiple_of(i * dim + pair * 2 * head, 128), 2 * head)
            k = qkv_ref[0, 0:length, lanes(1)]
            vt = qkv_ref[0, 0:length, lanes(2)].T
            for c in range(0, length, chunk):
                q = qkv_ref[0, c : c + chunk, lanes(0)]
                zero = jnp.zeros_like(q)
                both = jnp.concatenate([jnp.where(lane < head, q, zero), jnp.where(lane < head, zero, q)], 0)
                st = dot_nt(k, both)
                top = jnp.max(st, 0, keepdims=True) * scale
                e = jnp.exp2(st * scale - top)
                total = jnp.sum(e, 0, keepdims=True)
                p = (e * (1.0 / total)).astype(BF)
                o0 = dot(vt[0:head], p[:, 0:chunk])
                o1 = dot(vt[head:], p[:, chunk:])
                lse = top + jnp.log2(total)
                lse_ref[0, pl.ds(2 * pair, 1), c : c + chunk] = lse[:, 0:chunk]
                lse_ref[0, pl.ds(2 * pair + 1, 1), c : c + chunk] = lse[:, chunk:]
                att_ref[0, c : c + chunk, lanes(0)] = jnp.concatenate([o0, o1], 0).T.astype(BF)

    full = group_ref[clip] == 0
    pl.when(full)(lambda: attend(seq))
    pl.when(jnp.logical_not(full))(lambda: attend(seq // 2))


def weight_spec(index):
    return pl.BlockSpec((BLOCKS, 48, 768), lambda *g: (0, index, 0))


def forward_call(group_id, place, tokens, mask, pieces):
    clips, seq, dim = tokens.shape
    row = lambda *tail: pl.BlockSpec((1, *tail), lambda c, *_: (c,) + (0,) * len(tail))
    return pl.pallas_call(
        functools.partial(forward_kernel, len(pieces)),
        grid_spec=pltpu.PrefetchScalarGridSpec(
            num_scalar_prefetch=2,
            grid=(clips,),
            in_specs=[row(seq, dim), row(seq, 1)] + [pl.BlockSpec(memory_space=pl.ANY)] * len(pieces),
            out_specs=[row(seq, dim), row(seq, 3 * dim), row(seq, dim), row(HEADS, seq), whole(16, dim), whole(BLOCKS, 208, dim)],
            scratch_shapes=[pltpu.SemaphoreType.DMA((32,))],
        ),
        out_shape=[
            jax.ShapeDtypeStruct((clips, seq, dim), BF),
            jax.ShapeDtypeStruct((clips, seq, 3 * dim), BF),
            jax.ShapeDtypeStruct((clips, seq, dim), BF),
            jax.ShapeDtypeStruct((clips, HEADS, seq), F32),
            jax.ShapeDtypeStruct((16, dim), F32),
            jax.ShapeDtypeStruct((BLOCKS, 208, dim), BF),
        ],
        compiler_params=pltpu.CompilerParams(vmem_limit_bytes=VMEM_LIMIT),
        cost_estimate=pl.CostEstimate(flops=9 * 10**9, bytes_accessed=16 * 2**20, transcendentals=0),
        name="attention_forward",
    )(group_id, place, tokens, mask, *pieces)


def store_by_core(core, value, keep_ref, send_ref, rows):
    for own in range(2):

        @pl.when(core == own)
        def _():
            keep_ref[:, rows] = value[:, own]
            send_ref[:, rows] = value[:, 1 - own]


def mlp_kernel(
    group_ref, place_ref, tok_ref, mask_ref, cot_ref, att_ref, vec_ref, wo_ref, wu_ref, wd_ref,
    out_ref, gb_ref, gw_ref, keep_ref, send_ref, gvec_ref,
    hidden, n2, gr, act, gpre, acc, gn2,
):
    j = pl.program_id(0)
    last = pl.num_programs(0) - 1
    rows_all, dim = tok_ref.shape
    seq = rows_all // group_ref.shape[0]
    vec = lambda k: vec_ref[k : k + 1, :]
    step = 256
    keeps = [group_ref[r // seq] == 0 if (r % seq) >= seq // 2 else None for r in range(0, rows_all, step)]
    weight = [1.0 if keep is None else jnp.where(keep, 1.0, 0.0) for keep in keeps]

    @pl.when(j == 0)
    def _():
        gvec_ref[...] = jnp.zeros_like(gvec_ref)
        w_out = wo_ref[...].reshape(dim, dim)
        for i, r in enumerate(range(0, rows_all, step)):
            rows = slice(r, r + step)
            blended = jnp.where(mask_ref[rows] > 0, vec(EMBED), tok_ref[rows].astype(F32))
            h = blended + dot(att_ref[rows], w_out) + vec(B_OUT)
            hidden[rows] = h
            x_hat, _ = normalise(h)
            n2[rows] = (x_hat * vec(GAIN2) + vec(BIAS2)).astype(BF)
            g = cot_ref[rows].astype(F32) * weight[i]
            gr[rows] = g.astype(BF)
            gvec_ref[B_DOWN : B_DOWN + 1] += colsum(g)
            acc[rows] = h + vec(B_DOWN)
            gn2[rows] = jnp.zeros((step, dim), F32)

    @pl.when(j < last)
    def _():
        w_up = wu_ref[...].reshape(dim, dim)
        w_down = wd_ref[...].reshape(dim, dim)
        b_up = vec_ref[pl.ds(B_UP + j, 1), :]
        bsum = jnp.zeros((1, dim), F32)
        big = 512
        for r in range(0, rows_all, big):
            rows = slice(r, r + big)
            pre = dot(n2[rows], w_up) + b_up
            ga = dot_nt(gr[rows], w_down)
            value, slope = gelu_both(pre)
            value = value.astype(BF)
            act[rows] = value
            grad = (slope * ga).astype(BF)
            gpre[rows] = grad
            bsum += colsum(grad.astype(F32))
            acc[rows] += dot(value, w_down)
            gn2[rows] += dot_nt(grad, w_up)
        gvec_ref[pl.ds(B_UP + j, 1), :] = bsum
        gw_ref[...] = dot_tn(n2[...], gpre[...]).astype(BF).reshape(gw_ref.shape)
        down = dot_tn(act[...], gr[...]).astype(BF).reshape(2, 2, 192, dim)
        store_by_core(place_ref[2], down, keep_ref, send_ref, slice(0, 192))

    @pl.when(j == last)
    def _():
        for i, r in enumerate(range(0, rows_all, step)):
            rows = slice(r, r + step)
            out_ref[rows] = (acc[rows] * weight[i]).astype(BF)
            x_hat, scale = normalise(hidden[rows])
            q = gn2[rows]
            gvec_ref[GAIN2 : GAIN2 + 1] += colsum(q * x_hat)
            gvec_ref[BIAS2 : BIAS2 + 1] += colsum(q)
            gh = cot_ref[rows].astype(F32) * weight[i] + norm_back(x_hat, scale, q, vec(GAIN2))
            gb = gh.astype(BF)
            gb_ref[rows] = gb
            gvec_ref[B_OUT : B_OUT + 1] += colsum(gb.astype(F32))
        gw_ref[...] = dot_tn(att_ref[...], gb_ref[...]).astype(BF).reshape(gw_ref.shape)


def whole(*shape):
    return pl.BlockSpec(shape, lambda *g: (0,) * len(shape))


def mlp_call(group_id, place, tokens, mask, cotangent, att, vecs, w1, w2):
    rows, dim = tokens.shape
    out = lambda shape, kind: jax.ShapeDtypeStruct(shape, kind)
    return pl.pallas_call(
        mlp_kernel,
        grid_spec=pltpu.PrefetchScalarGridSpec(
            num_scalar_prefetch=2,
            grid=(5,),
            in_specs=[
                whole(rows, dim),
                whole(rows, 1),
                whole(rows, dim),
                whole(rows, dim),
                whole(*vecs.shape),
                weight_spec(3),
                pl.BlockSpec((BLOCKS, 48, dim), lambda j, *_: (0, 4 + jnp.minimum(j, 3), 0)),
                pl.BlockSpec((4, 192, dim), lambda j, *_: (jnp.minimum(j, 3), 0, 0)),
            ],
            out_specs=[
                whole(rows, dim),
                whole(rows, dim),
                pl.BlockSpec((BLOCKS, 48, dim), lambda j, *_: (0, j, 0)),
                pl.BlockSpec((2, 192, dim), lambda j, *_: (jnp.minimum(j, 3), 0, 0)),
                pl.BlockSpec((2, 192, dim), lambda j, *_: (jnp.minimum(j, 3), 0, 0)),
                whole(16, dim),
            ],
            scratch_shapes=[
                pltpu.VMEM((rows, dim), F32),
                pltpu.VMEM((rows, dim), BF),
                pltpu.VMEM((rows, dim), BF),
                pltpu.VMEM((rows, dim), BF),
                pltpu.VMEM((rows, dim), BF),
                pltpu.VMEM((rows, dim), F32),
                pltpu.VMEM((rows, dim), F32),
            ],
        ),
        out_shape=[
            out((rows, dim), BF),
            out((rows, dim), BF),
            out((BLOCKS, 240, dim), BF),
            out((BLOCKS // 2, 192, dim), BF),
            out((BLOCKS // 2, 192, dim), BF),
            out((16, dim), F32),
        ],
        compiler_params=pltpu.CompilerParams(vmem_limit_bytes=VMEM_LIMIT),
        cost_estimate=pl.CostEstimate(flops=45 * 10**9, bytes_accessed=30 * 2**20, transcendentals=0),
        name="mlp",
    )(group_id, place, tokens, mask, cotangent, att, vecs, w1, w2, w2)


GROUPS = 2


def attention_back_kernel(
    part, group_ref, place_ref, q_ref, k_ref, v_ref, lse_ref, gb_ref, wo_ref, normed_ref, gj, keep_ref, send_ref, gatt, all_gj
):
    clip = pl.program_id(0)
    seq, dim = gb_ref.shape[1], gb_ref.shape[2]
    wide = dim // GROUPS
    head = dim // HEADS
    scale = head**-0.5
    gatt[...] = dot_nt(gb_ref[0], wo_ref[...].reshape(wide, dim)).astype(BF)

    def back(length):
        if length < seq:
            gj[0, length:, :] = jnp.zeros((seq - length, 3 * wide), BF)
        lane = lax.broadcasted_iota(jnp.int32, (length, 2 * head), 1)

        @pl.loop(0, HEADS // 2 // GROUPS)
        def _(pair):
            lanes = lambda i: pl.ds(pl.multiple_of(i * wide + pair * 2 * head, 128), 2 * head)
            k = k_ref[0, 0:length, lanes(0)]
            v = v_ref[0, 0:length, lanes(0)]
            kt = k.T
            zero = jnp.zeros((length, 2 * head), BF)
            split = lambda a: jnp.concatenate([jnp.where(lane < head, a, zero), jnp.where(lane < head, zero, a)], 0)
            q = split(q_ref[0, 0:length, lanes(0)])
            ga = split(gatt[0:length, lanes(0)])
            first = part * (HEADS // GROUPS) + 2 * pair
            lse = jnp.concatenate([lse_ref[0, pl.ds(first + h, 1), 0:length] for h in range(2)], 1)
            p = jnp.exp2(dot_nt(k, q) * (scale * 1.4426950408889634) - lse)
            gp = dot_nt(v, ga)
            inner = jnp.sum(p * gp, 0, keepdims=True)
            ds = (p * (gp - inner)).astype(BF)
            dq = [dot(kt[h * head : (h + 1) * head], ds[:, h * length : (h + 1) * length]) for h in range(2)]
            gj[0, 0:length, lanes(0)] = (jnp.concatenate(dq, 0).T * scale).astype(BF)
            gj[0, 0:length, lanes(1)] = (dot(ds, q) * scale).astype(BF)
            gj[0, 0:length, lanes(2)] = dot(p.astype(BF), ga).astype(BF)

    full = group_ref[clip] == 0
    pl.when(full)(lambda: back(seq))
    pl.when(jnp.logical_not(full))(lambda: back(seq // 2))
    all_gj[pl.ds(clip * seq, seq)] = gj[0]

    @pl.when(clip == pl.num_programs(0) - 1)
    def _():
        grad = dot_tn(normed_ref[...], all_gj[...])
        for i in range(3):
            value = grad[:, i * wide : (i + 1) * wide].astype(BF).reshape(BLOCKS // 2, 2, 48, wide)
            store_by_core(place_ref[2], value, keep_ref, send_ref, slice(48 * i, 48 * (i + 1)))


def attention_back_call(part, group_id, place, qkv, lse, gb, w1, normed):
    clips, seq, dim = gb.shape
    wide = dim // GROUPS
    columns = lambda i: pl.BlockSpec((1, seq, wide), lambda c, *_: (c, 0, GROUPS * i + part))
    row = lambda *tail: pl.BlockSpec((1, *tail), lambda c, *_: (c,) + (0,) * len(tail))
    return pl.pallas_call(
        functools.partial(attention_back_kernel, part),
        grid_spec=pltpu.PrefetchScalarGridSpec(
            num_scalar_prefetch=2,
            grid=(clips,),
            in_specs=[
                columns(0),
                columns(1),
                columns(2),
                row(HEADS, seq),
                row(seq, dim),
                pl.BlockSpec((BLOCKS // GROUPS, 48, dim), lambda *g: (part, 3, 0)),
                whole(clips * seq, dim),
            ],
            out_specs=[row(seq, 3 * wide), whole(BLOCKS // 2, 144, wide), whole(BLOCKS // 2, 144, wide)],
            scratch_shapes=[pltpu.VMEM((seq, wide), BF), pltpu.VMEM((clips * seq, 3 * wide), BF)],
        ),
        out_shape=[
            jax.ShapeDtypeStruct((clips, seq, 3 * wide), BF),
            jax.ShapeDtypeStruct((BLOCKS // 2, 144, wide), BF),
            jax.ShapeDtypeStruct((BLOCKS // 2, 144, wide), BF),
        ],
        compiler_params=pltpu.CompilerParams(vmem_limit_bytes=VMEM_LIMIT),
        cost_estimate=pl.CostEstimate(flops=10**8, bytes_accessed=2**20, transcendentals=0),
        name="attention_backward",
    )(group_id, place, qkv, qkv, qkv, lse, gb, w1, normed)


def norm_one_kernel(
    place_ref, tok_ref, mask_ref, gb_ref, gj0_ref, gj1_ref, vec_ref, wq_ref, wk_ref, wv_ref, gmlp_ref,
    tg_ref, keep_ref, send_ref, gvec_ref,
):
    step = pl.program_id(0)
    dim = tok_ref.shape[1]
    wide = dim // GROUPS
    vec = lambda k: vec_ref[k : k + 1, :]

    @pl.when(step == 0)
    def _():
        gvec_ref[...] = gmlp_ref[...]

    gq, gk, gv = (
        jnp.concatenate([ref[:, i * wide : (i + 1) * wide] for ref in (gj0_ref, gj1_ref)], 1) for i in range(3)
    )
    gvec_ref[B_QUERY : B_QUERY + 1] += colsum(gq.astype(F32))
    gvec_ref[B_VALUE : B_VALUE + 1] += colsum(gv.astype(F32))
    g = dot_nt(gq, wq_ref[...].reshape(dim, dim))
    g += dot_nt(gk, wk_ref[...].reshape(dim, dim))
    g += dot_nt(gv, wv_ref[...].reshape(dim, dim))
    masked = mask_ref[...] > 0
    x_hat, r_std = normalise(jnp.where(masked, vec(EMBED), tok_ref[...].astype(F32)))
    gvec_ref[GAIN1 : GAIN1 + 1] += colsum(g * x_hat)
    gvec_ref[BIAS1 : BIAS1 + 1] += colsum(g)
    total = gb_ref[...].astype(F32) + norm_back(x_hat, r_std, g, vec(GAIN1))
    tg_ref[...] = jnp.where(masked, 0.0, total).astype(BF)
    gvec_ref[EMBED : EMBED + 1] += colsum(jnp.where(masked, total, 0.0))

    @pl.when(step == pl.num_programs(0) - 1)
    def _():
        table = gvec_ref[...]
        for i in range(BLOCKS):
            few = table[0:B_UP, 48 * i : 48 * (i + 1)]
            few = jnp.concatenate([few, jnp.zeros((B_UP, wide - 48), F32)], 1)
            at = 192 * (i % 4)
            up = table[B_UP + i // 4 : B_UP + i // 4 + 1, at : at + 192]
            up = jnp.concatenate([up, jnp.zeros((1, wide - 192), F32)], 1)
            few = jnp.concatenate([few, up, jnp.zeros((16 - B_UP - 1, wide), F32)], 0).astype(BF)
            for ref, same in ((keep_ref, True), (send_ref, False)):

                @pl.when((place_ref[2] == i % 2) == same)
                def _():
                    ref[i // 2] = few


def norm_one_call(place, tokens, mask, gb, gj0, gj1, vecs, w1, gvec):
    rows, dim = tokens.shape
    step = rows // 4
    part = lambda width: pl.BlockSpec((step, width), lambda i, *_: (i, 0))
    small = (BLOCKS // 2, 16, dim // GROUPS)
    return pl.pallas_call(
        norm_one_kernel,
        grid_spec=pltpu.PrefetchScalarGridSpec(
            num_scalar_prefetch=1,
            grid=(4,),
            in_specs=[
                part(dim),
                part(1),
                part(dim),
                part(3 * dim // GROUPS),
                part(3 * dim // GROUPS),
                whole(*vecs.shape),
                weight_spec(0),
                weight_spec(1),
                weight_spec(2),
                whole(16, dim),
            ],
            out_specs=[part(dim), whole(*small), whole(*small)],
            scratch_shapes=[pltpu.VMEM((16, dim), F32)],
        ),
        out_shape=[
            jax.ShapeDtypeStruct((rows, dim), BF),
            jax.ShapeDtypeStruct(small, BF),
            jax.ShapeDtypeStruct(small, BF),
        ],
        compiler_params=pltpu.CompilerParams(vmem_limit_bytes=VMEM_LIMIT),
        cost_estimate=pl.CostEstimate(flops=10**8, bytes_accessed=2**20, transcendentals=0),
        name="norm_one_backward",
    )(place, tokens, mask, gb, gj0, gj1, vecs, w1, w1, w1, gvec)


def to_blocks(gathered, kinds):
    n, rows, dim = gathered.shape
    m = n // BLOCKS
    parts = gathered.reshape(BLOCKS, m, kinds, rows // kinds, dim)
    return jnp.swapaxes(parts, 1, 2).reshape(BLOCKS, rows * m, dim)


def from_blocks(blocks, kinds, n):
    _, rows, dim = blocks.shape
    m = n // BLOCKS
    parts = blocks.reshape(BLOCKS, kinds, m, rows // (kinds * m), dim)
    return jnp.swapaxes(parts, 1, 2).reshape(n, rows // m, dim)


def split_columns(matrix, dim):
    return [matrix[:, i : i + dim] for i in range(0, matrix.shape[1], dim)]


def swap(bit):
    return [(i, i ^ bit) for i in range(BLOCKS)]


def turn(k):
    return [(i, (i + 4 * k) % BLOCKS) for i in range(BLOCKS)]


REP = [(0, 1), (1, 0)]


def gather_pieces(pack, r):
    lanes = pack.shape[1] // 2
    half = lax.dynamic_slice_in_dim(pack, r * lanes, lanes, 1)
    along_z = jnp.stack([half] + [lax.ppermute(half, "fsdp", turn(k)) for k in (1, 2, 3)])
    by_x = lax.ppermute(along_z, "rep", REP)
    by_y = lax.ppermute(along_z, "fsdp", swap(2))
    by_xy = lax.ppermute(by_x[:2], "fsdp", swap(2))
    by_yx = lax.ppermute(by_y[2:], "rep", REP)
    own = [along_z, by_x, by_y, by_xy, by_yx]
    return own + [lax.ppermute(piece, "fsdp", swap(1)) for piece in own]


def add(a, b):
    return (a.astype(F32) + b.astype(F32)).astype(BF)


def pick(a, i, axis):
    return lax.dynamic_index_in_dim(a, i, axis, keepdims=False)


def half_of(a, i):
    rows = a.shape[-2] // 2
    return lax.dynamic_slice_in_dim(a, i * rows, rows, a.ndim - 2)


def scatter_steps(keep, send, z, y, r):
    _, rows, dim = keep.shape
    got = lax.ppermute(send, "fsdp", swap(1))
    kept = yield (keep,)
    summed = add(kept[0], got).reshape(4, 2, rows, dim)
    a, b = summed[:2], summed[2:]
    kept = half_of(a, r), pick(b, y, 1)
    sent = yield half_of(a, 1 - r), pick(b, 1 - y, 1), *kept
    got = lax.ppermute(sent[0], "rep", REP), lax.ppermute(sent[1], "fsdp", swap(2))
    kept = yield sent[2:]
    a, b = add(kept[0], got[0]), add(kept[1], got[1])
    sent = yield pick(a, 1 - y, 1), half_of(b, 1 - r), pick(a, y, 1), half_of(b, r)
    got = lax.ppermute(sent[0], "fsdp", swap(2)), lax.ppermute(sent[1], "rep", REP)
    kept = yield sent[2:]
    both = jnp.concatenate([add(kept[0], got[0]), add(kept[1], got[1])])
    sent = yield tuple(pick(both, (z + k) % 4, 0) for k in range(4))
    got = [lax.ppermute(sent[k], "fsdp", turn(k)) for k in (1, 2, 3)]
    kept = yield sent[:1]
    total = kept[0].astype(F32)
    for term in got:
        total += term.astype(F32)
    mine = yield (total.astype(BF),)
    other = lax.ppermute(mine[0], "rep", REP)
    mine = (yield mine)[0]
    yield jnp.where(r == 0, jnp.concatenate([mine, other]), jnp.concatenate([other, mine])).astype(F32)


class Scatter:
    def __init__(self, *args):
        self.steps = scatter_steps(*args)
        self.value = next(self.steps)

    def go(self, *ties):
        self.value, *ties = lax.optimization_barrier((self.value, *ties))
        self.value = self.steps.send(self.value)
        return ties

    def finish(self):
        while isinstance(self.value, tuple):
            self.value = self.steps.send(self.value)
        return self.value


def by_core(keep, send, c):
    first, second = jnp.where(c == 0, keep, send), jnp.where(c == 0, send, keep)
    return jnp.stack([first, second], 1).reshape(BLOCKS, *keep.shape[1:])


def scatter_whole(send):
    own = lax.psum_scatter(send, "fsdp", scatter_dimension=0)
    other = lax.ppermute(own, "rep", REP)
    return own.astype(F32) + other.astype(F32)


def local(n, tokens, mask_pos, group_id, cotangent, *masters):
    clips, seq, dim = tokens.shape
    width = dim // n
    me, r = lax.axis_index("fsdp"), lax.axis_index("rep")
    z, y, c = me // 4, (me // 2) % 2, me % 2
    place = jnp.stack([z, y, c, r]).astype(jnp.int32)
    if n == BLOCKS:
        pack1, pack2 = pack_call(masters)
        w2 = lax.all_gather(pack2, "fsdp", axis=0)
        pieces = gather_pieces(pack1, r)
    else:
        (w_qkv, b_query, b_value, w_out, b_out, w_up, b_up, w_down, b_down,
         ln1_gain, ln1_bias, ln2_gain, ln2_bias, mask_embed) = (m.astype(BF) for m in masters)
        gather = lambda a: lax.all_gather(a, "fsdp", axis=0)
        vec_all = gather(
            jnp.concatenate(
                [b_query, b_value, b_out, b_down, ln1_gain, ln1_bias, ln2_gain, ln2_bias, mask_embed, b_up]
            )
        )
        flat = jnp.swapaxes(vec_all[:, : B_UP * width].reshape(n, B_UP, width), 0, 1).reshape(B_UP, BLOCKS, dim // BLOCKS)
        table = jnp.zeros((BLOCKS, 16, dim), BF)
        table = table.at[:, :B_UP, : dim // BLOCKS].set(jnp.swapaxes(flat, 0, 1))
        table = table.at[:, B_UP, : 4 * dim // BLOCKS].set(vec_all[:, B_UP * width :].reshape(BLOCKS, 4 * dim // BLOCKS))
        one = to_blocks(gather(jnp.concatenate(split_columns(w_qkv, dim) + [w_out])), 4)
        pieces = [jnp.concatenate([one, table], 1)]
        w2 = jnp.concatenate(
            [to_blocks(gather(w_down), 1), to_blocks(gather(jnp.concatenate(split_columns(w_up, dim))), 4)], 1
        )

    positions = lax.iota(jnp.int32, seq)
    mask = jnp.any(mask_pos[:, :, None] == positions[None, None, :], axis=1).astype(F32)[..., None]
    normed, qkv, att, lse, vecs, w1 = forward_call(group_id, place, tokens, mask, pieces)
    flat = lambda a: a.reshape(clips * seq, a.shape[-1])
    output, gb, g2, down_keep, down_send, gvec = mlp_call(
        group_id, place, flat(tokens), flat(mask), flat(cotangent), flat(att), vecs, w1, w2
    )
    gb3 = gb.reshape(tokens.shape)
    wide = dim // GROUPS
    back = lambda part, gb3: attention_back_call(part, group_id, place, qkv, lse, gb3, w1, flat(normed))
    after = lambda gj0, gj1, gvec: norm_one_call(place, flat(tokens), flat(mask), gb, flat(gj0), flat(gj1), vecs, w1, gvec)
    if n == BLOCKS:
        down = Scatter(down_keep, down_send, z, y, r)
        down.go()
        (gb3,) = down.go(gb3)
        gj0, keep0, send0 = back(0, gb3)
        keep0, send0 = down.go(keep0, send0)
        (gb3,) = down.go(gb3)
        first = Scatter(keep0, send0, z, y, r)
        gj1, keep1, send1 = back(1, gb3)
        keep1, send1 = down.go(keep1, send1)
        (gvec,) = down.go(gvec)
        first.go()
        (gvec,) = first.go(gvec)
        token_grad, keep2, send2 = after(gj0, gj1, gvec)
        keep2, send2 = down.go(keep2, send2)
        keep2, send2 = first.go(keep2, send2)
        second = Scatter(jnp.concatenate([keep1, keep2], 1), jnp.concatenate([send1, send2], 1), z, y, r)
        down_grad = down.finish()
        sum0 = first.finish()
        sum1 = second.finish()
        sum2 = scatter_whole(g2)
        up_grad, out_grad = sum2[: 4 * width], sum2[4 * width :]
        qkv_grad = jnp.concatenate([a[i * width : (i + 1) * width] for i in range(3) for a in (sum0, sum1)], 1)
        vg = [sum1[3 * width + k, :width] for k in range(B_UP)] + [sum1[3 * width + B_UP, : 4 * width]]
    else:
        (gj0, *parts0), (gj1, *parts1) = (back(part, gb3) for part in range(GROUPS))
        token_grad, *table = after(gj0, gj1, gvec)
        down_grad = scatter_whole(from_blocks(by_core(down_keep, down_send, place[2]), 1, n))
        rest = scatter_whole(from_blocks(g2, 5, n))
        up_grad, out_grad = rest[: 4 * width], rest[4 * width :]
        sums = [scatter_whole(from_blocks(by_core(*parts, place[2]), 3, n)) for parts in (parts0, parts1)]
        qkv_grad = jnp.concatenate([a[i * width : (i + 1) * width] for i in range(3) for a in sums], 1)
        table = by_core(*table, place[2])
        few = jnp.swapaxes(table[:, :B_UP, : dim // BLOCKS], 0, 1).reshape(B_UP, n, width)
        few = jnp.swapaxes(few, 0, 1).reshape(n, B_UP * width)
        line = scatter_whole(jnp.concatenate([few, table[:, B_UP, : 4 * dim // BLOCKS].reshape(n, 4 * width)], 1))
        vg = [line[i * width : (i + 1) * width] for i in range(B_UP)] + [line[B_UP * width :]]
    up_grad = jnp.concatenate([up_grad[i * width : (i + 1) * width] for i in range(4)], 1)
    return (
        output.reshape(tokens.shape),
        token_grad.reshape(tokens.shape),
        qkv_grad,
        vg[B_QUERY],
        vg[B_VALUE],
        out_grad,
        vg[B_OUT],
        up_grad,
        vg[B_UP],
        down_grad,
        vg[B_DOWN],
        vg[GAIN1],
        vg[BIAS1],
        vg[GAIN2],
        vg[BIAS2],
        vg[EMBED],
    )


def solution(mesh):
    clip3, clip2, clip1 = P(("rep", "fsdp"), None, None), P(("rep", "fsdp"), None), P(("rep", "fsdp"))
    mat, line = P("fsdp", None), P("fsdp")
    params = (mat, line, line, mat, line, mat, line, mat, line, line, line, line, line, line)
    return jax.shard_map(
        functools.partial(local, mesh.shape["fsdp"]),
        mesh=mesh,
        in_specs=(clip3, clip2, clip1, clip3) + params,
        out_specs=(clip3, clip3) + params,
        check_vma=False,
    )
```

```python
import functools

import jax
import jax.numpy as jnp
from jax import lax
from jax.experimental import pallas as pl
from jax.experimental.pallas import tpu as pltpu
from jax.sharding import PartitionSpec as P

HEADS = 12
BLOCKS = 16
EPS = 1e-06
BF = jnp.bfloat16
F32 = jnp.float32
VMEM_LIMIT = 56 * 1024 * 1024

B_QUERY, B_VALUE, B_OUT, B_DOWN, GAIN1, BIAS1, GAIN2, BIAS2, EMBED, B_UP = range(10)
VECS = 13


def dot(a, b):
    return jnp.dot(a, b, preferred_element_type=F32)


def dot_nt(a, b):
    return lax.dot_general(a, b, (((1,), (1,)), ((), ())), preferred_element_type=F32)


def dot_tn(a, b):
    return lax.dot_general(a, b, (((0,), (0,)), ((), ())), preferred_element_type=F32)


def normalise(values):
    centre = values - jnp.mean(values, -1, keepdims=True)
    spread = jnp.mean(centre * centre, -1, keepdims=True)
    r = lax.rsqrt(spread + EPS)
    return centre * r, r


def norm_back(x_hat, r, q, gain):
    qg = q * gain
    m1 = jnp.mean(qg, -1, keepdims=True)
    m2 = jnp.mean(qg * x_hat, -1, keepdims=True)
    return r * (qg - m1 - x_hat * m2)


def colsum(values):
    return jnp.sum(values, 0, keepdims=True)


def gelu_both(u):
    x = jnp.abs(u)
    t = pl.reciprocal(1.0 + x * (0.3275911 * 0.7071067811865476), approx=False)
    e = jnp.exp2(u * u * (-0.5 * 1.4426950408889634))
    poly = 0.5 * 1.061405429
    for c in (-1.453152027, 1.421413741, -0.284496736, 0.254829592):
        poly = poly * t + 0.5 * c
    tail = poly * t * e
    cdf = jnp.where(u < 0, tail, 1.0 - tail)
    return u * cdf, cdf + u * (e * 0.3989422804014327)


def pack_kernel(
    w_qkv, w_out, w_up, w_down, b_query, b_value, b_out, b_down, g1, b1, g2, b2, embed, b_up, one_ref, two_ref, table
):
    width, dim = w_out.shape
    for i in range(3):
        one_ref[i * width : (i + 1) * width] = w_qkv[:, i * dim : (i + 1) * dim].astype(BF)
    one_ref[3 * width : 4 * width] = w_out[...].astype(BF)
    table[...] = jnp.zeros_like(table)
    for k, ref in enumerate((b_query, b_value, b_out, b_down, g1, b1, g2, b2, embed, b_up)):
        table[k : k + 1, 0 : ref.shape[1]] = ref[...]
    one_ref[4 * width :] = table[...].astype(BF)
    two_ref[0 : 4 * width] = w_down[...].astype(BF)
    for i in range(4):
        two_ref[(4 + i) * width : (5 + i) * width] = w_up[:, i * dim : (i + 1) * dim].astype(BF)


def pack_call(masters):
    (w_qkv, b_query, b_value, w_out, b_out, w_up, b_up, w_down, b_down,
     ln1_gain, ln1_bias, ln2_gain, ln2_bias, mask_embed) = masters
    width, dim = w_out.shape
    vectors = (b_query, b_value, b_out, b_down, ln1_gain, ln1_bias, ln2_gain, ln2_bias, mask_embed, b_up)
    return pl.pallas_call(
        pack_kernel,
        out_shape=[
            jax.ShapeDtypeStruct((4 * width + 16, dim), BF),
            jax.ShapeDtypeStruct((8 * width, dim), BF),
        ],
        scratch_shapes=[pltpu.VMEM((16, dim), F32)],
        name="pack",
    )(w_qkv, w_out, w_up, w_down, *(v.reshape(1, -1) for v in vectors))


def load_pieces(place, pieces, dest, sems):
    z, y, c, r = (place[i] for i in range(4))
    half = dest.shape[2] // 2
    kinds = ((0, 0, 0), (1, 0, 0), (0, 1, 0), (1, 1, 0), (1, 1, 2))
    copies = []
    for p, ref in enumerate(pieces):
        dx, dy, first = kinds[p % 5]
        dc = p // 5
        for k in range(ref.shape[0]):
            at = ((z + 4 - k - first) % 4) * 4 + (y ^ dy) * 2 + (c ^ dc)
            lanes = pl.ds(pl.multiple_of((r ^ dx) * half, 128), half)
            copies.append(pltpu.make_async_copy(ref.at[k], dest.at[at, :, lanes], sems.at[len(copies)]))
    for copy in copies:
        copy.start()
    for copy in copies:
        copy.wait()


def forward_kernel(count, group_ref, place_ref, tok_ref, mask_ref, *refs):
    pieces = refs[:count]
    normed_ref, qkv_ref, att_ref, lse_ref, vec_ref, w1_ref, sems = refs[count:]
    clip = pl.program_id(0)
    seq, dim = tok_ref.shape[1], tok_ref.shape[2]

    @pl.when(clip == 0)
    def _():
        if count == 1:
            copy = pltpu.make_async_copy(pieces[0], w1_ref, sems.at[0])
            copy.start()
            copy.wait()
        else:
            load_pieces(place_ref, pieces, w1_ref, sems)
        table = [w1_ref[i, 192:208, :].astype(F32) for i in range(BLOCKS)]
        vec_ref[0:B_UP] = jnp.concatenate([t[0:B_UP, 0:48] for t in table], 1)
        for j in range(4):
            vec_ref[B_UP + j : B_UP + j + 1] = jnp.concatenate(
                [t[B_UP : B_UP + 1, 0:192] for t in table[4 * j : 4 * j + 4]], 1
            )
        vec_ref[VECS:] = jnp.zeros((16 - VECS, dim), F32)

    vec = lambda k: vec_ref[k : k + 1, :]
    weight = lambda k: w1_ref[:, 48 * k : 48 * (k + 1), :].reshape(dim, dim)
    step = seq // 2
    for r in range(0, seq, step):
        rows = slice(r, r + step)
        blended = jnp.where(mask_ref[0, rows] > 0, vec(EMBED), tok_ref[0, rows].astype(F32))
        x_hat, _ = normalise(blended)
        normed = (x_hat * vec(GAIN1) + vec(BIAS1)).astype(BF)
        normed_ref[0, rows] = normed
        qkv_ref[0, rows, 0:dim] = (dot(normed, weight(0)) + vec(B_QUERY)).astype(BF)
        qkv_ref[0, rows, dim : 2 * dim] = dot(normed, weight(1)).astype(BF)
        qkv_ref[0, rows, 2 * dim :] = (dot(normed, weight(2)) + vec(B_VALUE)).astype(BF)
    head = dim // HEADS
    scale = head**-0.5 * 1.4426950408889634

    def attend(length):
        if length < seq:
            att_ref[0, length:, :] = jnp.zeros((seq - length, dim), BF)
            lse_ref[0, :, :] = jnp.zeros((HEADS, seq), F32)
        chunk = min(length, 512)
        lane = lax.broadcasted_iota(jnp.int32, (chunk, 2 * head), 1)

        @pl.loop(0, HEADS // 2, unroll=2)
        def _(pair):
            lanes = lambda i: pl.ds(pl.multiple_of(i * dim + pair * 2 * head, 128), 2 * head)
            k = qkv_ref[0, 0:length, lanes(1)]
            vt = qkv_ref[0, 0:length, lanes(2)].T
            for c in range(0, length, chunk):
                q = qkv_ref[0, c : c + chunk, lanes(0)]
                zero = jnp.zeros_like(q)
                both = jnp.concatenate([jnp.where(lane < head, q, zero), jnp.where(lane < head, zero, q)], 0)
                st = dot_nt(k, both)
                top = jnp.max(st, 0, keepdims=True) * scale
                e = jnp.exp2(st * scale - top)
                total = jnp.sum(e, 0, keepdims=True)
                p = (e * (1.0 / total)).astype(BF)
                o0 = dot(vt[0:head], p[:, 0:chunk])
                o1 = dot(vt[head:], p[:, chunk:])
                lse = top + jnp.log2(total)
                lse_ref[0, pl.ds(2 * pair, 1), c : c + chunk] = lse[:, 0:chunk]
                lse_ref[0, pl.ds(2 * pair + 1, 1), c : c + chunk] = lse[:, chunk:]
                att_ref[0, c : c + chunk, lanes(0)] = jnp.concatenate([o0, o1], 0).T.astype(BF)

    full = group_ref[clip] == 0
    pl.when(full)(lambda: attend(seq))
    pl.when(jnp.logical_not(full))(lambda: attend(seq // 2))


def weight_spec(index):
    return pl.BlockSpec((BLOCKS, 48, 768), lambda *g: (0, index, 0))


def forward_call(group_id, place, tokens, mask, pieces):
    clips, seq, dim = tokens.shape
    row = lambda *tail: pl.BlockSpec((1, *tail), lambda c, *_: (c,) + (0,) * len(tail))
    return pl.pallas_call(
        functools.partial(forward_kernel, len(pieces)),
        grid_spec=pltpu.PrefetchScalarGridSpec(
            num_scalar_prefetch=2,
            grid=(clips,),
            in_specs=[row(seq, dim), row(seq, 1)] + [pl.BlockSpec(memory_space=pl.ANY)] * len(pieces),
            out_specs=[row(seq, dim), row(seq, 3 * dim), row(seq, dim), row(HEADS, seq), whole(16, dim), whole(BLOCKS, 208, dim)],
            scratch_shapes=[pltpu.SemaphoreType.DMA((32,))],
        ),
        out_shape=[
            jax.ShapeDtypeStruct((clips, seq, dim), BF),
            jax.ShapeDtypeStruct((clips, seq, 3 * dim), BF),
            jax.ShapeDtypeStruct((clips, seq, dim), BF),
            jax.ShapeDtypeStruct((clips, HEADS, seq), F32),
            jax.ShapeDtypeStruct((16, dim), F32),
            jax.ShapeDtypeStruct((BLOCKS, 208, dim), BF),
        ],
        compiler_params=pltpu.CompilerParams(vmem_limit_bytes=VMEM_LIMIT),
        cost_estimate=pl.CostEstimate(flops=9 * 10**9, bytes_accessed=16 * 2**20, transcendentals=0),
        name="attention_forward",
    )(group_id, place, tokens, mask, *pieces)


def store_by_core(core, value, keep_ref, send_ref, rows):
    for own in range(2):

        @pl.when(core == own)
        def _():
            keep_ref[:, rows] = value[:, own]
            send_ref[:, rows] = value[:, 1 - own]


def mlp_kernel(
    group_ref, place_ref, tok_ref, mask_ref, cot_ref, att_ref, vec_ref, wo_ref, wu_ref, wd_ref,
    out_ref, gb_ref, gw_ref, keep_ref, send_ref, gvec_ref,
    hidden, n2, gr, act, gpre, acc, gn2,
):
    j = pl.program_id(0)
    last = pl.num_programs(0) - 1
    rows_all, dim = tok_ref.shape
    seq = rows_all // group_ref.shape[0]
    vec = lambda k: vec_ref[k : k + 1, :]
    step = 256
    keeps = [group_ref[r // seq] == 0 if (r % seq) >= seq // 2 else None for r in range(0, rows_all, step)]
    weight = [1.0 if keep is None else jnp.where(keep, 1.0, 0.0) for keep in keeps]

    @pl.when(j == 0)
    def _():
        gvec_ref[...] = jnp.zeros_like(gvec_ref)
        w_out = wo_ref[...].reshape(dim, dim)
        for i, r in enumerate(range(0, rows_all, step)):
            rows = slice(r, r + step)
            blended = jnp.where(mask_ref[rows] > 0, vec(EMBED), tok_ref[rows].astype(F32))
            h = blended + dot(att_ref[rows], w_out) + vec(B_OUT)
            hidden[rows] = h
            x_hat, _ = normalise(h)
            n2[rows] = (x_hat * vec(GAIN2) + vec(BIAS2)).astype(BF)
            g = cot_ref[rows].astype(F32) * weight[i]
            gr[rows] = g.astype(BF)
            gvec_ref[B_DOWN : B_DOWN + 1] += colsum(g)
            acc[rows] = h + vec(B_DOWN)
            gn2[rows] = jnp.zeros((step, dim), F32)

    @pl.when(j < last)
    def _():
        w_up = wu_ref[...].reshape(dim, dim)
        w_down = wd_ref[...].reshape(dim, dim)
        b_up = vec_ref[pl.ds(B_UP + j, 1), :]
        bsum = jnp.zeros((1, dim), F32)
        big = 512
        for r in range(0, rows_all, big):
            rows = slice(r, r + big)
            pre = dot(n2[rows], w_up) + b_up
            ga = dot_nt(gr[rows], w_down)
            value, slope = gelu_both(pre)
            value = value.astype(BF)
            act[rows] = value
            grad = (slope * ga).astype(BF)
            gpre[rows] = grad
            bsum += colsum(grad.astype(F32))
            acc[rows] += dot(value, w_down)
            gn2[rows] += dot_nt(grad, w_up)
        gvec_ref[pl.ds(B_UP + j, 1), :] = bsum
        gw_ref[...] = dot_tn(n2[...], gpre[...]).astype(BF).reshape(gw_ref.shape)
        down = dot_tn(act[...], gr[...]).astype(BF).reshape(2, 2, 192, dim)
        store_by_core(place_ref[2], down, keep_ref, send_ref, slice(0, 192))

    @pl.when(j == last)
    def _():
        for i, r in enumerate(range(0, rows_all, step)):
            rows = slice(r, r + step)
            out_ref[rows] = (acc[rows] * weight[i]).astype(BF)
            x_hat, scale = normalise(hidden[rows])
            q = gn2[rows]
            gvec_ref[GAIN2 : GAIN2 + 1] += colsum(q * x_hat)
            gvec_ref[BIAS2 : BIAS2 + 1] += colsum(q)
            gh = cot_ref[rows].astype(F32) * weight[i] + norm_back(x_hat, scale, q, vec(GAIN2))
            gb = gh.astype(BF)
            gb_ref[rows] = gb
            gvec_ref[B_OUT : B_OUT + 1] += colsum(gb.astype(F32))
        gw_ref[...] = dot_tn(att_ref[...], gb_ref[...]).astype(BF).reshape(gw_ref.shape)


def whole(*shape):
    return pl.BlockSpec(shape, lambda *g: (0,) * len(shape))


def mlp_call(group_id, place, tokens, mask, cotangent, att, vecs, w1, w2):
    rows, dim = tokens.shape
    out = lambda shape, kind: jax.ShapeDtypeStruct(shape, kind)
    return pl.pallas_call(
        mlp_kernel,
        grid_spec=pltpu.PrefetchScalarGridSpec(
            num_scalar_prefetch=2,
            grid=(5,),
            in_specs=[
                whole(rows, dim),
                whole(rows, 1),
                whole(rows, dim),
                whole(rows, dim),
                whole(*vecs.shape),
                weight_spec(3),
                pl.BlockSpec((BLOCKS, 48, dim), lambda j, *_: (0, 4 + jnp.minimum(j, 3), 0)),
                pl.BlockSpec((4, 192, dim), lambda j, *_: (jnp.minimum(j, 3), 0, 0)),
            ],
            out_specs=[
                whole(rows, dim),
                whole(rows, dim),
                pl.BlockSpec((BLOCKS, 48, dim), lambda j, *_: (0, j, 0)),
                pl.BlockSpec((2, 192, dim), lambda j, *_: (jnp.minimum(j, 3), 0, 0)),
                pl.BlockSpec((2, 192, dim), lambda j, *_: (jnp.minimum(j, 3), 0, 0)),
                whole(16, dim),
            ],
            scratch_shapes=[
                pltpu.VMEM((rows, dim), F32),
                pltpu.VMEM((rows, dim), BF),
                pltpu.VMEM((rows, dim), BF),
                pltpu.VMEM((rows, dim), BF),
                pltpu.VMEM((rows, dim), BF),
                pltpu.VMEM((rows, dim), F32),
                pltpu.VMEM((rows, dim), F32),
            ],
        ),
        out_shape=[
            out((rows, dim), BF),
            out((rows, dim), BF),
            out((BLOCKS, 240, dim), BF),
            out((BLOCKS // 2, 192, dim), BF),
            out((BLOCKS // 2, 192, dim), BF),
            out((16, dim), F32),
        ],
        compiler_params=pltpu.CompilerParams(vmem_limit_bytes=VMEM_LIMIT),
        cost_estimate=pl.CostEstimate(flops=45 * 10**9, bytes_accessed=30 * 2**20, transcendentals=0),
        name="mlp",
    )(group_id, place, tokens, mask, cotangent, att, vecs, w1, w2, w2)


GROUPS = 2


def attention_back_kernel(
    part, group_ref, place_ref, q_ref, k_ref, v_ref, lse_ref, gb_ref, wo_ref, normed_ref, gj, keep_ref, send_ref, gatt, all_gj
):
    clip = pl.program_id(0)
    seq, dim = gb_ref.shape[1], gb_ref.shape[2]
    wide = dim // GROUPS
    head = dim // HEADS
    scale = head**-0.5
    gatt[...] = dot_nt(gb_ref[0], wo_ref[...].reshape(wide, dim)).astype(BF)

    def back(length):
        if length < seq:
            gj[0, length:, :] = jnp.zeros((seq - length, 3 * wide), BF)
        lane = lax.broadcasted_iota(jnp.int32, (length, 2 * head), 1)

        @pl.loop(0, HEADS // 2 // GROUPS)
        def _(pair):
            lanes = lambda i: pl.ds(pl.multiple_of(i * wide + pair * 2 * head, 128), 2 * head)
            k = k_ref[0, 0:length, lanes(0)]
            v = v_ref[0, 0:length, lanes(0)]
            kt = k.T
            zero = jnp.zeros((length, 2 * head), BF)
            split = lambda a: jnp.concatenate([jnp.where(lane < head, a, zero), jnp.where(lane < head, zero, a)], 0)
            q = split(q_ref[0, 0:length, lanes(0)])
            ga = split(gatt[0:length, lanes(0)])
            first = part * (HEADS // GROUPS) + 2 * pair
            lse = jnp.concatenate([lse_ref[0, pl.ds(first + h, 1), 0:length] for h in range(2)], 1)
            p = jnp.exp2(dot_nt(k, q) * (scale * 1.4426950408889634) - lse)
            gp = dot_nt(v, ga)
            inner = jnp.sum(p * gp, 0, keepdims=True)
            ds = (p * (gp - inner)).astype(BF)
            dq = [dot(kt[h * head : (h + 1) * head], ds[:, h * length : (h + 1) * length]) for h in range(2)]
            gj[0, 0:length, lanes(0)] = (jnp.concatenate(dq, 0).T * scale).astype(BF)
            gj[0, 0:length, lanes(1)] = (dot(ds, q) * scale).astype(BF)
            gj[0, 0:length, lanes(2)] = dot(p.astype(BF), ga).astype(BF)

    full = group_ref[clip] == 0
    pl.when(full)(lambda: back(seq))
    pl.when(jnp.logical_not(full))(lambda: back(seq // 2))
    all_gj[pl.ds(clip * seq, seq)] = gj[0]

    @pl.when(clip == pl.num_programs(0) - 1)
    def _():
        grad = dot_tn(normed_ref[...], all_gj[...])
        for i in range(3):
            value = grad[:, i * wide : (i + 1) * wide].astype(BF).reshape(BLOCKS // 2, 2, 48, wide)
            store_by_core(place_ref[2], value, keep_ref, send_ref, slice(48 * i, 48 * (i + 1)))


def attention_back_call(part, group_id, place, qkv, lse, gb, w1, normed):
    clips, seq, dim = gb.shape
    wide = dim // GROUPS
    columns = lambda i: pl.BlockSpec((1, seq, wide), lambda c, *_: (c, 0, GROUPS * i + part))
    row = lambda *tail: pl.BlockSpec((1, *tail), lambda c, *_: (c,) + (0,) * len(tail))
    return pl.pallas_call(
        functools.partial(attention_back_kernel, part),
        grid_spec=pltpu.PrefetchScalarGridSpec(
            num_scalar_prefetch=2,
            grid=(clips,),
            in_specs=[
                columns(0),
                columns(1),
                columns(2),
                row(HEADS, seq),
                row(seq, dim),
                pl.BlockSpec((BLOCKS // GROUPS, 48, dim), lambda *g: (part, 3, 0)),
                whole(clips * seq, dim),
            ],
            out_specs=[row(seq, 3 * wide), whole(BLOCKS // 2, 144, wide), whole(BLOCKS // 2, 144, wide)],
            scratch_shapes=[pltpu.VMEM((seq, wide), BF), pltpu.VMEM((clips * seq, 3 * wide), BF)],
        ),
        out_shape=[
            jax.ShapeDtypeStruct((clips, seq, 3 * wide), BF),
            jax.ShapeDtypeStruct((BLOCKS // 2, 144, wide), BF),
            jax.ShapeDtypeStruct((BLOCKS // 2, 144, wide), BF),
        ],
        compiler_params=pltpu.CompilerParams(vmem_limit_bytes=VMEM_LIMIT),
        cost_estimate=pl.CostEstimate(flops=10**8, bytes_accessed=2**20, transcendentals=0),
        name="attention_backward",
    )(group_id, place, qkv, qkv, qkv, lse, gb, w1, normed)


def norm_one_kernel(
    place_ref, tok_ref, mask_ref, gb_ref, gj0_ref, gj1_ref, vec_ref, wq_ref, wk_ref, wv_ref, gmlp_ref,
    tg_ref, keep_ref, send_ref, gvec_ref,
):
    step = pl.program_id(0)
    dim = tok_ref.shape[1]
    wide = dim // GROUPS
    vec = lambda k: vec_ref[k : k + 1, :]

    @pl.when(step == 0)
    def _():
        gvec_ref[...] = gmlp_ref[...]

    gq, gk, gv = (
        jnp.concatenate([ref[:, i * wide : (i + 1) * wide] for ref in (gj0_ref, gj1_ref)], 1) for i in range(3)
    )
    gvec_ref[B_QUERY : B_QUERY + 1] += colsum(gq.astype(F32))
    gvec_ref[B_VALUE : B_VALUE + 1] += colsum(gv.astype(F32))
    g = dot_nt(gq, wq_ref[...].reshape(dim, dim))
    g += dot_nt(gk, wk_ref[...].reshape(dim, dim))
    g += dot_nt(gv, wv_ref[...].reshape(dim, dim))
    masked = mask_ref[...] > 0
    x_hat, r_std = normalise(jnp.where(masked, vec(EMBED), tok_ref[...].astype(F32)))
    gvec_ref[GAIN1 : GAIN1 + 1] += colsum(g * x_hat)
    gvec_ref[BIAS1 : BIAS1 + 1] += colsum(g)
    total = gb_ref[...].astype(F32) + norm_back(x_hat, r_std, g, vec(GAIN1))
    tg_ref[...] = jnp.where(masked, 0.0, total).astype(BF)
    gvec_ref[EMBED : EMBED + 1] += colsum(jnp.where(masked, total, 0.0))

    @pl.when(step == pl.num_programs(0) - 1)
    def _():
        table = gvec_ref[...]
        for i in range(BLOCKS):
            few = table[0:B_UP, 48 * i : 48 * (i + 1)]
            few = jnp.concatenate([few, jnp.zeros((B_UP, wide - 48), F32)], 1)
            at = 192 * (i % 4)
            up = table[B_UP + i // 4 : B_UP + i // 4 + 1, at : at + 192]
            up = jnp.concatenate([up, jnp.zeros((1, wide - 192), F32)], 1)
            few = jnp.concatenate([few, up, jnp.zeros((16 - B_UP - 1, wide), F32)], 0).astype(BF)
            for ref, same in ((keep_ref, True), (send_ref, False)):

                @pl.when((place_ref[2] == i % 2) == same)
                def _():
                    ref[i // 2] = few


def norm_one_call(place, tokens, mask, gb, gj0, gj1, vecs, w1, gvec):
    rows, dim = tokens.shape
    step = rows // 4
    part = lambda width: pl.BlockSpec((step, width), lambda i, *_: (i, 0))
    small = (BLOCKS // 2, 16, dim // GROUPS)
    return pl.pallas_call(
        norm_one_kernel,
        grid_spec=pltpu.PrefetchScalarGridSpec(
            num_scalar_prefetch=1,
            grid=(4,),
            in_specs=[
                part(dim),
                part(1),
                part(dim),
                part(3 * dim // GROUPS),
                part(3 * dim // GROUPS),
                whole(*vecs.shape),
                weight_spec(0),
                weight_spec(1),
                weight_spec(2),
                whole(16, dim),
            ],
            out_specs=[part(dim), whole(*small), whole(*small)],
            scratch_shapes=[pltpu.VMEM((16, dim), F32)],
        ),
        out_shape=[
            jax.ShapeDtypeStruct((rows, dim), BF),
            jax.ShapeDtypeStruct(small, BF),
            jax.ShapeDtypeStruct(small, BF),
        ],
        compiler_params=pltpu.CompilerParams(vmem_limit_bytes=VMEM_LIMIT),
        cost_estimate=pl.CostEstimate(flops=10**8, bytes_accessed=2**20, transcendentals=0),
        name="norm_one_backward",
    )(place, tokens, mask, gb, gj0, gj1, vecs, w1, w1, w1, gvec)


def to_blocks(gathered, kinds):
    n, rows, dim = gathered.shape
    m = n // BLOCKS
    parts = gathered.reshape(BLOCKS, m, kinds, rows // kinds, dim)
    return jnp.swapaxes(parts, 1, 2).reshape(BLOCKS, rows * m, dim)


def from_blocks(blocks, kinds, n):
    _, rows, dim = blocks.shape
    m = n // BLOCKS
    parts = blocks.reshape(BLOCKS, kinds, m, rows // (kinds * m), dim)
    return jnp.swapaxes(parts, 1, 2).reshape(n, rows // m, dim)


def split_columns(matrix, dim):
    return [matrix[:, i : i + dim] for i in range(0, matrix.shape[1], dim)]


def swap(bit):
    return [(i, i ^ bit) for i in range(BLOCKS)]


def turn(k):
    return [(i, (i + 4 * k) % BLOCKS) for i in range(BLOCKS)]


REP = [(0, 1), (1, 0)]


def gather_pieces(pack, r):
    lanes = pack.shape[1] // 2
    half = lax.dynamic_slice_in_dim(pack, r * lanes, lanes, 1)
    along_z = jnp.stack([half] + [lax.ppermute(half, "fsdp", turn(k)) for k in (1, 2, 3)])
    by_x = lax.ppermute(along_z, "rep", REP)
    by_y = lax.ppermute(along_z, "fsdp", swap(2))
    by_xy = lax.ppermute(by_x[:2], "fsdp", swap(2))
    by_yx = lax.ppermute(by_y[2:], "rep", REP)
    own = [along_z, by_x, by_y, by_xy, by_yx]
    return own + [lax.ppermute(piece, "fsdp", swap(1)) for piece in own]


def add(a, b):
    return (a.astype(F32) + b.astype(F32)).astype(BF)


def pick(a, i, axis):
    return lax.dynamic_index_in_dim(a, i, axis, keepdims=False)


def half_of(a, i):
    rows = a.shape[-2] // 2
    return lax.dynamic_slice_in_dim(a, i * rows, rows, a.ndim - 2)


def scatter_steps(keep, send, z, y, r):
    got = [lax.ppermute(a, "fsdp", swap(1)) for a in send]
    kept = yield tuple(keep)
    summed = jnp.concatenate([add(*pair) for pair in zip(kept, got)], 1)
    summed = summed.reshape(4, 2, *summed.shape[1:])
    a, b = summed[:2], summed[2:]
    kept = half_of(a, r), pick(b, y, 1)
    sent = yield half_of(a, 1 - r), pick(b, 1 - y, 1), *kept
    got = lax.ppermute(sent[0], "rep", REP), lax.ppermute(sent[1], "fsdp", swap(2))
    kept = yield sent[2:]
    a, b = add(kept[0], got[0]), add(kept[1], got[1])
    sent = yield pick(a, 1 - y, 1), half_of(b, 1 - r), pick(a, y, 1), half_of(b, r)
    got = lax.ppermute(sent[0], "fsdp", swap(2)), lax.ppermute(sent[1], "rep", REP)
    kept = yield sent[2:]
    both = jnp.concatenate([add(kept[0], got[0]), add(kept[1], got[1])])
    sent = yield tuple(pick(both, (z + k) % 4, 0) for k in range(4))
    got = [lax.ppermute(sent[k], "fsdp", turn(k)) for k in (1, 2, 3)]
    kept = yield sent[:1]
    total = kept[0].astype(F32)
    for term in got:
        total += term.astype(F32)
    mine = yield (total.astype(BF),)
    other = lax.ppermute(mine[0], "rep", REP)
    mine = (yield mine)[0]
    yield jnp.where(r == 0, jnp.concatenate([mine, other]), jnp.concatenate([other, mine])).astype(F32)


class Scatter:
    def __init__(self, *args):
        self.steps = scatter_steps(*args)
        self.value = next(self.steps)


def step(scatters, *ties):
    values, ties = lax.optimization_barrier(([s.value for s in scatters], list(ties)))
    for s, value in zip(scatters, values):
        s.value = s.steps.send(value)
    return ties


def by_core(keep, send, c):
    first, second = jnp.where(c == 0, keep, send), jnp.where(c == 0, send, keep)
    return jnp.stack([first, second], 1).reshape(BLOCKS, *keep.shape[1:])


def scatter_whole(send):
    own = lax.psum_scatter(send, "fsdp", scatter_dimension=0)
    other = lax.ppermute(own, "rep", REP)
    return own.astype(F32) + other.astype(F32)


def local(n, tokens, mask_pos, group_id, cotangent, *masters):
    clips, seq, dim = tokens.shape
    width = dim // n
    me, r = lax.axis_index("fsdp"), lax.axis_index("rep")
    z, y, c = me // 4, (me // 2) % 2, me % 2
    place = jnp.stack([z, y, c, r]).astype(jnp.int32)
    if n == BLOCKS:
        pack1, pack2 = pack_call(masters)
        w2 = lax.all_gather(pack2, "fsdp", axis=0)
        pieces = gather_pieces(pack1, r)
    else:
        (w_qkv, b_query, b_value, w_out, b_out, w_up, b_up, w_down, b_down,
         ln1_gain, ln1_bias, ln2_gain, ln2_bias, mask_embed) = (m.astype(BF) for m in masters)
        gather = lambda a: lax.all_gather(a, "fsdp", axis=0)
        vec_all = gather(
            jnp.concatenate(
                [b_query, b_value, b_out, b_down, ln1_gain, ln1_bias, ln2_gain, ln2_bias, mask_embed, b_up]
            )
        )
        flat = jnp.swapaxes(vec_all[:, : B_UP * width].reshape(n, B_UP, width), 0, 1).reshape(B_UP, BLOCKS, dim // BLOCKS)
        table = jnp.zeros((BLOCKS, 16, dim), BF)
        table = table.at[:, :B_UP, : dim // BLOCKS].set(jnp.swapaxes(flat, 0, 1))
        table = table.at[:, B_UP, : 4 * dim // BLOCKS].set(vec_all[:, B_UP * width :].reshape(BLOCKS, 4 * dim // BLOCKS))
        one = to_blocks(gather(jnp.concatenate(split_columns(w_qkv, dim) + [w_out])), 4)
        pieces = [jnp.concatenate([one, table], 1)]
        w2 = jnp.concatenate(
            [to_blocks(gather(w_down), 1), to_blocks(gather(jnp.concatenate(split_columns(w_up, dim))), 4)], 1
        )

    positions = lax.iota(jnp.int32, seq)
    mask = jnp.any(mask_pos[:, :, None] == positions[None, None, :], axis=1).astype(F32)[..., None]
    normed, qkv, att, lse, vecs, w1 = forward_call(group_id, place, tokens, mask, pieces)
    flat = lambda a: a.reshape(clips * seq, a.shape[-1])
    output, gb, g2, down_keep, down_send, gvec = mlp_call(
        group_id, place, flat(tokens), flat(mask), flat(cotangent), flat(att), vecs, w1, w2
    )
    gb3 = gb.reshape(tokens.shape)
    wide = dim // GROUPS
    back = lambda part, gb3: attention_back_call(part, group_id, place, qkv, lse, gb3, w1, flat(normed))
    after = lambda gj0, gj1, gvec: norm_one_call(place, flat(tokens), flat(mask), gb, flat(gj0), flat(gj1), vecs, w1, gvec)
    if n == BLOCKS:
        down = Scatter([down_keep], [down_send], z, y, r)
        step([down])
        (gb3,) = step([down], gb3)
        gj0, keep0, send0 = back(0, gb3)
        keep0, send0 = step([down], keep0, send0)
        (gb3,) = step([down], gb3)
        gj1, keep1, send1 = back(1, gb3)
        keep0, keep1, send0, send1 = step([down], keep0, keep1, send0, send1)
        rest = Scatter([keep0, keep1], [send0, send1], z, y, r)
        step([rest])
        (gvec,) = step([rest], gvec)
        token_grad, keep2, send2 = after(gj0, gj1, gvec)
        keep2, send2 = step([rest], keep2, send2)
        keep2, send2 = step([down, rest], keep2, send2)
        few = add(keep2, lax.ppermute(send2, "fsdp", swap(1))).reshape(4, 2, *keep2.shape[1:])
        few = add(pick(few, y, 1), lax.ppermute(pick(few, 1 - y, 1), "fsdp", swap(2)))
        few = step([down, rest], *(pick(few, (z + k) % 4, 0) for k in range(4)))
        own2 = lax.psum_scatter(g2, "fsdp", scatter_dimension=0)
        *few, own2 = step([down, rest], *few, own2)
        other2 = lax.ppermute(own2, "rep", REP)
        got = [lax.ppermute(few[k], "fsdp", turn(k)) for k in (1, 2, 3)]
        few, own2 = step([down, rest], few[0], own2)
        total = few.astype(F32)
        for term in got:
            total += term.astype(F32)
        (few,) = step([rest], total.astype(BF))
        sum2 = own2.astype(F32) + other2.astype(F32)
        few = few.astype(F32) + lax.ppermute(few, "rep", REP).astype(F32)
        sum1 = rest.steps.send(rest.value)
        down_grad = down.value
        up_grad, out_grad = sum2[: 4 * width], sum2[4 * width :]
        qkv_grad = jnp.concatenate([sum1[i * width : (i + 1) * width] for i in (0, 3, 1, 4, 2, 5)], 1)
        vg = [few[k, :width] for k in range(B_UP)] + [few[B_UP, : 4 * width]]
    else:
        (gj0, *parts0), (gj1, *parts1) = (back(part, gb3) for part in range(GROUPS))
        token_grad, *table = after(gj0, gj1, gvec)
        down_grad = scatter_whole(from_blocks(by_core(down_keep, down_send, place[2]), 1, n))
        rest = scatter_whole(from_blocks(g2, 5, n))
        up_grad, out_grad = rest[: 4 * width], rest[4 * width :]
        sums = [scatter_whole(from_blocks(by_core(*parts, place[2]), 3, n)) for parts in (parts0, parts1)]
        qkv_grad = jnp.concatenate([a[i * width : (i + 1) * width] for i in range(3) for a in sums], 1)
        table = by_core(*table, place[2])
        few = jnp.swapaxes(table[:, :B_UP, : dim // BLOCKS], 0, 1).reshape(B_UP, n, width)
        few = jnp.swapaxes(few, 0, 1).reshape(n, B_UP * width)
        line = scatter_whole(jnp.concatenate([few, table[:, B_UP, : 4 * dim // BLOCKS].reshape(n, 4 * width)], 1))
        vg = [line[i * width : (i + 1) * width] for i in range(B_UP)] + [line[B_UP * width :]]
    up_grad = jnp.concatenate([up_grad[i * width : (i + 1) * width] for i in range(4)], 1)
    return (
        output.reshape(tokens.shape),
        token_grad.reshape(tokens.shape),
        qkv_grad,
        vg[B_QUERY],
        vg[B_VALUE],
        out_grad,
        vg[B_OUT],
        up_grad,
        vg[B_UP],
        down_grad,
        vg[B_DOWN],
        vg[GAIN1],
        vg[BIAS1],
        vg[GAIN2],
        vg[BIAS2],
        vg[EMBED],
    )


def solution(mesh):
    clip3, clip2, clip1 = P(("rep", "fsdp"), None, None), P(("rep", "fsdp"), None), P(("rep", "fsdp"))
    mat, line = P("fsdp", None), P("fsdp")
    params = (mat, line, line, mat, line, mat, line, mat, line, line, line, line, line, line)
    return jax.shard_map(
        functools.partial(local, mesh.shape["fsdp"]),
        mesh=mesh,
        in_specs=(clip3, clip2, clip1, clip3) + params,
        out_specs=(clip3, clip3) + params,
        check_vma=False,
    )
```

```python
import functools

import jax
import jax.numpy as jnp
from jax import lax
from jax.experimental import pallas as pl
from jax.experimental.pallas import tpu as pltpu
from jax.sharding import PartitionSpec as P

HEADS = 12
BLOCKS = 16
EPS = 1e-06
BF = jnp.bfloat16
F32 = jnp.float32
VMEM_LIMIT = 56 * 1024 * 1024

B_QUERY, B_VALUE, B_OUT, B_DOWN, GAIN1, BIAS1, GAIN2, BIAS2, EMBED, B_UP = range(10)
VECS = 13


def dot(a, b):
    return jnp.dot(a, b, preferred_element_type=F32)


def dot_nt(a, b):
    return lax.dot_general(a, b, (((1,), (1,)), ((), ())), preferred_element_type=F32)


def dot_tn(a, b):
    return lax.dot_general(a, b, (((0,), (0,)), ((), ())), preferred_element_type=F32)


def normalise(values):
    centre = values - jnp.mean(values, -1, keepdims=True)
    spread = jnp.mean(centre * centre, -1, keepdims=True)
    r = lax.rsqrt(spread + EPS)
    return centre * r, r


def norm_back(x_hat, r, q, gain):
    qg = q * gain
    m1 = jnp.mean(qg, -1, keepdims=True)
    m2 = jnp.mean(qg * x_hat, -1, keepdims=True)
    return r * (qg - m1 - x_hat * m2)


def colsum(values):
    return jnp.sum(values, 0, keepdims=True)


def gelu_both(u):
    x = jnp.abs(u)
    t = pl.reciprocal(1.0 + x * (0.3275911 * 0.7071067811865476), approx=False)
    e = jnp.exp2(u * u * (-0.5 * 1.4426950408889634))
    poly = 0.5 * 1.061405429
    for c in (-1.453152027, 1.421413741, -0.284496736, 0.254829592):
        poly = poly * t + 0.5 * c
    tail = poly * t * e
    cdf = jnp.where(u < 0, tail, 1.0 - tail)
    return u * cdf, cdf + u * (e * 0.3989422804014327)


def pack_kernel(
    w_qkv, w_out, w_up, w_down, b_query, b_value, b_out, b_down, g1, b1, g2, b2, embed, b_up, one_ref, two_ref, table
):
    width, dim = w_out.shape
    for i in range(3):
        one_ref[i * width : (i + 1) * width] = w_qkv[:, i * dim : (i + 1) * dim].astype(BF)
    one_ref[3 * width : 4 * width] = w_out[...].astype(BF)
    table[...] = jnp.zeros_like(table)
    for k, ref in enumerate((b_query, b_value, b_out, b_down, g1, b1, g2, b2, embed, b_up)):
        table[k : k + 1, 0 : ref.shape[1]] = ref[...]
    one_ref[4 * width :] = table[...].astype(BF)
    two_ref[0 : 4 * width] = w_down[...].astype(BF)
    for i in range(4):
        two_ref[(4 + i) * width : (5 + i) * width] = w_up[:, i * dim : (i + 1) * dim].astype(BF)


def pack_call(masters):
    (w_qkv, b_query, b_value, w_out, b_out, w_up, b_up, w_down, b_down,
     ln1_gain, ln1_bias, ln2_gain, ln2_bias, mask_embed) = masters
    width, dim = w_out.shape
    vectors = (b_query, b_value, b_out, b_down, ln1_gain, ln1_bias, ln2_gain, ln2_bias, mask_embed, b_up)
    return pl.pallas_call(
        pack_kernel,
        out_shape=[
            jax.ShapeDtypeStruct((4 * width + 16, dim), BF),
            jax.ShapeDtypeStruct((8 * width, dim), BF),
        ],
        scratch_shapes=[pltpu.VMEM((16, dim), F32)],
        name="pack",
    )(w_qkv, w_out, w_up, w_down, *(v.reshape(1, -1) for v in vectors))


def load_pieces(place, pieces, dest, sems):
    z, y, c, r = (place[i] for i in range(4))
    half = dest.shape[2] // 2
    kinds = ((0, 0, 0), (1, 0, 0), (0, 1, 0), (1, 1, 0), (1, 1, 2))
    copies = []
    for p, ref in enumerate(pieces):
        dx, dy, first = kinds[p % 5]
        dc = p // 5
        for k in range(ref.shape[0]):
            at = ((z + 4 - k - first) % 4) * 4 + (y ^ dy) * 2 + (c ^ dc)
            lanes = pl.ds(pl.multiple_of((r ^ dx) * half, 128), half)
            copies.append(pltpu.make_async_copy(ref.at[k], dest.at[at, :, lanes], sems.at[len(copies)]))
    for copy in copies:
        copy.start()
    for copy in copies:
        copy.wait()


def forward_kernel(count, group_ref, place_ref, tok_ref, mask_ref, *refs):
    pieces = refs[:count]
    normed_ref, qkv_ref, att_ref, lse_ref, vec_ref, w1_ref, sems = refs[count:]
    clip = pl.program_id(0)
    seq, dim = tok_ref.shape[1], tok_ref.shape[2]

    @pl.when(clip == 0)
    def _():
        if count == 1:
            copy = pltpu.make_async_copy(pieces[0], w1_ref, sems.at[0])
            copy.start()
            copy.wait()
        else:
            load_pieces(place_ref, pieces, w1_ref, sems)
        table = [w1_ref[i, 192:208, :].astype(F32) for i in range(BLOCKS)]
        vec_ref[0:B_UP] = jnp.concatenate([t[0:B_UP, 0:48] for t in table], 1)
        for j in range(4):
            vec_ref[B_UP + j : B_UP + j + 1] = jnp.concatenate(
                [t[B_UP : B_UP + 1, 0:192] for t in table[4 * j : 4 * j + 4]], 1
            )
        vec_ref[VECS:] = jnp.zeros((16 - VECS, dim), F32)

    vec = lambda k: vec_ref[k : k + 1, :]
    weight = lambda k: w1_ref[:, 48 * k : 48 * (k + 1), :].reshape(dim, dim)
    step = seq // 2
    for r in range(0, seq, step):
        rows = slice(r, r + step)
        blended = jnp.where(mask_ref[0, rows] > 0, vec(EMBED), tok_ref[0, rows].astype(F32))
        x_hat, _ = normalise(blended)
        normed = (x_hat * vec(GAIN1) + vec(BIAS1)).astype(BF)
        normed_ref[0, rows] = normed
        qkv_ref[0, rows, 0:dim] = (dot(normed, weight(0)) + vec(B_QUERY)).astype(BF)
        qkv_ref[0, rows, dim : 2 * dim] = dot(normed, weight(1)).astype(BF)
        qkv_ref[0, rows, 2 * dim :] = (dot(normed, weight(2)) + vec(B_VALUE)).astype(BF)
    head = dim // HEADS
    scale = head**-0.5 * 1.4426950408889634

    def attend(length):
        if length < seq:
            att_ref[0, length:, :] = jnp.zeros((seq - length, dim), BF)
            lse_ref[0, :, :] = jnp.zeros((HEADS, seq), F32)
        chunk = min(length, 512)
        lane = lax.broadcasted_iota(jnp.int32, (chunk, 2 * head), 1)

        @pl.loop(0, HEADS // 2, unroll=2)
        def _(pair):
            lanes = lambda i: pl.ds(pl.multiple_of(i * dim + pair * 2 * head, 128), 2 * head)
            k = qkv_ref[0, 0:length, lanes(1)]
            vt = qkv_ref[0, 0:length, lanes(2)].T
            for c in range(0, length, chunk):
                q = qkv_ref[0, c : c + chunk, lanes(0)]
                zero = jnp.zeros_like(q)
                both = jnp.concatenate([jnp.where(lane < head, q, zero), jnp.where(lane < head, zero, q)], 0)
                st = dot_nt(k, both)
                top = jnp.max(st, 0, keepdims=True) * scale
                e = jnp.exp2(st * scale - top)
                total = jnp.sum(e, 0, keepdims=True)
                p = (e * (1.0 / total)).astype(BF)
                o0 = dot(vt[0:head], p[:, 0:chunk])
                o1 = dot(vt[head:], p[:, chunk:])
                lse = top + jnp.log2(total)
                lse_ref[0, pl.ds(2 * pair, 1), c : c + chunk] = lse[:, 0:chunk]
                lse_ref[0, pl.ds(2 * pair + 1, 1), c : c + chunk] = lse[:, chunk:]
                att_ref[0, c : c + chunk, lanes(0)] = jnp.concatenate([o0, o1], 0).T.astype(BF)

    full = group_ref[clip] == 0
    pl.when(full)(lambda: attend(seq))
    pl.when(jnp.logical_not(full))(lambda: attend(seq // 2))


def weight_spec(index):
    return pl.BlockSpec((BLOCKS, 48, 768), lambda *g: (0, index, 0))


def forward_call(group_id, place, tokens, mask, pieces):
    clips, seq, dim = tokens.shape
    row = lambda *tail: pl.BlockSpec((1, *tail), lambda c, *_: (c,) + (0,) * len(tail))
    return pl.pallas_call(
        functools.partial(forward_kernel, len(pieces)),
        grid_spec=pltpu.PrefetchScalarGridSpec(
            num_scalar_prefetch=2,
            grid=(clips,),
            in_specs=[row(seq, dim), row(seq, 1)] + [pl.BlockSpec(memory_space=pl.ANY)] * len(pieces),
            out_specs=[row(seq, dim), row(seq, 3 * dim), row(seq, dim), row(HEADS, seq), whole(16, dim), whole(BLOCKS, 208, dim)],
            scratch_shapes=[pltpu.SemaphoreType.DMA((32,))],
        ),
        out_shape=[
            jax.ShapeDtypeStruct((clips, seq, dim), BF),
            jax.ShapeDtypeStruct((clips, seq, 3 * dim), BF),
            jax.ShapeDtypeStruct((clips, seq, dim), BF),
            jax.ShapeDtypeStruct((clips, HEADS, seq), F32),
            jax.ShapeDtypeStruct((16, dim), F32),
            jax.ShapeDtypeStruct((BLOCKS, 208, dim), BF),
        ],
        compiler_params=pltpu.CompilerParams(vmem_limit_bytes=VMEM_LIMIT),
        cost_estimate=pl.CostEstimate(flops=9 * 10**9, bytes_accessed=16 * 2**20, transcendentals=0),
        name="attention_forward",
    )(group_id, place, tokens, mask, *pieces)


def store_by_core(core, value, keep_ref, send_ref, rows):
    for own in range(2):

        @pl.when(core == own)
        def _():
            keep_ref[:, rows] = value[:, own]
            send_ref[:, rows] = value[:, 1 - own]


def mlp_kernel(
    group_ref, place_ref, tok_ref, mask_ref, cot_ref, att_ref, vec_ref, wo_ref, wu_ref, wd_ref,
    out_ref, gb_ref, gw_ref, keep_ref, send_ref, gvec_ref,
    hidden, n2, gr, act, gpre, acc, gn2,
):
    j = pl.program_id(0)
    last = pl.num_programs(0) - 1
    rows_all, dim = tok_ref.shape
    seq = rows_all // group_ref.shape[0]
    vec = lambda k: vec_ref[k : k + 1, :]
    step = 256
    keeps = [group_ref[r // seq] == 0 if (r % seq) >= seq // 2 else None for r in range(0, rows_all, step)]
    weight = [1.0 if keep is None else jnp.where(keep, 1.0, 0.0) for keep in keeps]

    @pl.when(j == 0)
    def _():
        gvec_ref[...] = jnp.zeros_like(gvec_ref)
        w_out = wo_ref[...].reshape(dim, dim)
        for i, r in enumerate(range(0, rows_all, step)):
            rows = slice(r, r + step)
            blended = jnp.where(mask_ref[rows] > 0, vec(EMBED), tok_ref[rows].astype(F32))
            h = blended + dot(att_ref[rows], w_out) + vec(B_OUT)
            hidden[rows] = h
            x_hat, _ = normalise(h)
            n2[rows] = (x_hat * vec(GAIN2) + vec(BIAS2)).astype(BF)
            g = cot_ref[rows].astype(F32) * weight[i]
            gr[rows] = g.astype(BF)
            gvec_ref[B_DOWN : B_DOWN + 1] += colsum(g)
            acc[rows] = h + vec(B_DOWN)
            gn2[rows] = jnp.zeros((step, dim), F32)

    @pl.when(j < last)
    def _():
        w_up = wu_ref[...].reshape(dim, dim)
        w_down = wd_ref[...].reshape(dim, dim)
        b_up = vec_ref[pl.ds(B_UP + j, 1), :]
        bsum = jnp.zeros((1, dim), F32)
        big = 512
        for r in range(0, rows_all, big):
            rows = slice(r, r + big)
            pre = dot(n2[rows], w_up) + b_up
            ga = dot_nt(gr[rows], w_down)
            value, slope = gelu_both(pre)
            value = value.astype(BF)
            act[rows] = value
            grad = (slope * ga).astype(BF)
            gpre[rows] = grad
            bsum += colsum(grad.astype(F32))
            acc[rows] += dot(value, w_down)
            gn2[rows] += dot_nt(grad, w_up)
        gvec_ref[pl.ds(B_UP + j, 1), :] = bsum
        gw_ref[...] = dot_tn(n2[...], gpre[...]).astype(BF).reshape(gw_ref.shape)
        down = dot_tn(act[...], gr[...]).astype(BF).reshape(2, 2, 192, dim)
        store_by_core(place_ref[2], down, keep_ref, send_ref, slice(0, 192))

    @pl.when(j == last)
    def _():
        for i, r in enumerate(range(0, rows_all, step)):
            rows = slice(r, r + step)
            out_ref[rows] = (acc[rows] * weight[i]).astype(BF)
            x_hat, scale = normalise(hidden[rows])
            q = gn2[rows]
            gvec_ref[GAIN2 : GAIN2 + 1] += colsum(q * x_hat)
            gvec_ref[BIAS2 : BIAS2 + 1] += colsum(q)
            gh = cot_ref[rows].astype(F32) * weight[i] + norm_back(x_hat, scale, q, vec(GAIN2))
            gb = gh.astype(BF)
            gb_ref[rows] = gb
            gvec_ref[B_OUT : B_OUT + 1] += colsum(gb.astype(F32))
        gw_ref[...] = dot_tn(att_ref[...], gb_ref[...]).astype(BF).reshape(gw_ref.shape)


def whole(*shape):
    return pl.BlockSpec(shape, lambda *g: (0,) * len(shape))


def mlp_call(group_id, place, tokens, mask, cotangent, att, vecs, w1, w2):
    rows, dim = tokens.shape
    out = lambda shape, kind: jax.ShapeDtypeStruct(shape, kind)
    return pl.pallas_call(
        mlp_kernel,
        grid_spec=pltpu.PrefetchScalarGridSpec(
            num_scalar_prefetch=2,
            grid=(5,),
            in_specs=[
                whole(rows, dim),
                whole(rows, 1),
                whole(rows, dim),
                whole(rows, dim),
                whole(*vecs.shape),
                weight_spec(3),
                pl.BlockSpec((BLOCKS, 48, dim), lambda j, *_: (0, 4 + jnp.minimum(j, 3), 0)),
                pl.BlockSpec((4, 192, dim), lambda j, *_: (jnp.minimum(j, 3), 0, 0)),
            ],
            out_specs=[
                whole(rows, dim),
                whole(rows, dim),
                pl.BlockSpec((BLOCKS, 48, dim), lambda j, *_: (0, j, 0)),
                pl.BlockSpec((2, 192, dim), lambda j, *_: (jnp.minimum(j, 3), 0, 0)),
                pl.BlockSpec((2, 192, dim), lambda j, *_: (jnp.minimum(j, 3), 0, 0)),
                whole(16, dim),
            ],
            scratch_shapes=[
                pltpu.VMEM((rows, dim), F32),
                pltpu.VMEM((rows, dim), BF),
                pltpu.VMEM((rows, dim), BF),
                pltpu.VMEM((rows, dim), BF),
                pltpu.VMEM((rows, dim), BF),
                pltpu.VMEM((rows, dim), F32),
                pltpu.VMEM((rows, dim), F32),
            ],
        ),
        out_shape=[
            out((rows, dim), BF),
            out((rows, dim), BF),
            out((BLOCKS, 240, dim), BF),
            out((BLOCKS // 2, 192, dim), BF),
            out((BLOCKS // 2, 192, dim), BF),
            out((16, dim), F32),
        ],
        compiler_params=pltpu.CompilerParams(vmem_limit_bytes=VMEM_LIMIT),
        cost_estimate=pl.CostEstimate(flops=45 * 10**9, bytes_accessed=30 * 2**20, transcendentals=0),
        name="mlp",
    )(group_id, place, tokens, mask, cotangent, att, vecs, w1, w2, w2)


GROUPS = 2


def attention_back_kernel(
    part, group_ref, place_ref, q_ref, k_ref, v_ref, lse_ref, gb_ref, wo_ref, normed_ref, gj, keep_ref, send_ref, gatt, all_gj
):
    clip = pl.program_id(0)
    seq, dim = gb_ref.shape[1], gb_ref.shape[2]
    wide = dim // GROUPS
    head = dim // HEADS
    scale = head**-0.5
    gatt[...] = dot_nt(gb_ref[0], wo_ref[...].reshape(wide, dim)).astype(BF)

    def back(length):
        if length < seq:
            gj[0, length:, :] = jnp.zeros((seq - length, 3 * wide), BF)
        lane = lax.broadcasted_iota(jnp.int32, (length, 2 * head), 1)

        @pl.loop(0, HEADS // 2 // GROUPS, unroll=3)
        def _(pair):
            lanes = lambda i: pl.ds(pl.multiple_of(i * wide + pair * 2 * head, 128), 2 * head)
            k = k_ref[0, 0:length, lanes(0)]
            v = v_ref[0, 0:length, lanes(0)]
            kt = k.T
            zero = jnp.zeros((length, 2 * head), BF)
            split = lambda a: jnp.concatenate([jnp.where(lane < head, a, zero), jnp.where(lane < head, zero, a)], 0)
            q = split(q_ref[0, 0:length, lanes(0)])
            ga = split(gatt[0:length, lanes(0)])
            first = part * (HEADS // GROUPS) + 2 * pair
            lse = jnp.concatenate([lse_ref[0, pl.ds(first + h, 1), 0:length] for h in range(2)], 1)
            p = jnp.exp2(dot_nt(k, q) * (scale * 1.4426950408889634) - lse)
            gp = dot_nt(v, ga)
            inner = jnp.sum(p * gp, 0, keepdims=True)
            ds = (p * (gp - inner)).astype(BF)
            dq = [dot(kt[h * head : (h + 1) * head], ds[:, h * length : (h + 1) * length]) for h in range(2)]
            gj[0, 0:length, lanes(0)] = (jnp.concatenate(dq, 0).T * scale).astype(BF)
            gj[0, 0:length, lanes(1)] = (dot(ds, q) * scale).astype(BF)
            gj[0, 0:length, lanes(2)] = dot(p.astype(BF), ga).astype(BF)

    full = group_ref[clip] == 0
    pl.when(full)(lambda: back(seq))
    pl.when(jnp.logical_not(full))(lambda: back(seq // 2))
    all_gj[pl.ds(clip * seq, seq)] = gj[0]

    @pl.when(clip == pl.num_programs(0) - 1)
    def _():
        grad = dot_tn(normed_ref[...], all_gj[...])
        for i in range(3):
            value = grad[:, i * wide : (i + 1) * wide].astype(BF).reshape(BLOCKS // 2, 2, 48, wide)
            store_by_core(place_ref[2], value, keep_ref, send_ref, slice(48 * i, 48 * (i + 1)))


def attention_back_call(part, group_id, place, qkv, lse, gb, w1, normed):
    clips, seq, dim = gb.shape
    wide = dim // GROUPS
    columns = lambda i: pl.BlockSpec((1, seq, wide), lambda c, *_: (c, 0, GROUPS * i + part))
    row = lambda *tail: pl.BlockSpec((1, *tail), lambda c, *_: (c,) + (0,) * len(tail))
    return pl.pallas_call(
        functools.partial(attention_back_kernel, part),
        grid_spec=pltpu.PrefetchScalarGridSpec(
            num_scalar_prefetch=2,
            grid=(clips,),
            in_specs=[
                columns(0),
                columns(1),
                columns(2),
                row(HEADS, seq),
                row(seq, dim),
                pl.BlockSpec((BLOCKS // GROUPS, 48, dim), lambda *g: (part, 3, 0)),
                whole(clips * seq, dim),
            ],
            out_specs=[row(seq, 3 * wide), whole(BLOCKS // 2, 144, wide), whole(BLOCKS // 2, 144, wide)],
            scratch_shapes=[pltpu.VMEM((seq, wide), BF), pltpu.VMEM((clips * seq, 3 * wide), BF)],
        ),
        out_shape=[
            jax.ShapeDtypeStruct((clips, seq, 3 * wide), BF),
            jax.ShapeDtypeStruct((BLOCKS // 2, 144, wide), BF),
            jax.ShapeDtypeStruct((BLOCKS // 2, 144, wide), BF),
        ],
        compiler_params=pltpu.CompilerParams(vmem_limit_bytes=32 * 2**20),
        cost_estimate=pl.CostEstimate(flops=10**8, bytes_accessed=2**20, transcendentals=0),
        name="attention_backward",
    )(group_id, place, qkv, qkv, qkv, lse, gb, w1, normed)


def norm_one_kernel(
    place_ref, tok_ref, mask_ref, gb_ref, gj0_ref, gj1_ref, vec_ref, wq_ref, wk_ref, wv_ref, gmlp_ref,
    tg_ref, keep_ref, send_ref, gvec_ref,
):
    step = pl.program_id(0)
    dim = tok_ref.shape[1]
    wide = dim // GROUPS
    vec = lambda k: vec_ref[k : k + 1, :]

    @pl.when(step == 0)
    def _():
        gvec_ref[...] = gmlp_ref[...]

    gq, gk, gv = (
        jnp.concatenate([ref[:, i * wide : (i + 1) * wide] for ref in (gj0_ref, gj1_ref)], 1) for i in range(3)
    )
    gvec_ref[B_QUERY : B_QUERY + 1] += colsum(gq.astype(F32))
    gvec_ref[B_VALUE : B_VALUE + 1] += colsum(gv.astype(F32))
    g = dot_nt(gq, wq_ref[...].reshape(dim, dim))
    g += dot_nt(gk, wk_ref[...].reshape(dim, dim))
    g += dot_nt(gv, wv_ref[...].reshape(dim, dim))
    masked = mask_ref[...] > 0
    x_hat, r_std = normalise(jnp.where(masked, vec(EMBED), tok_ref[...].astype(F32)))
    gvec_ref[GAIN1 : GAIN1 + 1] += colsum(g * x_hat)
    gvec_ref[BIAS1 : BIAS1 + 1] += colsum(g)
    total = gb_ref[...].astype(F32) + norm_back(x_hat, r_std, g, vec(GAIN1))
    tg_ref[...] = jnp.where(masked, 0.0, total).astype(BF)
    gvec_ref[EMBED : EMBED + 1] += colsum(jnp.where(masked, total, 0.0))

    @pl.when(step == pl.num_programs(0) - 1)
    def _():
        table = gvec_ref[...]
        for i in range(BLOCKS):
            few = table[0:B_UP, 48 * i : 48 * (i + 1)]
            few = jnp.concatenate([few, jnp.zeros((B_UP, wide - 48), F32)], 1)
            at = 192 * (i % 4)
            up = table[B_UP + i // 4 : B_UP + i // 4 + 1, at : at + 192]
            up = jnp.concatenate([up, jnp.zeros((1, wide - 192), F32)], 1)
            few = jnp.concatenate([few, up, jnp.zeros((16 - B_UP - 1, wide), F32)], 0).astype(BF)
            for ref, same in ((keep_ref, True), (send_ref, False)):

                @pl.when((place_ref[2] == i % 2) == same)
                def _():
                    ref[i // 2] = few


def norm_one_call(place, tokens, mask, gb, gj0, gj1, vecs, w1, gvec):
    rows, dim = tokens.shape
    step = rows // 4
    part = lambda width: pl.BlockSpec((step, width), lambda i, *_: (i, 0))
    small = (BLOCKS // 2, 16, dim // GROUPS)
    return pl.pallas_call(
        norm_one_kernel,
        grid_spec=pltpu.PrefetchScalarGridSpec(
            num_scalar_prefetch=1,
            grid=(4,),
            in_specs=[
                part(dim),
                part(1),
                part(dim),
                part(3 * dim // GROUPS),
                part(3 * dim // GROUPS),
                whole(*vecs.shape),
                weight_spec(0),
                weight_spec(1),
                weight_spec(2),
                whole(16, dim),
            ],
            out_specs=[part(dim), whole(*small), whole(*small)],
            scratch_shapes=[pltpu.VMEM((16, dim), F32)],
        ),
        out_shape=[
            jax.ShapeDtypeStruct((rows, dim), BF),
            jax.ShapeDtypeStruct(small, BF),
            jax.ShapeDtypeStruct(small, BF),
        ],
        compiler_params=pltpu.CompilerParams(vmem_limit_bytes=28 * 2**20),
        cost_estimate=pl.CostEstimate(flops=10**8, bytes_accessed=2**20, transcendentals=0),
        name="norm_one_backward",
    )(place, tokens, mask, gb, gj0, gj1, vecs, w1, w1, w1, gvec)


def to_blocks(gathered, kinds):
    n, rows, dim = gathered.shape
    m = n // BLOCKS
    parts = gathered.reshape(BLOCKS, m, kinds, rows // kinds, dim)
    return jnp.swapaxes(parts, 1, 2).reshape(BLOCKS, rows * m, dim)


def from_blocks(blocks, kinds, n):
    _, rows, dim = blocks.shape
    m = n // BLOCKS
    parts = blocks.reshape(BLOCKS, kinds, m, rows // (kinds * m), dim)
    return jnp.swapaxes(parts, 1, 2).reshape(n, rows // m, dim)


def split_columns(matrix, dim):
    return [matrix[:, i : i + dim] for i in range(0, matrix.shape[1], dim)]


def swap(bit):
    return [(i, i ^ bit) for i in range(BLOCKS)]


def turn(k):
    return [(i, (i + 4 * k) % BLOCKS) for i in range(BLOCKS)]


REP = [(0, 1), (1, 0)]


def gather_pieces(pack, r):
    lanes = pack.shape[1] // 2
    half = lax.dynamic_slice_in_dim(pack, r * lanes, lanes, 1)
    along_z = jnp.stack([half] + [lax.ppermute(half, "fsdp", turn(k)) for k in (1, 2, 3)])
    by_x = lax.ppermute(along_z, "rep", REP)
    by_y = lax.ppermute(along_z, "fsdp", swap(2))
    by_xy = lax.ppermute(by_x[:2], "fsdp", swap(2))
    by_yx = lax.ppermute(by_y[2:], "rep", REP)
    own = [along_z, by_x, by_y, by_xy, by_yx]
    return own + [lax.ppermute(piece, "fsdp", swap(1)) for piece in own]


def add(a, b):
    return (a.astype(F32) + b.astype(F32)).astype(BF)


def pick(a, i, axis):
    return lax.dynamic_index_in_dim(a, i, axis, keepdims=False)


def half_of(a, i):
    rows = a.shape[-2] // 2
    return lax.dynamic_slice_in_dim(a, i * rows, rows, a.ndim - 2)


def scatter_steps(keep, send, z, y, r, extra=()):
    got = [lax.ppermute(a, "fsdp", swap(1)) for a in send]
    kept = yield tuple(keep)
    summed = jnp.concatenate([add(*pair) for pair in zip(kept, got)], 1)
    summed = summed.reshape(4, 2, *summed.shape[1:])
    a, b = summed[:2], summed[2:]
    kept = half_of(a, r), pick(b, y, 1)
    sent = yield half_of(a, 1 - r), pick(b, 1 - y, 1), *kept
    got = lax.ppermute(sent[0], "rep", REP), lax.ppermute(sent[1], "fsdp", swap(2))
    kept = yield sent[2:]
    a, b = add(kept[0], got[0]), add(kept[1], got[1])
    sent = yield pick(a, 1 - y, 1), half_of(b, 1 - r), pick(a, y, 1), half_of(b, r)
    got = lax.ppermute(sent[0], "fsdp", swap(2)), lax.ppermute(sent[1], "rep", REP)
    kept = yield sent[2:]
    both = jnp.concatenate([add(kept[0], got[0]), add(kept[1], got[1])])
    half = both.shape[1]
    both = jnp.concatenate([both, *extra], 1)
    sent = yield tuple(pick(both, (z + k) % 4, 0) for k in range(4))
    got = [lax.ppermute(sent[k], "fsdp", turn(k)) for k in (1, 2, 3)]
    kept = yield sent[:1]
    total = kept[0].astype(F32)
    for term in got:
        total += term.astype(F32)
    mine = yield (total.astype(BF),)
    other = lax.ppermute(mine[0], "rep", REP)
    mine = (yield mine)[0]
    few = mine[half:].astype(F32) + other[half:].astype(F32)
    mine, other = mine[:half], other[:half]
    yield jnp.where(r == 0, jnp.concatenate([mine, other]), jnp.concatenate([other, mine])).astype(F32), few


class Scatter:
    def __init__(self, *args):
        self.steps = scatter_steps(*args)
        self.value = next(self.steps)


def step(scatters, *ties):
    values, ties = lax.optimization_barrier(([s.value for s in scatters], list(ties)))
    for s, value in zip(scatters, values):
        s.value = s.steps.send(value)
    return ties


def by_core(keep, send, c):
    first, second = jnp.where(c == 0, keep, send), jnp.where(c == 0, send, keep)
    return jnp.stack([first, second], 1).reshape(BLOCKS, *keep.shape[1:])


def scatter_whole(send):
    own = lax.psum_scatter(send, "fsdp", scatter_dimension=0)
    other = lax.ppermute(own, "rep", REP)
    return own.astype(F32) + other.astype(F32)


def local(n, tokens, mask_pos, group_id, cotangent, *masters):
    clips, seq, dim = tokens.shape
    width = dim // n
    me, r = lax.axis_index("fsdp"), lax.axis_index("rep")
    z, y, c = me // 4, (me // 2) % 2, me % 2
    place = jnp.stack([z, y, c, r]).astype(jnp.int32)
    if n == BLOCKS:
        pack1, pack2 = pack_call(masters)
        w2 = lax.all_gather(pack2, "fsdp", axis=0)
        pieces = gather_pieces(pack1, r)
    else:
        (w_qkv, b_query, b_value, w_out, b_out, w_up, b_up, w_down, b_down,
         ln1_gain, ln1_bias, ln2_gain, ln2_bias, mask_embed) = (m.astype(BF) for m in masters)
        gather = lambda a: lax.all_gather(a, "fsdp", axis=0)
        vec_all = gather(
            jnp.concatenate(
                [b_query, b_value, b_out, b_down, ln1_gain, ln1_bias, ln2_gain, ln2_bias, mask_embed, b_up]
            )
        )
        flat = jnp.swapaxes(vec_all[:, : B_UP * width].reshape(n, B_UP, width), 0, 1).reshape(B_UP, BLOCKS, dim // BLOCKS)
        table = jnp.zeros((BLOCKS, 16, dim), BF)
        table = table.at[:, :B_UP, : dim // BLOCKS].set(jnp.swapaxes(flat, 0, 1))
        table = table.at[:, B_UP, : 4 * dim // BLOCKS].set(vec_all[:, B_UP * width :].reshape(BLOCKS, 4 * dim // BLOCKS))
        one = to_blocks(gather(jnp.concatenate(split_columns(w_qkv, dim) + [w_out])), 4)
        pieces = [jnp.concatenate([one, table], 1)]
        w2 = jnp.concatenate(
            [to_blocks(gather(w_down), 1), to_blocks(gather(jnp.concatenate(split_columns(w_up, dim))), 4)], 1
        )

    positions = lax.iota(jnp.int32, seq)
    mask = jnp.any(mask_pos[:, :, None] == positions[None, None, :], axis=1).astype(F32)[..., None]
    normed, qkv, att, lse, vecs, w1 = forward_call(group_id, place, tokens, mask, pieces)
    flat = lambda a: a.reshape(clips * seq, a.shape[-1])
    output, gb, g2, down_keep, down_send, gvec = mlp_call(
        group_id, place, flat(tokens), flat(mask), flat(cotangent), flat(att), vecs, w1, w2
    )
    gb3 = gb.reshape(tokens.shape)
    wide = dim // GROUPS
    back = lambda part, gb3: attention_back_call(part, group_id, place, qkv, lse, gb3, w1, flat(normed))
    after = lambda gj0, gj1, gvec: norm_one_call(place, flat(tokens), flat(mask), gb, flat(gj0), flat(gj1), vecs, w1, gvec)
    if n == BLOCKS:
        down = Scatter([down_keep], [down_send], z, y, r)
        step([down])
        (gb3,) = step([down], gb3)
        gj0, keep0, send0 = back(0, gb3)
        keep0, send0 = step([down], keep0, send0)
        (gb3,) = step([down], gb3)
        gj1, keep1, send1 = back(1, gb3)
        keep0, keep1, send0, send1 = step([down], keep0, keep1, send0, send1)
        extra = []
        rest = Scatter([keep0, keep1], [send0, send1], z, y, r, extra)
        step([rest])
        (gvec,) = step([rest], gvec)
        token_grad, keep2, send2 = after(gj0, gj1, gvec)
        keep2, send2 = step([rest], keep2, send2)
        keep2, send2 = step([down, rest], keep2, send2)
        few = add(keep2, lax.ppermute(send2, "fsdp", swap(1))).reshape(4, 2, *keep2.shape[1:])
        few = add(pick(few, y, 1), lax.ppermute(pick(few, 1 - y, 1), "fsdp", swap(2)))
        extra.append(few)
        step([down, rest])
        own2 = lax.psum_scatter(g2, "fsdp", scatter_dimension=0)
        (own2,) = step([down, rest], own2)
        other2 = lax.ppermute(own2, "rep", REP)
        (own2,) = step([down, rest], own2)
        step([rest])
        sum2 = own2.astype(F32) + other2.astype(F32)
        sum1, few = rest.steps.send(rest.value)
        down_grad, _ = down.value
        up_grad, out_grad = sum2[: 4 * width], sum2[4 * width :]
        qkv_grad = jnp.concatenate([sum1[i * width : (i + 1) * width] for i in (0, 3, 1, 4, 2, 5)], 1)
        vg = [few[k, :width] for k in range(B_UP)] + [few[B_UP, : 4 * width]]
    else:
        (gj0, *parts0), (gj1, *parts1) = (back(part, gb3) for part in range(GROUPS))
        token_grad, *table = after(gj0, gj1, gvec)
        down_grad = scatter_whole(from_blocks(by_core(down_keep, down_send, place[2]), 1, n))
        rest = scatter_whole(from_blocks(g2, 5, n))
        up_grad, out_grad = rest[: 4 * width], rest[4 * width :]
        sums = [scatter_whole(from_blocks(by_core(*parts, place[2]), 3, n)) for parts in (parts0, parts1)]
        qkv_grad = jnp.concatenate([a[i * width : (i + 1) * width] for i in range(3) for a in sums], 1)
        table = by_core(*table, place[2])
        few = jnp.swapaxes(table[:, :B_UP, : dim // BLOCKS], 0, 1).reshape(B_UP, n, width)
        few = jnp.swapaxes(few, 0, 1).reshape(n, B_UP * width)
        line = scatter_whole(jnp.concatenate([few, table[:, B_UP, : 4 * dim // BLOCKS].reshape(n, 4 * width)], 1))
        vg = [line[i * width : (i + 1) * width] for i in range(B_UP)] + [line[B_UP * width :]]
    up_grad = jnp.concatenate([up_grad[i * width : (i + 1) * width] for i in range(4)], 1)
    return (
        output.reshape(tokens.shape),
        token_grad.reshape(tokens.shape),
        qkv_grad,
        vg[B_QUERY],
        vg[B_VALUE],
        out_grad,
        vg[B_OUT],
        up_grad,
        vg[B_UP],
        down_grad,
        vg[B_DOWN],
        vg[GAIN1],
        vg[BIAS1],
        vg[GAIN2],
        vg[BIAS2],
        vg[EMBED],
    )


def solution(mesh):
    clip3, clip2, clip1 = P(("rep", "fsdp"), None, None), P(("rep", "fsdp"), None), P(("rep", "fsdp"))
    mat, line = P("fsdp", None), P("fsdp")
    params = (mat, line, line, mat, line, mat, line, mat, line, line, line, line, line, line)
    return jax.shard_map(
        functools.partial(local, mesh.shape["fsdp"]),
        mesh=mesh,
        in_specs=(clip3, clip2, clip1, clip3) + params,
        out_specs=(clip3, clip3) + params,
        check_vma=False,
    )
```

```python
import functools

import jax
import jax.numpy as jnp
from jax import lax
from jax.experimental import pallas as pl
from jax.experimental.pallas import tpu as pltpu
from jax.sharding import PartitionSpec as P

HEADS = 12
BLOCKS = 16
EPS = 1e-06
BF = jnp.bfloat16
F32 = jnp.float32
VMEM_LIMIT = 56 * 1024 * 1024

B_QUERY, B_VALUE, B_OUT, B_DOWN, GAIN1, BIAS1, GAIN2, BIAS2, EMBED, B_UP = range(10)
VECS = 13


def dot(a, b):
    return jnp.dot(a, b, preferred_element_type=F32)


def dot_nt(a, b):
    return lax.dot_general(a, b, (((1,), (1,)), ((), ())), preferred_element_type=F32)


def dot_tn(a, b):
    return lax.dot_general(a, b, (((0,), (0,)), ((), ())), preferred_element_type=F32)


def normalise(values):
    centre = values - jnp.mean(values, -1, keepdims=True)
    spread = jnp.mean(centre * centre, -1, keepdims=True)
    r = lax.rsqrt(spread + EPS)
    return centre * r, r


def norm_back(x_hat, r, q, gain):
    qg = q * gain
    m1 = jnp.mean(qg, -1, keepdims=True)
    m2 = jnp.mean(qg * x_hat, -1, keepdims=True)
    return r * (qg - m1 - x_hat * m2)


def colsum(values):
    return jnp.sum(values, 0, keepdims=True)


def gelu_both(u):
    x = jnp.abs(u)
    t = pl.reciprocal(1.0 + x * (0.3275911 * 0.7071067811865476), approx=False)
    e = jnp.exp2(u * u * (-0.5 * 1.4426950408889634))
    poly = 0.5 * 1.061405429
    for c in (-1.453152027, 1.421413741, -0.284496736, 0.254829592):
        poly = poly * t + 0.5 * c
    tail = poly * t * e
    cdf = jnp.where(u < 0, tail, 1.0 - tail)
    return u * cdf, cdf + u * (e * 0.3989422804014327)


def pack_kernel(
    w_qkv, w_out, w_up, w_down, b_query, b_value, b_out, b_down, g1, b1, g2, b2, embed, b_up, one_ref, two_ref, table
):
    width, dim = w_out.shape
    for i in range(3):
        one_ref[i * width : (i + 1) * width] = w_qkv[:, i * dim : (i + 1) * dim].astype(BF)
    one_ref[3 * width : 4 * width] = w_out[...].astype(BF)
    table[...] = jnp.zeros_like(table)
    for k, ref in enumerate((b_query, b_value, b_out, b_down, g1, b1, g2, b2, embed, b_up)):
        table[k : k + 1, 0 : ref.shape[1]] = ref[...]
    one_ref[4 * width :] = table[...].astype(BF)
    two_ref[0 : 4 * width] = w_down[...].astype(BF)
    for i in range(4):
        two_ref[(4 + i) * width : (5 + i) * width] = w_up[:, i * dim : (i + 1) * dim].astype(BF)


def pack_call(masters):
    (w_qkv, b_query, b_value, w_out, b_out, w_up, b_up, w_down, b_down,
     ln1_gain, ln1_bias, ln2_gain, ln2_bias, mask_embed) = masters
    width, dim = w_out.shape
    vectors = (b_query, b_value, b_out, b_down, ln1_gain, ln1_bias, ln2_gain, ln2_bias, mask_embed, b_up)
    return pl.pallas_call(
        pack_kernel,
        out_shape=[
            jax.ShapeDtypeStruct((4 * width + 16, dim), BF),
            jax.ShapeDtypeStruct((8 * width, dim), BF),
        ],
        scratch_shapes=[pltpu.VMEM((16, dim), F32)],
        name="pack",
    )(w_qkv, w_out, w_up, w_down, *(v.reshape(1, -1) for v in vectors))


def load_pieces(place, pieces, dest, sems):
    z, y, c, r = (place[i] for i in range(4))
    half = dest.shape[2] // 2
    kinds = ((0, 0, 0), (1, 0, 0), (0, 1, 0), (1, 1, 0), (1, 1, 2))
    copies = []
    for p, ref in enumerate(pieces):
        dx, dy, first = kinds[p % 5]
        dc = p // 5
        for k in range(ref.shape[0]):
            at = ((z + 4 - k - first) % 4) * 4 + (y ^ dy) * 2 + (c ^ dc)
            lanes = pl.ds(pl.multiple_of((r ^ dx) * half, 128), half)
            copies.append(pltpu.make_async_copy(ref.at[k], dest.at[at, :, lanes], sems.at[len(copies)]))
    for copy in copies:
        copy.start()
    for copy in copies:
        copy.wait()


def forward_kernel(count, group_ref, place_ref, tok_ref, mask_ref, *refs):
    pieces = refs[:count]
    normed_ref, qkv_ref, att_ref, lse_ref, vec_ref, w1_ref, sems = refs[count:]
    clip = pl.program_id(0)
    seq, dim = tok_ref.shape[1], tok_ref.shape[2]

    @pl.when(clip == 0)
    def _():
        if count == 1:
            copy = pltpu.make_async_copy(pieces[0], w1_ref, sems.at[0])
            copy.start()
            copy.wait()
        else:
            load_pieces(place_ref, pieces, w1_ref, sems)
        table = [w1_ref[i, 192:208, :].astype(F32) for i in range(BLOCKS)]
        vec_ref[0:B_UP] = jnp.concatenate([t[0:B_UP, 0:48] for t in table], 1)
        for j in range(4):
            vec_ref[B_UP + j : B_UP + j + 1] = jnp.concatenate(
                [t[B_UP : B_UP + 1, 0:192] for t in table[4 * j : 4 * j + 4]], 1
            )
        vec_ref[VECS:] = jnp.zeros((16 - VECS, dim), F32)

    vec = lambda k: vec_ref[k : k + 1, :]
    weight = lambda k: w1_ref[:, 48 * k : 48 * (k + 1), :].reshape(dim, dim)
    step = seq // 2
    for r in range(0, seq, step):
        rows = slice(r, r + step)
        blended = jnp.where(mask_ref[0, rows] > 0, vec(EMBED), tok_ref[0, rows].astype(F32))
        x_hat, _ = normalise(blended)
        normed = (x_hat * vec(GAIN1) + vec(BIAS1)).astype(BF)
        normed_ref[0, rows] = normed
        qkv_ref[0, rows, 0:dim] = (dot(normed, weight(0)) + vec(B_QUERY)).astype(BF)
        qkv_ref[0, rows, dim : 2 * dim] = dot(normed, weight(1)).astype(BF)
        qkv_ref[0, rows, 2 * dim :] = (dot(normed, weight(2)) + vec(B_VALUE)).astype(BF)
    head = dim // HEADS
    scale = head**-0.5 * 1.4426950408889634

    def attend(length):
        if length < seq:
            att_ref[0, length:, :] = jnp.zeros((seq - length, dim), BF)
            lse_ref[0, :, :] = jnp.zeros((HEADS, seq), F32)
        chunk = min(length, 512)
        lane = lax.broadcasted_iota(jnp.int32, (chunk, 2 * head), 1)

        @pl.loop(0, HEADS // 2, unroll=2)
        def _(pair):
            lanes = lambda i: pl.ds(pl.multiple_of(i * dim + pair * 2 * head, 128), 2 * head)
            k = qkv_ref[0, 0:length, lanes(1)]
            vt = qkv_ref[0, 0:length, lanes(2)].T
            for c in range(0, length, chunk):
                q = qkv_ref[0, c : c + chunk, lanes(0)]
                zero = jnp.zeros_like(q)
                both = jnp.concatenate([jnp.where(lane < head, q, zero), jnp.where(lane < head, zero, q)], 0)
                st = dot_nt(k, both)
                top = jnp.max(st, 0, keepdims=True) * scale
                e = jnp.exp2(st * scale - top)
                total = jnp.sum(e, 0, keepdims=True)
                p = (e * (1.0 / total)).astype(BF)
                o0 = dot(vt[0:head], p[:, 0:chunk])
                o1 = dot(vt[head:], p[:, chunk:])
                lse = top + jnp.log2(total)
                lse_ref[0, pl.ds(2 * pair, 1), c : c + chunk] = lse[:, 0:chunk]
                lse_ref[0, pl.ds(2 * pair + 1, 1), c : c + chunk] = lse[:, chunk:]
                att_ref[0, c : c + chunk, lanes(0)] = jnp.concatenate([o0, o1], 0).T.astype(BF)

    full = group_ref[clip] == 0
    pl.when(full)(lambda: attend(seq))
    pl.when(jnp.logical_not(full))(lambda: attend(seq // 2))


def weight_spec(index):
    return pl.BlockSpec((BLOCKS, 48, 768), lambda *g: (0, index, 0))


def forward_call(group_id, place, tokens, mask, pieces):
    clips, seq, dim = tokens.shape
    row = lambda *tail: pl.BlockSpec((1, *tail), lambda c, *_: (c,) + (0,) * len(tail))
    return pl.pallas_call(
        functools.partial(forward_kernel, len(pieces)),
        grid_spec=pltpu.PrefetchScalarGridSpec(
            num_scalar_prefetch=2,
            grid=(clips,),
            in_specs=[row(seq, dim), row(seq, 1)] + [pl.BlockSpec(memory_space=pl.ANY)] * len(pieces),
            out_specs=[row(seq, dim), row(seq, 3 * dim), row(seq, dim), row(HEADS, seq), whole(16, dim), whole(BLOCKS, 208, dim)],
            scratch_shapes=[pltpu.SemaphoreType.DMA((32,))],
        ),
        out_shape=[
            jax.ShapeDtypeStruct((clips, seq, dim), BF),
            jax.ShapeDtypeStruct((clips, seq, 3 * dim), BF),
            jax.ShapeDtypeStruct((clips, seq, dim), BF),
            jax.ShapeDtypeStruct((clips, HEADS, seq), F32),
            jax.ShapeDtypeStruct((16, dim), F32),
            jax.ShapeDtypeStruct((BLOCKS, 208, dim), BF),
        ],
        compiler_params=pltpu.CompilerParams(vmem_limit_bytes=VMEM_LIMIT),
        cost_estimate=pl.CostEstimate(flops=9 * 10**9, bytes_accessed=16 * 2**20, transcendentals=0),
        name="attention_forward",
    )(group_id, place, tokens, mask, *pieces)


def store_by_core(core, value, keep_ref, send_ref, rows):
    for own in range(2):

        @pl.when(core == own)
        def _():
            keep_ref[:, rows] = value[:, own]
            send_ref[:, rows] = value[:, 1 - own]


def mlp_kernel(
    group_ref, place_ref, tok_ref, mask_ref, cot_ref, att_ref, vec_ref, wo_ref, wu_ref, wd_ref,
    out_ref, gb_ref, gw_ref, keep_ref, send_ref, keep_out_ref, send_out_ref, gvec_ref,
    hidden, n2, gr, act, gpre, acc, gn2,
):
    j = pl.program_id(0)
    last = pl.num_programs(0) - 1
    rows_all, dim = tok_ref.shape
    seq = rows_all // group_ref.shape[0]
    vec = lambda k: vec_ref[k : k + 1, :]
    step = 256
    keeps = [group_ref[r // seq] == 0 if (r % seq) >= seq // 2 else None for r in range(0, rows_all, step)]
    weight = [1.0 if keep is None else jnp.where(keep, 1.0, 0.0) for keep in keeps]

    @pl.when(j == 0)
    def _():
        gvec_ref[...] = jnp.zeros_like(gvec_ref)
        w_out = wo_ref[...].reshape(dim, dim)
        for i, r in enumerate(range(0, rows_all, step)):
            rows = slice(r, r + step)
            blended = jnp.where(mask_ref[rows] > 0, vec(EMBED), tok_ref[rows].astype(F32))
            h = blended + dot(att_ref[rows], w_out) + vec(B_OUT)
            hidden[rows] = h
            x_hat, _ = normalise(h)
            n2[rows] = (x_hat * vec(GAIN2) + vec(BIAS2)).astype(BF)
            g = cot_ref[rows].astype(F32) * weight[i]
            gr[rows] = g.astype(BF)
            gvec_ref[B_DOWN : B_DOWN + 1] += colsum(g)
            acc[rows] = h + vec(B_DOWN)
            gn2[rows] = jnp.zeros((step, dim), F32)

    @pl.when(j < last)
    def _():
        w_up = wu_ref[...].reshape(dim, dim)
        w_down = wd_ref[...].reshape(dim, dim)
        b_up = vec_ref[pl.ds(B_UP + j, 1), :]
        bsum = jnp.zeros((1, dim), F32)
        big = 512
        for r in range(0, rows_all, big):
            rows = slice(r, r + big)
            pre = dot(n2[rows], w_up) + b_up
            ga = dot_nt(gr[rows], w_down)
            value, slope = gelu_both(pre)
            value = value.astype(BF)
            act[rows] = value
            grad = (slope * ga).astype(BF)
            gpre[rows] = grad
            bsum += colsum(grad.astype(F32))
            acc[rows] += dot(value, w_down)
            gn2[rows] += dot_nt(grad, w_up)
        gvec_ref[pl.ds(B_UP + j, 1), :] = bsum
        gw_ref[...] = dot_tn(n2[...], gpre[...]).astype(BF).reshape(gw_ref.shape)
        down = dot_tn(act[...], gr[...]).astype(BF).reshape(2, 2, 192, dim)
        store_by_core(place_ref[2], down, keep_ref, send_ref, slice(0, 192))

    @pl.when(j == last)
    def _():
        for i, r in enumerate(range(0, rows_all, step)):
            rows = slice(r, r + step)
            out_ref[rows] = (acc[rows] * weight[i]).astype(BF)
            x_hat, scale = normalise(hidden[rows])
            q = gn2[rows]
            gvec_ref[GAIN2 : GAIN2 + 1] += colsum(q * x_hat)
            gvec_ref[BIAS2 : BIAS2 + 1] += colsum(q)
            gh = cot_ref[rows].astype(F32) * weight[i] + norm_back(x_hat, scale, q, vec(GAIN2))
            gb = gh.astype(BF)
            gb_ref[rows] = gb
            gvec_ref[B_OUT : B_OUT + 1] += colsum(gb.astype(F32))
        grad = dot_tn(att_ref[...], gb_ref[...]).astype(BF).reshape(BLOCKS // 2, 2, 48, dim)
        store_by_core(place_ref[2], grad, keep_out_ref, send_out_ref, slice(0, 48))


def whole(*shape):
    return pl.BlockSpec(shape, lambda *g: (0,) * len(shape))


def mlp_call(group_id, place, tokens, mask, cotangent, att, vecs, w1, w2):
    rows, dim = tokens.shape
    out = lambda shape, kind: jax.ShapeDtypeStruct(shape, kind)
    return pl.pallas_call(
        mlp_kernel,
        grid_spec=pltpu.PrefetchScalarGridSpec(
            num_scalar_prefetch=2,
            grid=(5,),
            in_specs=[
                whole(rows, dim),
                whole(rows, 1),
                whole(rows, dim),
                whole(rows, dim),
                whole(*vecs.shape),
                weight_spec(3),
                pl.BlockSpec((BLOCKS, 48, dim), lambda j, *_: (0, 4 + jnp.minimum(j, 3), 0)),
                pl.BlockSpec((4, 192, dim), lambda j, *_: (jnp.minimum(j, 3), 0, 0)),
            ],
            out_specs=[
                whole(rows, dim),
                whole(rows, dim),
                pl.BlockSpec((BLOCKS, 48, dim), lambda j, *_: (0, jnp.minimum(j, 3), 0)),
                pl.BlockSpec((2, 192, dim), lambda j, *_: (jnp.minimum(j, 3), 0, 0)),
                pl.BlockSpec((2, 192, dim), lambda j, *_: (jnp.minimum(j, 3), 0, 0)),
                whole(BLOCKS // 2, 48, dim),
                whole(BLOCKS // 2, 48, dim),
                whole(16, dim),
            ],
            scratch_shapes=[
                pltpu.VMEM((rows, dim), F32),
                pltpu.VMEM((rows, dim), BF),
                pltpu.VMEM((rows, dim), BF),
                pltpu.VMEM((rows, dim), BF),
                pltpu.VMEM((rows, dim), BF),
                pltpu.VMEM((rows, dim), F32),
                pltpu.VMEM((rows, dim), F32),
            ],
        ),
        out_shape=[
            out((rows, dim), BF),
            out((rows, dim), BF),
            out((BLOCKS, 192, dim), BF),
            out((BLOCKS // 2, 192, dim), BF),
            out((BLOCKS // 2, 192, dim), BF),
            out((BLOCKS // 2, 48, dim), BF),
            out((BLOCKS // 2, 48, dim), BF),
            out((16, dim), F32),
        ],
        compiler_params=pltpu.CompilerParams(vmem_limit_bytes=VMEM_LIMIT),
        cost_estimate=pl.CostEstimate(flops=45 * 10**9, bytes_accessed=30 * 2**20, transcendentals=0),
        name="mlp",
    )(group_id, place, tokens, mask, cotangent, att, vecs, w1, w2, w2)


GROUPS = 2


def attention_back_kernel(
    part, group_ref, place_ref, q_ref, k_ref, v_ref, lse_ref, gb_ref, wo_ref, normed_ref, gj, keep_ref, send_ref, gatt, all_gj
):
    clip = pl.program_id(0)
    seq, dim = gb_ref.shape[1], gb_ref.shape[2]
    wide = dim // GROUPS
    head = dim // HEADS
    scale = head**-0.5
    gatt[...] = dot_nt(gb_ref[0], wo_ref[...].reshape(wide, dim)).astype(BF)

    def back(length):
        if length < seq:
            gj[0, length:, :] = jnp.zeros((seq - length, 3 * wide), BF)
        lane = lax.broadcasted_iota(jnp.int32, (length, 2 * head), 1)

        @pl.loop(0, HEADS // 2 // GROUPS, unroll=3)
        def _(pair):
            lanes = lambda i: pl.ds(pl.multiple_of(i * wide + pair * 2 * head, 128), 2 * head)
            k = k_ref[0, 0:length, lanes(0)]
            v = v_ref[0, 0:length, lanes(0)]
            kt = k.T
            zero = jnp.zeros((length, 2 * head), BF)
            split = lambda a: jnp.concatenate([jnp.where(lane < head, a, zero), jnp.where(lane < head, zero, a)], 0)
            q = split(q_ref[0, 0:length, lanes(0)])
            ga = split(gatt[0:length, lanes(0)])
            first = part * (HEADS // GROUPS) + 2 * pair
            lse = jnp.concatenate([lse_ref[0, pl.ds(first + h, 1), 0:length] for h in range(2)], 1)
            p = jnp.exp2(dot_nt(k, q) * (scale * 1.4426950408889634) - lse)
            gp = dot_nt(v, ga)
            inner = jnp.sum(p * gp, 0, keepdims=True)
            ds = (p * (gp - inner)).astype(BF)
            dq = [dot(kt[h * head : (h + 1) * head], ds[:, h * length : (h + 1) * length]) for h in range(2)]
            gj[0, 0:length, lanes(0)] = (jnp.concatenate(dq, 0).T * scale).astype(BF)
            gj[0, 0:length, lanes(1)] = (dot(ds, q) * scale).astype(BF)
            gj[0, 0:length, lanes(2)] = dot(p.astype(BF), ga).astype(BF)

    full = group_ref[clip] == 0
    pl.when(full)(lambda: back(seq))
    pl.when(jnp.logical_not(full))(lambda: back(seq // 2))
    all_gj[pl.ds(clip * seq, seq)] = gj[0]

    @pl.when(clip == pl.num_programs(0) - 1)
    def _():
        grad = dot_tn(normed_ref[...], all_gj[...])
        for i in range(3):
            value = grad[:, i * wide : (i + 1) * wide].astype(BF).reshape(BLOCKS // 2, 2, 48, wide)
            store_by_core(place_ref[2], value, keep_ref, send_ref, slice(48 * i, 48 * (i + 1)))


def attention_back_call(part, group_id, place, qkv, lse, gb, w1, normed):
    clips, seq, dim = gb.shape
    wide = dim // GROUPS
    columns = lambda i: pl.BlockSpec((1, seq, wide), lambda c, *_: (c, 0, GROUPS * i + part))
    row = lambda *tail: pl.BlockSpec((1, *tail), lambda c, *_: (c,) + (0,) * len(tail))
    return pl.pallas_call(
        functools.partial(attention_back_kernel, part),
        grid_spec=pltpu.PrefetchScalarGridSpec(
            num_scalar_prefetch=2,
            grid=(clips,),
            in_specs=[
                columns(0),
                columns(1),
                columns(2),
                row(HEADS, seq),
                row(seq, dim),
                pl.BlockSpec((BLOCKS // GROUPS, 48, dim), lambda *g: (part, 3, 0)),
                whole(clips * seq, dim),
            ],
            out_specs=[row(seq, 3 * wide), whole(BLOCKS // 2, 144, wide), whole(BLOCKS // 2, 144, wide)],
            scratch_shapes=[pltpu.VMEM((seq, wide), BF), pltpu.VMEM((clips * seq, 3 * wide), BF)],
        ),
        out_shape=[
            jax.ShapeDtypeStruct((clips, seq, 3 * wide), BF),
            jax.ShapeDtypeStruct((BLOCKS // 2, 144, wide), BF),
            jax.ShapeDtypeStruct((BLOCKS // 2, 144, wide), BF),
        ],
        compiler_params=pltpu.CompilerParams(vmem_limit_bytes=32 * 2**20),
        cost_estimate=pl.CostEstimate(flops=10**8, bytes_accessed=2**20, transcendentals=0),
        name="attention_backward",
    )(group_id, place, qkv, qkv, qkv, lse, gb, w1, normed)


def norm_one_kernel(
    place_ref, tok_ref, mask_ref, gb_ref, gj0_ref, gj1_ref, vec_ref, wq_ref, wk_ref, wv_ref, gmlp_ref,
    tg_ref, keep_ref, send_ref, gvec_ref,
):
    step = pl.program_id(0)
    dim = tok_ref.shape[1]
    wide = dim // GROUPS
    vec = lambda k: vec_ref[k : k + 1, :]

    @pl.when(step == 0)
    def _():
        gvec_ref[...] = gmlp_ref[...]

    gq, gk, gv = (
        jnp.concatenate([ref[:, i * wide : (i + 1) * wide] for ref in (gj0_ref, gj1_ref)], 1) for i in range(3)
    )
    gvec_ref[B_QUERY : B_QUERY + 1] += colsum(gq.astype(F32))
    gvec_ref[B_VALUE : B_VALUE + 1] += colsum(gv.astype(F32))
    g = dot_nt(gq, wq_ref[...].reshape(dim, dim))
    g += dot_nt(gk, wk_ref[...].reshape(dim, dim))
    g += dot_nt(gv, wv_ref[...].reshape(dim, dim))
    masked = mask_ref[...] > 0
    x_hat, r_std = normalise(jnp.where(masked, vec(EMBED), tok_ref[...].astype(F32)))
    gvec_ref[GAIN1 : GAIN1 + 1] += colsum(g * x_hat)
    gvec_ref[BIAS1 : BIAS1 + 1] += colsum(g)
    total = gb_ref[...].astype(F32) + norm_back(x_hat, r_std, g, vec(GAIN1))
    tg_ref[...] = jnp.where(masked, 0.0, total).astype(BF)
    gvec_ref[EMBED : EMBED + 1] += colsum(jnp.where(masked, total, 0.0))

    @pl.when(step == pl.num_programs(0) - 1)
    def _():
        table = gvec_ref[...]
        for i in range(BLOCKS):
            few = table[0:B_UP, 48 * i : 48 * (i + 1)]
            few = jnp.concatenate([few, jnp.zeros((B_UP, wide - 48), F32)], 1)
            at = 192 * (i % 4)
            up = table[B_UP + i // 4 : B_UP + i // 4 + 1, at : at + 192]
            up = jnp.concatenate([up, jnp.zeros((1, wide - 192), F32)], 1)
            few = jnp.concatenate([few, up, jnp.zeros((16 - B_UP - 1, wide), F32)], 0).astype(BF)
            for ref, same in ((keep_ref, True), (send_ref, False)):

                @pl.when((place_ref[2] == i % 2) == same)
                def _():
                    ref[i // 2] = few


def norm_one_call(place, tokens, mask, gb, gj0, gj1, vecs, w1, gvec):
    rows, dim = tokens.shape
    step = rows // 4
    part = lambda width: pl.BlockSpec((step, width), lambda i, *_: (i, 0))
    small = (BLOCKS // 2, 16, dim // GROUPS)
    return pl.pallas_call(
        norm_one_kernel,
        grid_spec=pltpu.PrefetchScalarGridSpec(
            num_scalar_prefetch=1,
            grid=(4,),
            in_specs=[
                part(dim),
                part(1),
                part(dim),
                part(3 * dim // GROUPS),
                part(3 * dim // GROUPS),
                whole(*vecs.shape),
                weight_spec(0),
                weight_spec(1),
                weight_spec(2),
                whole(16, dim),
            ],
            out_specs=[part(dim), whole(*small), whole(*small)],
            scratch_shapes=[pltpu.VMEM((16, dim), F32)],
        ),
        out_shape=[
            jax.ShapeDtypeStruct((rows, dim), BF),
            jax.ShapeDtypeStruct(small, BF),
            jax.ShapeDtypeStruct(small, BF),
        ],
        compiler_params=pltpu.CompilerParams(vmem_limit_bytes=28 * 2**20),
        cost_estimate=pl.CostEstimate(flops=10**8, bytes_accessed=2**20, transcendentals=0),
        name="norm_one_backward",
    )(place, tokens, mask, gb, gj0, gj1, vecs, w1, w1, w1, gvec)


def to_blocks(gathered, kinds):
    n, rows, dim = gathered.shape
    m = n // BLOCKS
    parts = gathered.reshape(BLOCKS, m, kinds, rows // kinds, dim)
    return jnp.swapaxes(parts, 1, 2).reshape(BLOCKS, rows * m, dim)


def from_blocks(blocks, kinds, n):
    _, rows, dim = blocks.shape
    m = n // BLOCKS
    parts = blocks.reshape(BLOCKS, kinds, m, rows // (kinds * m), dim)
    return jnp.swapaxes(parts, 1, 2).reshape(n, rows // m, dim)


def split_columns(matrix, dim):
    return [matrix[:, i : i + dim] for i in range(0, matrix.shape[1], dim)]


def swap(bit):
    return [(i, i ^ bit) for i in range(BLOCKS)]


def turn(k):
    return [(i, (i + 4 * k) % BLOCKS) for i in range(BLOCKS)]


REP = [(0, 1), (1, 0)]


def gather_pieces(pack, r):
    lanes = pack.shape[1] // 2
    half = lax.dynamic_slice_in_dim(pack, r * lanes, lanes, 1)
    along_z = jnp.stack([half] + [lax.ppermute(half, "fsdp", turn(k)) for k in (1, 2, 3)])
    by_x = lax.ppermute(along_z, "rep", REP)
    by_y = lax.ppermute(along_z, "fsdp", swap(2))
    by_xy = lax.ppermute(by_x[:2], "fsdp", swap(2))
    by_yx = lax.ppermute(by_y[2:], "rep", REP)
    own = [along_z, by_x, by_y, by_xy, by_yx]
    return own + [lax.ppermute(piece, "fsdp", swap(1)) for piece in own]


def add(a, b):
    return (a.astype(F32) + b.astype(F32)).astype(BF)


def pick(a, i, axis):
    return lax.dynamic_index_in_dim(a, i, axis, keepdims=False)


def half_of(a, i):
    rows = a.shape[-2] // 2
    return lax.dynamic_slice_in_dim(a, i * rows, rows, a.ndim - 2)


def scatter_steps(keep, send, z, y, r, extra=()):
    got = [lax.ppermute(a, "fsdp", swap(1)) for a in send]
    kept = yield tuple(keep)
    summed = jnp.concatenate([add(*pair) for pair in zip(kept, got)], 1)
    summed = summed.reshape(4, 2, *summed.shape[1:])
    a, b = summed[:2], summed[2:]
    kept = half_of(a, r), pick(b, y, 1)
    sent = yield half_of(a, 1 - r), pick(b, 1 - y, 1), *kept
    got = lax.ppermute(sent[0], "rep", REP), lax.ppermute(sent[1], "fsdp", swap(2))
    kept = yield sent[2:]
    a, b = add(kept[0], got[0]), add(kept[1], got[1])
    sent = yield pick(a, 1 - y, 1), half_of(b, 1 - r), pick(a, y, 1), half_of(b, r)
    got = lax.ppermute(sent[0], "fsdp", swap(2)), lax.ppermute(sent[1], "rep", REP)
    kept = yield sent[2:]
    both = jnp.concatenate([add(kept[0], got[0]), add(kept[1], got[1])])
    half = both.shape[1]
    both = jnp.concatenate([both, *extra], 1)
    sent = yield tuple(pick(both, (z + k) % 4, 0) for k in range(4))
    got = [lax.ppermute(sent[k], "fsdp", turn(k)) for k in (1, 2, 3)]
    kept = yield sent[:1]
    total = kept[0].astype(F32)
    for term in got:
        total += term.astype(F32)
    mine = yield (total.astype(BF),)
    other = lax.ppermute(mine[0], "rep", REP)
    mine = (yield mine)[0]
    few = mine[half:].astype(F32) + other[half:].astype(F32)
    mine, other = mine[:half], other[:half]
    yield jnp.where(r == 0, jnp.concatenate([mine, other]), jnp.concatenate([other, mine])).astype(F32), few


class Scatter:
    def __init__(self, *args):
        self.steps = scatter_steps(*args)
        self.value = next(self.steps)


def step(scatters, *ties):
    values, ties = lax.optimization_barrier(([s.value for s in scatters], list(ties)))
    for s, value in zip(scatters, values):
        s.value = s.steps.send(value)
    return ties


def by_core(keep, send, c):
    first, second = jnp.where(c == 0, keep, send), jnp.where(c == 0, send, keep)
    return jnp.stack([first, second], 1).reshape(BLOCKS, *keep.shape[1:])


def scatter_whole(send):
    own = lax.psum_scatter(send, "fsdp", scatter_dimension=0)
    other = lax.ppermute(own, "rep", REP)
    return own.astype(F32) + other.astype(F32)


def local(n, tokens, mask_pos, group_id, cotangent, *masters):
    clips, seq, dim = tokens.shape
    width = dim // n
    me, r = lax.axis_index("fsdp"), lax.axis_index("rep")
    z, y, c = me // 4, (me // 2) % 2, me % 2
    place = jnp.stack([z, y, c, r]).astype(jnp.int32)
    if n == BLOCKS:
        pack1, pack2 = pack_call(masters)
        w2 = lax.all_gather(pack2, "fsdp", axis=0)
        pieces = gather_pieces(pack1, r)
    else:
        (w_qkv, b_query, b_value, w_out, b_out, w_up, b_up, w_down, b_down,
         ln1_gain, ln1_bias, ln2_gain, ln2_bias, mask_embed) = (m.astype(BF) for m in masters)
        gather = lambda a: lax.all_gather(a, "fsdp", axis=0)
        vec_all = gather(
            jnp.concatenate(
                [b_query, b_value, b_out, b_down, ln1_gain, ln1_bias, ln2_gain, ln2_bias, mask_embed, b_up]
            )
        )
        flat = jnp.swapaxes(vec_all[:, : B_UP * width].reshape(n, B_UP, width), 0, 1).reshape(B_UP, BLOCKS, dim // BLOCKS)
        table = jnp.zeros((BLOCKS, 16, dim), BF)
        table = table.at[:, :B_UP, : dim // BLOCKS].set(jnp.swapaxes(flat, 0, 1))
        table = table.at[:, B_UP, : 4 * dim // BLOCKS].set(vec_all[:, B_UP * width :].reshape(BLOCKS, 4 * dim // BLOCKS))
        one = to_blocks(gather(jnp.concatenate(split_columns(w_qkv, dim) + [w_out])), 4)
        pieces = [jnp.concatenate([one, table], 1)]
        w2 = jnp.concatenate(
            [to_blocks(gather(w_down), 1), to_blocks(gather(jnp.concatenate(split_columns(w_up, dim))), 4)], 1
        )

    positions = lax.iota(jnp.int32, seq)
    mask = jnp.any(mask_pos[:, :, None] == positions[None, None, :], axis=1).astype(F32)[..., None]
    normed, qkv, att, lse, vecs, w1 = forward_call(group_id, place, tokens, mask, pieces)
    flat = lambda a: a.reshape(clips * seq, a.shape[-1])
    output, gb, g2, down_keep, down_send, out_keep, out_send, gvec = mlp_call(
        group_id, place, flat(tokens), flat(mask), flat(cotangent), flat(att), vecs, w1, w2
    )
    gb3 = gb.reshape(tokens.shape)
    wide = dim // GROUPS
    back = lambda part, gb3: attention_back_call(part, group_id, place, qkv, lse, gb3, w1, flat(normed))
    after = lambda gj0, gj1, gvec: norm_one_call(place, flat(tokens), flat(mask), gb, flat(gj0), flat(gj1), vecs, w1, gvec)
    if n == BLOCKS:
        down = Scatter([down_keep, out_keep], [down_send, out_send], z, y, r)
        step([down])
        (gb3,) = step([down], gb3)
        gj0, keep0, send0 = back(0, gb3)
        keep0, send0 = step([down], keep0, send0)
        (gb3,) = step([down], gb3)
        gj1, keep1, send1 = back(1, gb3)
        keep0, keep1, send0, send1 = step([down], keep0, keep1, send0, send1)
        extra = []
        rest = Scatter([keep0, keep1], [send0, send1], z, y, r, extra)
        step([rest])
        (gvec,) = step([rest], gvec)
        token_grad, keep2, send2 = after(gj0, gj1, gvec)
        keep2, send2 = step([rest], keep2, send2)
        rest.value, keep2, send2 = lax.optimization_barrier((rest.value, keep2, send2))
        few = add(keep2, lax.ppermute(send2, "fsdp", swap(1))).reshape(4, 2, *keep2.shape[1:])
        few = step([down, rest], pick(few, 1 - y, 1), pick(few, y, 1))
        few = add(few[1], lax.ppermute(few[0], "fsdp", swap(2)))
        extra.append(few)
        step([down, rest])
        own2 = lax.psum_scatter(g2, "fsdp", scatter_dimension=0)
        (own2,) = step([down, rest], own2)
        other2 = lax.ppermute(own2, "rep", REP)
        (own2,) = step([down, rest], own2)
        step([rest])
        sum2 = own2.astype(F32) + other2.astype(F32)
        sum1, few = rest.steps.send(rest.value)
        down_grad, _ = down.value
        up_grad, down_grad, out_grad = sum2, down_grad[: 4 * width], down_grad[4 * width :]
        qkv_grad = jnp.concatenate([sum1[i * width : (i + 1) * width] for i in (0, 3, 1, 4, 2, 5)], 1)
        vg = [few[k, :width] for k in range(B_UP)] + [few[B_UP, : 4 * width]]
    else:
        (gj0, *parts0), (gj1, *parts1) = (back(part, gb3) for part in range(GROUPS))
        token_grad, *table = after(gj0, gj1, gvec)
        down_grad = scatter_whole(from_blocks(by_core(down_keep, down_send, place[2]), 1, n))
        up_grad = scatter_whole(from_blocks(g2, 4, n))
        out_grad = scatter_whole(from_blocks(by_core(out_keep, out_send, place[2]), 1, n))
        sums = [scatter_whole(from_blocks(by_core(*parts, place[2]), 3, n)) for parts in (parts0, parts1)]
        qkv_grad = jnp.concatenate([a[i * width : (i + 1) * width] for i in range(3) for a in sums], 1)
        table = by_core(*table, place[2])
        few = jnp.swapaxes(table[:, :B_UP, : dim // BLOCKS], 0, 1).reshape(B_UP, n, width)
        few = jnp.swapaxes(few, 0, 1).reshape(n, B_UP * width)
        line = scatter_whole(jnp.concatenate([few, table[:, B_UP, : 4 * dim // BLOCKS].reshape(n, 4 * width)], 1))
        vg = [line[i * width : (i + 1) * width] for i in range(B_UP)] + [line[B_UP * width :]]
    up_grad = jnp.concatenate([up_grad[i * width : (i + 1) * width] for i in range(4)], 1)
    return (
        output.reshape(tokens.shape),
        token_grad.reshape(tokens.shape),
        qkv_grad,
        vg[B_QUERY],
        vg[B_VALUE],
        out_grad,
        vg[B_OUT],
        up_grad,
        vg[B_UP],
        down_grad,
        vg[B_DOWN],
        vg[GAIN1],
        vg[BIAS1],
        vg[GAIN2],
        vg[BIAS2],
        vg[EMBED],
    )


def solution(mesh):
    clip3, clip2, clip1 = P(("rep", "fsdp"), None, None), P(("rep", "fsdp"), None), P(("rep", "fsdp"))
    mat, line = P("fsdp", None), P("fsdp")
    params = (mat, line, line, mat, line, mat, line, mat, line, line, line, line, line, line)
    return jax.shard_map(
        functools.partial(local, mesh.shape["fsdp"]),
        mesh=mesh,
        in_specs=(clip3, clip2, clip1, clip3) + params,
        out_specs=(clip3, clip3) + params,
        check_vma=False,
    )
```

```python
import functools

import jax
import jax.numpy as jnp
from jax import lax
from jax.experimental import pallas as pl
from jax.experimental.pallas import tpu as pltpu
from jax.sharding import PartitionSpec as P

HEADS = 12
BLOCKS = 16
EPS = 1e-06
BF = jnp.bfloat16
F32 = jnp.float32
VMEM_LIMIT = 56 * 1024 * 1024

B_QUERY, B_VALUE, B_OUT, B_DOWN, GAIN1, BIAS1, GAIN2, BIAS2, EMBED, B_UP = range(10)
VECS = 13


def dot(a, b):
    return jnp.dot(a, b, preferred_element_type=F32)


def dot_nt(a, b):
    return lax.dot_general(a, b, (((1,), (1,)), ((), ())), preferred_element_type=F32)


def dot_tn(a, b):
    return lax.dot_general(a, b, (((0,), (0,)), ((), ())), preferred_element_type=F32)


def normalise(values):
    centre = values - jnp.mean(values, -1, keepdims=True)
    spread = jnp.mean(centre * centre, -1, keepdims=True)
    r = lax.rsqrt(spread + EPS)
    return centre * r, r


def norm_back(x_hat, r, q, gain):
    qg = q * gain
    m1 = jnp.mean(qg, -1, keepdims=True)
    m2 = jnp.mean(qg * x_hat, -1, keepdims=True)
    return r * (qg - m1 - x_hat * m2)


def colsum(values):
    return jnp.sum(values, 0, keepdims=True)


def gelu_both(u):
    x = jnp.abs(u)
    t = pl.reciprocal(1.0 + x * (0.3275911 * 0.7071067811865476), approx=False)
    e = jnp.exp2(u * u * (-0.5 * 1.4426950408889634))
    poly = 0.5 * 1.061405429
    for c in (-1.453152027, 1.421413741, -0.284496736, 0.254829592):
        poly = poly * t + 0.5 * c
    tail = poly * t * e
    cdf = jnp.where(u < 0, tail, 1.0 - tail)
    return u * cdf, cdf + u * (e * 0.3989422804014327)


def pack_kernel(
    w_qkv, w_out, w_up, w_down, b_query, b_value, b_out, b_down, g1, b1, g2, b2, embed, b_up, one_ref, two_ref, table
):
    width, dim = w_out.shape
    for i in range(3):
        one_ref[i * width : (i + 1) * width] = w_qkv[:, i * dim : (i + 1) * dim].astype(BF)
    one_ref[3 * width : 4 * width] = w_out[...].astype(BF)
    table[...] = jnp.zeros_like(table)
    for k, ref in enumerate((b_query, b_value, b_out, b_down, g1, b1, g2, b2, embed, b_up)):
        table[k : k + 1, 0 : ref.shape[1]] = ref[...]
    one_ref[4 * width :] = table[...].astype(BF)
    two_ref[0 : 4 * width] = w_down[...].astype(BF)
    for i in range(4):
        two_ref[(4 + i) * width : (5 + i) * width] = w_up[:, i * dim : (i + 1) * dim].astype(BF)


def pack_call(masters):
    (w_qkv, b_query, b_value, w_out, b_out, w_up, b_up, w_down, b_down,
     ln1_gain, ln1_bias, ln2_gain, ln2_bias, mask_embed) = masters
    width, dim = w_out.shape
    vectors = (b_query, b_value, b_out, b_down, ln1_gain, ln1_bias, ln2_gain, ln2_bias, mask_embed, b_up)
    return pl.pallas_call(
        pack_kernel,
        out_shape=[
            jax.ShapeDtypeStruct((4 * width + 16, dim), BF),
            jax.ShapeDtypeStruct((8 * width, dim), BF),
        ],
        scratch_shapes=[pltpu.VMEM((16, dim), F32)],
        name="pack",
    )(w_qkv, w_out, w_up, w_down, *(v.reshape(1, -1) for v in vectors))


def load_pieces(place, pieces, dest, sems):
    z, y, c, r = (place[i] for i in range(4))
    half = dest.shape[2] // 2
    kinds = ((0, 0, 0), (1, 0, 0), (0, 1, 0), (1, 1, 0), (1, 1, 2))
    copies = []
    for p, ref in enumerate(pieces):
        dx, dy, first = kinds[p % 5]
        dc = p // 5
        for k in range(ref.shape[0]):
            at = ((z + 4 - k - first) % 4) * 4 + (y ^ dy) * 2 + (c ^ dc)
            lanes = pl.ds(pl.multiple_of((r ^ dx) * half, 128), half)
            copies.append(pltpu.make_async_copy(ref.at[k], dest.at[at, :, lanes], sems.at[len(copies)]))
    for copy in copies:
        copy.start()
    for copy in copies:
        copy.wait()


def forward_kernel(count, group_ref, place_ref, tok_ref, mask_ref, *refs):
    pieces = refs[:count]
    normed_ref, qkv_ref, att_ref, lse_ref, vec_ref, w1_ref, sems = refs[count:]
    clip = pl.program_id(0)
    seq, dim = tok_ref.shape[1], tok_ref.shape[2]

    @pl.when(clip == 0)
    def _():
        if count == 1:
            copy = pltpu.make_async_copy(pieces[0], w1_ref, sems.at[0])
            copy.start()
            copy.wait()
        else:
            load_pieces(place_ref, pieces, w1_ref, sems)
        table = [w1_ref[i, 192:208, :].astype(F32) for i in range(BLOCKS)]
        vec_ref[0:B_UP] = jnp.concatenate([t[0:B_UP, 0:48] for t in table], 1)
        for j in range(4):
            vec_ref[B_UP + j : B_UP + j + 1] = jnp.concatenate(
                [t[B_UP : B_UP + 1, 0:192] for t in table[4 * j : 4 * j + 4]], 1
            )
        vec_ref[VECS:] = jnp.zeros((16 - VECS, dim), F32)

    vec = lambda k: vec_ref[k : k + 1, :]
    weight = lambda k: w1_ref[:, 48 * k : 48 * (k + 1), :].reshape(dim, dim)
    step = seq // 2
    for r in range(0, seq, step):
        rows = slice(r, r + step)
        blended = jnp.where(mask_ref[0, rows] > 0, vec(EMBED), tok_ref[0, rows].astype(F32))
        x_hat, _ = normalise(blended)
        normed = (x_hat * vec(GAIN1) + vec(BIAS1)).astype(BF)
        normed_ref[0, rows] = normed
        qkv_ref[0, rows, 0:dim] = (dot(normed, weight(0)) + vec(B_QUERY)).astype(BF)
        qkv_ref[0, rows, dim : 2 * dim] = dot(normed, weight(1)).astype(BF)
        qkv_ref[0, rows, 2 * dim :] = (dot(normed, weight(2)) + vec(B_VALUE)).astype(BF)
    head = dim // HEADS
    scale = head**-0.5 * 1.4426950408889634

    def attend(length):
        if length < seq:
            att_ref[0, length:, :] = jnp.zeros((seq - length, dim), BF)
            lse_ref[0, :, :] = jnp.zeros((HEADS, seq), F32)
        chunk = min(length, 512)
        lane = lax.broadcasted_iota(jnp.int32, (chunk, 2 * head), 1)

        @pl.loop(0, HEADS // 2, unroll=2)
        def _(pair):
            lanes = lambda i: pl.ds(pl.multiple_of(i * dim + pair * 2 * head, 128), 2 * head)
            k = qkv_ref[0, 0:length, lanes(1)]
            vt = qkv_ref[0, 0:length, lanes(2)].T
            for c in range(0, length, chunk):
                q = qkv_ref[0, c : c + chunk, lanes(0)]
                zero = jnp.zeros_like(q)
                both = jnp.concatenate([jnp.where(lane < head, q, zero), jnp.where(lane < head, zero, q)], 0)
                st = dot_nt(k, both)
                top = jnp.max(st, 0, keepdims=True) * scale
                e = jnp.exp2(st * scale - top)
                total = jnp.sum(e, 0, keepdims=True)
                p = (e * (1.0 / total)).astype(BF)
                o0 = dot(vt[0:head], p[:, 0:chunk])
                o1 = dot(vt[head:], p[:, chunk:])
                lse = top + jnp.log2(total)
                lse_ref[0, pl.ds(2 * pair, 1), c : c + chunk] = lse[:, 0:chunk]
                lse_ref[0, pl.ds(2 * pair + 1, 1), c : c + chunk] = lse[:, chunk:]
                att_ref[0, c : c + chunk, lanes(0)] = jnp.concatenate([o0, o1], 0).T.astype(BF)

    full = group_ref[clip] == 0
    pl.when(full)(lambda: attend(seq))
    pl.when(jnp.logical_not(full))(lambda: attend(seq // 2))


def weight_spec(index):
    return pl.BlockSpec((BLOCKS, 48, 768), lambda *g: (0, index, 0))


def forward_call(group_id, place, tokens, mask, pieces):
    clips, seq, dim = tokens.shape
    row = lambda *tail: pl.BlockSpec((1, *tail), lambda c, *_: (c,) + (0,) * len(tail))
    return pl.pallas_call(
        functools.partial(forward_kernel, len(pieces)),
        grid_spec=pltpu.PrefetchScalarGridSpec(
            num_scalar_prefetch=2,
            grid=(clips,),
            in_specs=[row(seq, dim), row(seq, 1)] + [pl.BlockSpec(memory_space=pl.ANY)] * len(pieces),
            out_specs=[row(seq, dim), row(seq, 3 * dim), row(seq, dim), row(HEADS, seq), whole(16, dim), whole(BLOCKS, 208, dim)],
            scratch_shapes=[pltpu.SemaphoreType.DMA((32,))],
        ),
        out_shape=[
            jax.ShapeDtypeStruct((clips, seq, dim), BF),
            jax.ShapeDtypeStruct((clips, seq, 3 * dim), BF),
            jax.ShapeDtypeStruct((clips, seq, dim), BF),
            jax.ShapeDtypeStruct((clips, HEADS, seq), F32),
            jax.ShapeDtypeStruct((16, dim), F32),
            jax.ShapeDtypeStruct((BLOCKS, 208, dim), BF),
        ],
        compiler_params=pltpu.CompilerParams(vmem_limit_bytes=VMEM_LIMIT),
        cost_estimate=pl.CostEstimate(flops=9 * 10**9, bytes_accessed=16 * 2**20, transcendentals=0),
        name="attention_forward",
    )(group_id, place, tokens, mask, *pieces)


def store_by_core(core, value, keep_ref, send_ref, rows):
    for own in range(2):

        @pl.when(core == own)
        def _():
            keep_ref[:, rows] = value[:, own]
            send_ref[:, rows] = value[:, 1 - own]


def mlp_kernel(
    group_ref, place_ref, tok_ref, mask_ref, cot_ref, att_ref, vec_ref, wo_ref, wu_ref, wd_ref,
    out_ref, gb_ref, gw_ref, keep_ref, send_ref, gvec_ref,
    hidden, n2, gr, act, gpre, acc, gn2,
):
    j = pl.program_id(0)
    last = pl.num_programs(0) - 1
    rows_all, dim = tok_ref.shape
    seq = rows_all // group_ref.shape[0]
    vec = lambda k: vec_ref[k : k + 1, :]
    step = 256
    keeps = [group_ref[r // seq] == 0 if (r % seq) >= seq // 2 else None for r in range(0, rows_all, step)]
    weight = [1.0 if keep is None else jnp.where(keep, 1.0, 0.0) for keep in keeps]

    @pl.when(j == 0)
    def _():
        gvec_ref[...] = jnp.zeros_like(gvec_ref)
        w_out = wo_ref[...].reshape(dim, dim)
        for i, r in enumerate(range(0, rows_all, step)):
            rows = slice(r, r + step)
            blended = jnp.where(mask_ref[rows] > 0, vec(EMBED), tok_ref[rows].astype(F32))
            h = blended + dot(att_ref[rows], w_out) + vec(B_OUT)
            hidden[rows] = h
            x_hat, _ = normalise(h)
            n2[rows] = (x_hat * vec(GAIN2) + vec(BIAS2)).astype(BF)
            g = cot_ref[rows].astype(F32) * weight[i]
            gr[rows] = g.astype(BF)
            gvec_ref[B_DOWN : B_DOWN + 1] += colsum(g)
            acc[rows] = h + vec(B_DOWN)
            gn2[rows] = jnp.zeros((step, dim), F32)

    @pl.when(j < last)
    def _():
        w_up = wu_ref[...].reshape(dim, dim)
        w_down = wd_ref[...].reshape(dim, dim)
        b_up = vec_ref[pl.ds(B_UP + j, 1), :]
        bsum = jnp.zeros((1, dim), F32)
        big = 512
        for r in range(0, rows_all, big):
            rows = slice(r, r + big)
            pre = dot(n2[rows], w_up) + b_up
            ga = dot_nt(gr[rows], w_down)
            value, slope = gelu_both(pre)
            value = value.astype(BF)
            act[rows] = value
            grad = (slope * ga).astype(BF)
            gpre[rows] = grad
            bsum += colsum(grad.astype(F32))
            acc[rows] += dot(value, w_down)
            gn2[rows] += dot_nt(grad, w_up)
        gvec_ref[pl.ds(B_UP + j, 1), :] = bsum
        gw_ref[...] = dot_tn(n2[...], gpre[...]).astype(BF).reshape(gw_ref.shape)
        down = dot_tn(act[...], gr[...]).astype(BF).reshape(2, 2, 192, dim)
        store_by_core(place_ref[2], down, keep_ref, send_ref, slice(0, 192))

    @pl.when(j == last)
    def _():
        for i, r in enumerate(range(0, rows_all, step)):
            rows = slice(r, r + step)
            out_ref[rows] = (acc[rows] * weight[i]).astype(BF)
            x_hat, scale = normalise(hidden[rows])
            q = gn2[rows]
            gvec_ref[GAIN2 : GAIN2 + 1] += colsum(q * x_hat)
            gvec_ref[BIAS2 : BIAS2 + 1] += colsum(q)
            gh = cot_ref[rows].astype(F32) * weight[i] + norm_back(x_hat, scale, q, vec(GAIN2))
            gb = gh.astype(BF)
            gb_ref[rows] = gb
            gvec_ref[B_OUT : B_OUT + 1] += colsum(gb.astype(F32))
        gw_ref[...] = dot_tn(att_ref[...], gb_ref[...]).astype(BF).reshape(gw_ref.shape)


def whole(*shape):
    return pl.BlockSpec(shape, lambda *g: (0,) * len(shape))


def mlp_call(group_id, place, tokens, mask, cotangent, att, vecs, w1, w2):
    rows, dim = tokens.shape
    out = lambda shape, kind: jax.ShapeDtypeStruct(shape, kind)
    return pl.pallas_call(
        mlp_kernel,
        grid_spec=pltpu.PrefetchScalarGridSpec(
            num_scalar_prefetch=2,
            grid=(5,),
            in_specs=[
                whole(rows, dim),
                whole(rows, 1),
                whole(rows, dim),
                whole(rows, dim),
                whole(*vecs.shape),
                weight_spec(3),
                pl.BlockSpec((BLOCKS, 48, dim), lambda j, *_: (0, 4 + jnp.minimum(j, 3), 0)),
                pl.BlockSpec((4, 192, dim), lambda j, *_: (jnp.minimum(j, 3), 0, 0)),
            ],
            out_specs=[
                whole(rows, dim),
                whole(rows, dim),
                pl.BlockSpec((BLOCKS, 48, dim), lambda j, *_: (0, j, 0)),
                pl.BlockSpec((2, 192, dim), lambda j, *_: (jnp.minimum(j, 3), 0, 0)),
                pl.BlockSpec((2, 192, dim), lambda j, *_: (jnp.minimum(j, 3), 0, 0)),
                whole(16, dim),
            ],
            scratch_shapes=[
                pltpu.VMEM((rows, dim), F32),
                pltpu.VMEM((rows, dim), BF),
                pltpu.VMEM((rows, dim), BF),
                pltpu.VMEM((rows, dim), BF),
                pltpu.VMEM((rows, dim), BF),
                pltpu.VMEM((rows, dim), F32),
                pltpu.VMEM((rows, dim), F32),
            ],
        ),
        out_shape=[
            out((rows, dim), BF),
            out((rows, dim), BF),
            out((BLOCKS, 240, dim), BF),
            out((BLOCKS // 2, 192, dim), BF),
            out((BLOCKS // 2, 192, dim), BF),
            out((16, dim), F32),
        ],
        compiler_params=pltpu.CompilerParams(vmem_limit_bytes=VMEM_LIMIT),
        cost_estimate=pl.CostEstimate(flops=45 * 10**9, bytes_accessed=30 * 2**20, transcendentals=0),
        name="mlp",
    )(group_id, place, tokens, mask, cotangent, att, vecs, w1, w2, w2)


GROUPS = 2


def attention_back_kernel(
    part, group_ref, place_ref, q_ref, k_ref, v_ref, lse_ref, gb_ref, wo_ref, normed_ref, gj, keep_ref, send_ref, gatt, all_gj
):
    clip = pl.program_id(0)
    seq, dim = gb_ref.shape[1], gb_ref.shape[2]
    wide = dim // GROUPS
    head = dim // HEADS
    scale = head**-0.5
    gatt[...] = dot_nt(gb_ref[0], wo_ref[...].reshape(wide, dim)).astype(BF)

    def back(length):
        if length < seq:
            gj[0, length:, :] = jnp.zeros((seq - length, 3 * wide), BF)
        lane = lax.broadcasted_iota(jnp.int32, (length, 2 * head), 1)

        @pl.loop(0, HEADS // 2 // GROUPS, unroll=3)
        def _(pair):
            lanes = lambda i: pl.ds(pl.multiple_of(i * wide + pair * 2 * head, 128), 2 * head)
            k = k_ref[0, 0:length, lanes(0)]
            v = v_ref[0, 0:length, lanes(0)]
            kt = k.T
            zero = jnp.zeros((length, 2 * head), BF)
            split = lambda a: jnp.concatenate([jnp.where(lane < head, a, zero), jnp.where(lane < head, zero, a)], 0)
            q = split(q_ref[0, 0:length, lanes(0)])
            ga = split(gatt[0:length, lanes(0)])
            first = part * (HEADS // GROUPS) + 2 * pair
            lse = jnp.concatenate([lse_ref[0, pl.ds(first + h, 1), 0:length] for h in range(2)], 1)
            p = jnp.exp2(dot_nt(k, q) * (scale * 1.4426950408889634) - lse)
            gp = dot_nt(v, ga)
            inner = jnp.sum(p * gp, 0, keepdims=True)
            ds = (p * (gp - inner)).astype(BF)
            dq = [dot(kt[h * head : (h + 1) * head], ds[:, h * length : (h + 1) * length]) for h in range(2)]
            gj[0, 0:length, lanes(0)] = (jnp.concatenate(dq, 0).T * scale).astype(BF)
            gj[0, 0:length, lanes(1)] = (dot(ds, q) * scale).astype(BF)
            gj[0, 0:length, lanes(2)] = dot(p.astype(BF), ga).astype(BF)

    full = group_ref[clip] == 0
    pl.when(full)(lambda: back(seq))
    pl.when(jnp.logical_not(full))(lambda: back(seq // 2))
    all_gj[pl.ds(clip * seq, seq)] = gj[0]

    @pl.when(clip == pl.num_programs(0) - 1)
    def _():
        grad = dot_tn(normed_ref[...], all_gj[...])
        for i in range(3):
            value = grad[:, i * wide : (i + 1) * wide].astype(BF).reshape(BLOCKS // 2, 2, 48, wide)
            store_by_core(place_ref[2], value, keep_ref, send_ref, slice(48 * i, 48 * (i + 1)))


def attention_back_call(part, group_id, place, qkv, lse, gb, w1, normed):
    clips, seq, dim = gb.shape
    wide = dim // GROUPS
    columns = lambda i: pl.BlockSpec((1, seq, wide), lambda c, *_: (c, 0, GROUPS * i + part))
    row = lambda *tail: pl.BlockSpec((1, *tail), lambda c, *_: (c,) + (0,) * len(tail))
    return pl.pallas_call(
        functools.partial(attention_back_kernel, part),
        grid_spec=pltpu.PrefetchScalarGridSpec(
            num_scalar_prefetch=2,
            grid=(clips,),
            in_specs=[
                columns(0),
                columns(1),
                columns(2),
                row(HEADS, seq),
                row(seq, dim),
                pl.BlockSpec((BLOCKS // GROUPS, 48, dim), lambda *g: (part, 3, 0)),
                whole(clips * seq, dim),
            ],
            out_specs=[row(seq, 3 * wide), whole(BLOCKS // 2, 144, wide), whole(BLOCKS // 2, 144, wide)],
            scratch_shapes=[pltpu.VMEM((seq, wide), BF), pltpu.VMEM((clips * seq, 3 * wide), BF)],
        ),
        out_shape=[
            jax.ShapeDtypeStruct((clips, seq, 3 * wide), BF),
            jax.ShapeDtypeStruct((BLOCKS // 2, 144, wide), BF),
            jax.ShapeDtypeStruct((BLOCKS // 2, 144, wide), BF),
        ],
        compiler_params=pltpu.CompilerParams(vmem_limit_bytes=28 * 2**20),
        cost_estimate=pl.CostEstimate(flops=10**8, bytes_accessed=2**20, transcendentals=0),
        name="attention_backward",
    )(group_id, place, qkv, qkv, qkv, lse, gb, w1, normed)


def norm_one_kernel(
    place_ref, tok_ref, mask_ref, gb_ref, gj0_ref, gj1_ref, vec_ref, wq_ref, wk_ref, wv_ref, gmlp_ref,
    tg_ref, keep_ref, send_ref, gvec_ref,
):
    step = pl.program_id(0)
    dim = tok_ref.shape[1]
    wide = dim // GROUPS
    vec = lambda k: vec_ref[k : k + 1, :]

    @pl.when(step == 0)
    def _():
        gvec_ref[...] = gmlp_ref[...]

    gq, gk, gv = (
        jnp.concatenate([ref[:, i * wide : (i + 1) * wide] for ref in (gj0_ref, gj1_ref)], 1) for i in range(3)
    )
    gvec_ref[B_QUERY : B_QUERY + 1] += colsum(gq.astype(F32))
    gvec_ref[B_VALUE : B_VALUE + 1] += colsum(gv.astype(F32))
    g = dot_nt(gq, wq_ref[...].reshape(dim, dim))
    g += dot_nt(gk, wk_ref[...].reshape(dim, dim))
    g += dot_nt(gv, wv_ref[...].reshape(dim, dim))
    masked = mask_ref[...] > 0
    x_hat, r_std = normalise(jnp.where(masked, vec(EMBED), tok_ref[...].astype(F32)))
    gvec_ref[GAIN1 : GAIN1 + 1] += colsum(g * x_hat)
    gvec_ref[BIAS1 : BIAS1 + 1] += colsum(g)
    total = gb_ref[...].astype(F32) + norm_back(x_hat, r_std, g, vec(GAIN1))
    tg_ref[...] = jnp.where(masked, 0.0, total).astype(BF)
    gvec_ref[EMBED : EMBED + 1] += colsum(jnp.where(masked, total, 0.0))

    @pl.when(step == pl.num_programs(0) - 1)
    def _():
        table = gvec_ref[...]
        for i in range(BLOCKS):
            few = table[0:B_UP, 48 * i : 48 * (i + 1)]
            few = jnp.concatenate([few, jnp.zeros((B_UP, wide - 48), F32)], 1)
            at = 192 * (i % 4)
            up = table[B_UP + i // 4 : B_UP + i // 4 + 1, at : at + 192]
            up = jnp.concatenate([up, jnp.zeros((1, wide - 192), F32)], 1)
            few = jnp.concatenate([few, up, jnp.zeros((16 - B_UP - 1, wide), F32)], 0).astype(BF)
            for ref, same in ((keep_ref, True), (send_ref, False)):

                @pl.when((place_ref[2] == i % 2) == same)
                def _():
                    ref[i // 2] = few


def norm_one_call(place, tokens, mask, gb, gj0, gj1, vecs, w1, gvec):
    rows, dim = tokens.shape
    step = rows // 4
    part = lambda width: pl.BlockSpec((step, width), lambda i, *_: (i, 0))
    small = (BLOCKS // 2, 16, dim // GROUPS)
    return pl.pallas_call(
        norm_one_kernel,
        grid_spec=pltpu.PrefetchScalarGridSpec(
            num_scalar_prefetch=1,
            grid=(4,),
            in_specs=[
                part(dim),
                part(1),
                part(dim),
                part(3 * dim // GROUPS),
                part(3 * dim // GROUPS),
                whole(*vecs.shape),
                weight_spec(0),
                weight_spec(1),
                weight_spec(2),
                whole(16, dim),
            ],
            out_specs=[part(dim), whole(*small), whole(*small)],
            scratch_shapes=[pltpu.VMEM((16, dim), F32)],
        ),
        out_shape=[
            jax.ShapeDtypeStruct((rows, dim), BF),
            jax.ShapeDtypeStruct(small, BF),
            jax.ShapeDtypeStruct(small, BF),
        ],
        compiler_params=pltpu.CompilerParams(vmem_limit_bytes=28 * 2**20),
        cost_estimate=pl.CostEstimate(flops=10**8, bytes_accessed=2**20, transcendentals=0),
        name="norm_one_backward",
    )(place, tokens, mask, gb, gj0, gj1, vecs, w1, w1, w1, gvec)


def to_blocks(gathered, kinds):
    n, rows, dim = gathered.shape
    m = n // BLOCKS
    parts = gathered.reshape(BLOCKS, m, kinds, rows // kinds, dim)
    return jnp.swapaxes(parts, 1, 2).reshape(BLOCKS, rows * m, dim)


def from_blocks(blocks, kinds, n):
    _, rows, dim = blocks.shape
    m = n // BLOCKS
    parts = blocks.reshape(BLOCKS, kinds, m, rows // (kinds * m), dim)
    return jnp.swapaxes(parts, 1, 2).reshape(n, rows // m, dim)


def split_columns(matrix, dim):
    return [matrix[:, i : i + dim] for i in range(0, matrix.shape[1], dim)]


def swap(bit):
    return [(i, i ^ bit) for i in range(BLOCKS)]


def turn(k):
    return [(i, (i + 4 * k) % BLOCKS) for i in range(BLOCKS)]


REP = [(0, 1), (1, 0)]


def gather_pieces(pack, r):
    lanes = pack.shape[1] // 2
    half = lax.dynamic_slice_in_dim(pack, r * lanes, lanes, 1)
    along_z = jnp.stack([half] + [lax.ppermute(half, "fsdp", turn(k)) for k in (1, 2, 3)])
    by_x = lax.ppermute(along_z, "rep", REP)
    by_y = lax.ppermute(along_z, "fsdp", swap(2))
    by_xy = lax.ppermute(by_x[:2], "fsdp", swap(2))
    by_yx = lax.ppermute(by_y[2:], "rep", REP)
    own = [along_z, by_x, by_y, by_xy, by_yx]
    return own + [lax.ppermute(piece, "fsdp", swap(1)) for piece in own]


def add(a, b):
    return (a.astype(F32) + b.astype(F32)).astype(BF)


def pick(a, i, axis):
    return lax.dynamic_index_in_dim(a, i, axis, keepdims=False)


def half_of(a, i):
    rows = a.shape[-2] // 2
    return lax.dynamic_slice_in_dim(a, i * rows, rows, a.ndim - 2)


def scatter_steps(keep, send, z, y, r, extra=()):
    got = [lax.ppermute(a, "fsdp", swap(1)) for a in send]
    kept = yield tuple(keep)
    summed = jnp.concatenate([add(*pair) for pair in zip(kept, got)], 1)
    summed = summed.reshape(4, 2, *summed.shape[1:])
    a, b = summed[:2], summed[2:]
    kept = half_of(a, r), pick(b, y, 1)
    sent = yield half_of(a, 1 - r), pick(b, 1 - y, 1), *kept
    got = lax.ppermute(sent[0], "rep", REP), lax.ppermute(sent[1], "fsdp", swap(2))
    kept = yield sent[2:]
    a, b = add(kept[0], got[0]), add(kept[1], got[1])
    sent = yield pick(a, 1 - y, 1), half_of(b, 1 - r), pick(a, y, 1), half_of(b, r)
    got = lax.ppermute(sent[0], "fsdp", swap(2)), lax.ppermute(sent[1], "rep", REP)
    kept = yield sent[2:]
    both = jnp.concatenate([add(kept[0], got[0]), add(kept[1], got[1])])
    half = both.shape[1]
    both = jnp.concatenate([both, *extra], 1)
    sent = yield tuple(pick(both, (z + k) % 4, 0) for k in range(4))
    got = [lax.ppermute(sent[k], "fsdp", turn(k)) for k in (1, 2, 3)]
    kept = yield sent[:1]
    total = kept[0].astype(F32)
    for term in got:
        total += term.astype(F32)
    mine = yield (total.astype(BF),)
    other = lax.ppermute(mine[0], "rep", REP)
    mine = (yield mine)[0]
    few = mine[half:].astype(F32) + other[half:].astype(F32)
    mine, other = mine[:half], other[:half]
    yield jnp.where(r == 0, jnp.concatenate([mine, other]), jnp.concatenate([other, mine])).astype(F32), few


class Scatter:
    def __init__(self, *args):
        self.steps = scatter_steps(*args)
        self.value = next(self.steps)


def step(scatters, *ties):
    values, ties = lax.optimization_barrier(([s.value for s in scatters], list(ties)))
    for s, value in zip(scatters, values):
        s.value = s.steps.send(value)
    return ties


def by_core(keep, send, c):
    first, second = jnp.where(c == 0, keep, send), jnp.where(c == 0, send, keep)
    return jnp.stack([first, second], 1).reshape(BLOCKS, *keep.shape[1:])


def scatter_whole(send):
    own = lax.psum_scatter(send, "fsdp", scatter_dimension=0)
    other = lax.ppermute(own, "rep", REP)
    return own.astype(F32) + other.astype(F32)


def local(n, tokens, mask_pos, group_id, cotangent, *masters):
    clips, seq, dim = tokens.shape
    width = dim // n
    me, r = lax.axis_index("fsdp"), lax.axis_index("rep")
    z, y, c = me // 4, (me // 2) % 2, me % 2
    place = jnp.stack([z, y, c, r]).astype(jnp.int32)
    if n == BLOCKS:
        pack1, pack2 = pack_call(masters)
        w2 = lax.all_gather(pack2, "fsdp", axis=0)
        pieces = gather_pieces(pack1, r)
    else:
        (w_qkv, b_query, b_value, w_out, b_out, w_up, b_up, w_down, b_down,
         ln1_gain, ln1_bias, ln2_gain, ln2_bias, mask_embed) = (m.astype(BF) for m in masters)
        gather = lambda a: lax.all_gather(a, "fsdp", axis=0)
        vec_all = gather(
            jnp.concatenate(
                [b_query, b_value, b_out, b_down, ln1_gain, ln1_bias, ln2_gain, ln2_bias, mask_embed, b_up]
            )
        )
        flat = jnp.swapaxes(vec_all[:, : B_UP * width].reshape(n, B_UP, width), 0, 1).reshape(B_UP, BLOCKS, dim // BLOCKS)
        table = jnp.zeros((BLOCKS, 16, dim), BF)
        table = table.at[:, :B_UP, : dim // BLOCKS].set(jnp.swapaxes(flat, 0, 1))
        table = table.at[:, B_UP, : 4 * dim // BLOCKS].set(vec_all[:, B_UP * width :].reshape(BLOCKS, 4 * dim // BLOCKS))
        one = to_blocks(gather(jnp.concatenate(split_columns(w_qkv, dim) + [w_out])), 4)
        pieces = [jnp.concatenate([one, table], 1)]
        w2 = jnp.concatenate(
            [to_blocks(gather(w_down), 1), to_blocks(gather(jnp.concatenate(split_columns(w_up, dim))), 4)], 1
        )

    positions = lax.iota(jnp.int32, seq)
    mask = jnp.any(mask_pos[:, :, None] == positions[None, None, :], axis=1).astype(F32)[..., None]
    normed, qkv, att, lse, vecs, w1 = forward_call(group_id, place, tokens, mask, pieces)
    flat = lambda a: a.reshape(clips * seq, a.shape[-1])
    output, gb, g2, down_keep, down_send, gvec = mlp_call(
        group_id, place, flat(tokens), flat(mask), flat(cotangent), flat(att), vecs, w1, w2
    )
    gb3 = gb.reshape(tokens.shape)
    wide = dim // GROUPS
    back = lambda part, gb3: attention_back_call(part, group_id, place, qkv, lse, gb3, w1, flat(normed))
    after = lambda gj0, gj1, gvec: norm_one_call(place, flat(tokens), flat(mask), gb, flat(gj0), flat(gj1), vecs, w1, gvec)
    if n == BLOCKS:
        down = Scatter([down_keep], [down_send], z, y, r)
        step([down])
        (gb3,) = step([down], gb3)
        gj0, keep0, send0 = back(0, gb3)
        keep0, send0 = step([down], keep0, send0)
        (gb3,) = step([down], gb3)
        gj1, keep1, send1 = back(1, gb3)
        keep0, keep1, send0, send1 = step([down], keep0, keep1, send0, send1)
        extra = []
        rest = Scatter([keep0, keep1], [send0, send1], z, y, r, extra)
        step([rest])
        (gvec,) = step([rest], gvec)
        token_grad, keep2, send2 = after(gj0, gj1, gvec)
        keep2, send2 = step([rest], keep2, send2)
        keep2, send2 = step([down, rest], keep2, send2)
        few = add(keep2, lax.ppermute(send2, "fsdp", swap(1))).reshape(4, 2, *keep2.shape[1:])
        few = add(pick(few, y, 1), lax.ppermute(pick(few, 1 - y, 1), "fsdp", swap(2)))
        extra.append(few)
        step([down, rest])
        own2 = lax.psum_scatter(g2, "fsdp", scatter_dimension=0)
        (own2,) = step([down, rest], own2)
        other2 = lax.ppermute(own2, "rep", REP)
        (own2,) = step([down, rest], own2)
        step([rest])
        sum2 = own2.astype(F32) + other2.astype(F32)
        sum1, few = rest.steps.send(rest.value)
        down_grad, _ = down.value
        up_grad, out_grad = sum2[: 4 * width], sum2[4 * width :]
        qkv_grad = jnp.concatenate([sum1[i * width : (i + 1) * width] for i in (0, 3, 1, 4, 2, 5)], 1)
        vg = [few[k, :width] for k in range(B_UP)] + [few[B_UP, : 4 * width]]
    else:
        (gj0, *parts0), (gj1, *parts1) = (back(part, gb3) for part in range(GROUPS))
        token_grad, *table = after(gj0, gj1, gvec)
        down_grad = scatter_whole(from_blocks(by_core(down_keep, down_send, place[2]), 1, n))
        rest = scatter_whole(from_blocks(g2, 5, n))
        up_grad, out_grad = rest[: 4 * width], rest[4 * width :]
        sums = [scatter_whole(from_blocks(by_core(*parts, place[2]), 3, n)) for parts in (parts0, parts1)]
        qkv_grad = jnp.concatenate([a[i * width : (i + 1) * width] for i in range(3) for a in sums], 1)
        table = by_core(*table, place[2])
        few = jnp.swapaxes(table[:, :B_UP, : dim // BLOCKS], 0, 1).reshape(B_UP, n, width)
        few = jnp.swapaxes(few, 0, 1).reshape(n, B_UP * width)
        line = scatter_whole(jnp.concatenate([few, table[:, B_UP, : 4 * dim // BLOCKS].reshape(n, 4 * width)], 1))
        vg = [line[i * width : (i + 1) * width] for i in range(B_UP)] + [line[B_UP * width :]]
    up_grad = jnp.concatenate([up_grad[i * width : (i + 1) * width] for i in range(4)], 1)
    return (
        output.reshape(tokens.shape),
        token_grad.reshape(tokens.shape),
        qkv_grad,
        vg[B_QUERY],
        vg[B_VALUE],
        out_grad,
        vg[B_OUT],
        up_grad,
        vg[B_UP],
        down_grad,
        vg[B_DOWN],
        vg[GAIN1],
        vg[BIAS1],
        vg[GAIN2],
        vg[BIAS2],
        vg[EMBED],
    )


def solution(mesh):
    clip3, clip2, clip1 = P(("rep", "fsdp"), None, None), P(("rep", "fsdp"), None), P(("rep", "fsdp"))
    mat, line = P("fsdp", None), P("fsdp")
    params = (mat, line, line, mat, line, mat, line, mat, line, line, line, line, line, line)
    return jax.shard_map(
        functools.partial(local, mesh.shape["fsdp"]),
        mesh=mesh,
        in_specs=(clip3, clip2, clip1, clip3) + params,
        out_specs=(clip3, clip3) + params,
        check_vma=False,
    )
```
